32 devices in a mesh: dp: 8 (over y, x, core), shard: 4 (over z).
Axes of the slice: x: 2, y: 2, z: 4, core: 2. Of those that a mesh axis runs over, the one named last changes fastest.
Arguments:
- tokens: bfloat16 [4096, 2048], P(('dp', 'shard')), may hold values from -6 to 6
- cotangent: bfloat16 [4096, 2048], P(('dp', 'shard')), may hold values from -6 to 6
- gain_first: bfloat16 [2048], replicated, may hold values from 0.5 to 1.5
- gain_second: bfloat16 [2048], replicated, may hold values from 0.5 to 1.5
- router_attn: bfloat16 [2048, 8], replicated, may hold values from -0.09375 to 0.09375
- router_mlp: bfloat16 [2048, 8], replicated, may hold values from -0.09375 to 0.09375
- query_w: bfloat16 [8, 2048, 2048], P(None, None, 'shard'), may hold values from -0.125 to 0.125
- key_w: bfloat16 [2048, 2048], P(None, 'shard'), may hold values from -0.125 to 0.125
- value_w: bfloat16 [2048, 2048], P(None, 'shard'), may hold values from -0.125 to 0.125
- output_w: bfloat16 [8, 2048, 2048], P(None, 'shard'), may hold values from -0.75 to 0.75
- gate_w: bfloat16 [2048, 45056], P(None, 'dp'), may hold values from -0.125 to 0.125
- up_w: bfloat16 [2048, 45056], P(None, 'dp'), may hold values from -0.125 to 0.125
- down_w: bfloat16 [45056, 2048], P('dp'), may hold values from -0.078125 to 0.078125
- query_a: bfloat16 [8, 8, 2048, 16], replicated, may hold values from -0.125 to 0.125
- query_b: bfloat16 [8, 8, 16, 2048], P(None, None, None, 'shard'), may hold values from -0.75 to 0.75
- key_a: bfloat16 [8, 2048, 16], replicated, may hold values from -0.125 to 0.125
- key_b: bfloat16 [8, 16, 2048], P(None, None, 'shard'), may hold values from -0.75 to 0.75
- value_a: bfloat16 [8, 2048, 16], replicated, may hold values from -0.125 to 0.125
- value_b: bfloat16 [8, 16, 2048], P(None, None, 'shard'), may hold values from -0.75 to 0.75
- output_a: bfloat16 [8, 8, 2048, 16], P(None, None, 'shard'), may hold values from -0.75 to 0.75
- output_b: bfloat16 [8, 8, 16, 2048], replicated, may hold values from -0.75 to 0.75
- gate_a: bfloat16 [8, 8, 2048, 16], replicated, may hold values from -0.125 to 0.125
- gate_b: bfloat16 [8, 16, 45056], P(None, None, 'dp'), may hold values from -0.75 to 0.75
- up_a: bfloat16 [8, 8, 2048, 16], replicated, may hold values from -0.125 to 0.125
- up_b: bfloat16 [8, 16, 45056], P(None, None, 'dp'), may hold values from -0.75 to 0.75
- down_a: bfloat16 [8, 45056, 16], P(None, 'dp'), may hold values from -0.078125 to 0.078125
- down_b: bfloat16 [8, 8, 16, 2048], replicated, may hold values from -0.75 to 0.75
- adapter_ids: int32 [8], replicated, may hold values from 0 to 7
- attn_routes: int32 [4096, 2], P('dp'), may hold values from 0 to 7, all different within a row; in each aligned block of 512 rows (0 to 511, 512 to 1023, ...) at most 160 rows name the same one
- mlp_routes: int32 [4096, 2], P(('dp', 'shard')), may hold values from 0 to 7, all different within a row; in each aligned block of 128 rows (0 to 127, 128 to 255, ...) at most 40 rows name the same one
Outputs:
- layer_out: bfloat16 [4096, 2048], P(('dp', 'shard'))
- input_grad: float32 [4096, 2048], P(('dp', 'shard'))
- grad_query_a: float32 [8, 8, 2048, 16], P(None, None, ('dp', 'shard'))
- grad_query_b: float32 [8, 8, 16, 2048], P(None, None, 'dp', 'shard')
- grad_key_a: float32 [8, 2048, 16], P(None, ('dp', 'shard'))
- grad_key_b: float32 [8, 16, 2048], P(None, 'dp', 'shard')
- grad_value_a: float32 [8, 2048, 16], P(None, ('dp', 'shard'))
- grad_value_b: float32 [8, 16, 2048], P(None, 'dp', 'shard')
- grad_output_a: float32 [8, 8, 2048, 16], P(None, None, 'shard', 'dp')
- grad_output_b: float32 [8, 8, 16, 2048], P(None, None, None, ('dp', 'shard'))
- grad_gate_a: float32 [8, 8, 2048, 16], P(None, None, ('dp', 'shard'))
- grad_gate_b: float32 [8, 16, 45056], P(None, None, ('dp', 'shard'))
- grad_up_a: float32 [8, 8, 2048, 16], P(None, None, ('dp', 'shard'))
- grad_up_b: float32 [8, 16, 45056], P(None, None, ('dp', 'shard'))
- grad_down_a: float32 [8, 45056, 16], P(None, ('dp', 'shard'))
- grad_down_b: float32 [8, 8, 16, 2048], P(None, None, None, ('dp', 'shard'))
The draws below stay inside these ranges and needn't reach their ends.
Inputs may be any that keep to these rules, and one draw needn't show every extreme that they name: `attn_routes`: each row names two different experts. In the 512 rows of one sequence no expert is named by more than 160 rows, and in some sequence one is named by exactly 160 rows. `mlp_routes`: each row names two different experts. In the 128 rows of one device no expert is named by more than 40 rows, and on some device one is named by exactly 40 rows.
All inputs are finite; a program needn't handle non-finite values.
Results may differ from the reference program's by a relative error of at most 0.024.
Values may be sent and summed in bfloat16 or wider, within the bound.
No kernel may reach another device: no remote copies, remote signals or barrier semaphores. Data moves between devices by JAX's collectives and lax.ppermute only.
A program may use at most 576 MiB of HBM per device.

```python
import math
import jax
import jax.numpy as jnp
import numpy as np
from jax import lax

D = 2048
HEADS = 16
HD = 128
FF = 5632
EXPERTS = 8
ATT_EXPERTS = 8
TOPK = 2
ADAPTERS = 8
RANK = 16
TOK_DEV = 128
LEN = 512
SEQS = 8
TOKENS = 4096
CAP_ATT = 160
CAP_MLP = 40


def set_ends(array, own_key, smallest, high):
    longest = array.shape.index(max(array.shape))
    spots = []
    for shift in (0, 1):
        where = [jax.random.randint(jax.random.fold_in(own_key, axis), (), 0, length) for axis, length in enumerate(array.shape)]
        where[longest] = (where[longest] + shift) % array.shape[longest]
        spots.append(tuple(where))
    return array.at[spots[0]].set(smallest).at[spots[1]].set(high)


def block_scale(stream_key, extent, pieces, least, high):
    factor_of = 1.0
    for axis_at, blocks in pieces:
        draws = jax.random.uniform(jax.random.fold_in(jax.random.fold_in(stream_key, 6), axis_at), (blocks,), jnp.float32, least / len(pieces), high / len(pieces))
        factor_of = factor_of * jnp.repeat(jnp.exp(draws), extent[axis_at] // blocks).reshape((-1,) + (1,) * (len(extent) - 1 - axis_at))
    return factor_of


def shared_out(rng, own, number, rows, amount, top, most, slope):
    sequence = jax.random.permutation(rng, amount)
    heavy_load, usual = portions_of(amount, rows * top, most, slope, True), portions_of(amount, rows * top, most, slope, False)
    places = jnp.arange(amount)

    def named(tallies, rotation):
        used = int((tallies > 0).sum())
        fixed = max(1, used // 4)
        passed = fixed + (places - fixed + rotation * (used - fixed)) % max(1, amount - fixed)
        return jnp.zeros((amount,), jnp.int32).at[sequence[jnp.where(places < fixed, places, passed)]].set(jnp.asarray(tallies, jnp.int32))

    tallies = jnp.where(number % 4 == 0, named(heavy_load, number // 4), named(usual, number - number // 4 - 1))
    mixed = jax.random.permutation(jax.random.fold_in(own, 3), amount)
    donor, taker = mixed[0:amount // 2 * 2:2], mixed[1:amount // 2 * 2:2]
    margin = jnp.minimum(tallies[donor] - 1, most - tallies[taker]) // 2
    margin = jnp.where((donor == sequence[0]) | (taker == sequence[0]) | (tallies[taker] == 0), 0, jnp.maximum(margin, 0))
    passed = jax.random.randint(jax.random.fold_in(own, 4), (amount // 2,), 0, 1 << 20) % (margin + 1)
    tallies = tallies.at[donor].add(-passed).at[taker].add(passed)
    items = jnp.searchsorted(jnp.cumsum(tallies), jnp.arange(rows * top), side="right").astype(jnp.int32)
    grid = items.reshape(top, rows).T
    grid = grid[jax.random.permutation(jax.random.fold_in(own, 1), rows)]
    rotation = jax.random.randint(jax.random.fold_in(own, 2), (rows, 1), 0, top)
    return jnp.take_along_axis(grid, (jnp.arange(top)[None, :] + rotation) % top, axis=1)


def portions_of(number_of, total, reach, skew, full):
    weights = [(1 << 20) // math.isqrt(rank ** skew) + 1 for rank in range(1, number_of + 1)]
    largest = reach if full else min(reach, max(-(-total // number_of), total * weights[0] // sum(weights)))
    least = 1 if total - largest >= number_of - 1 else 0
    given, surplus = [largest] + [least] * (number_of - 1), total - largest - least * (number_of - 1)
    while surplus > 0:
        free = [i for i in range(1, number_of) if given[i] < largest] or [i for i in range(1, number_of) if given[i] < reach]
        pool, left = sum([weights[i] for i in free]), surplus
        for i in free:
            more = min(reach - given[i], max(1, left * weights[i] // pool), surplus)
            given[i] = given[i] + more
            surplus = surplus - more
    return np.array(given)


def noise(own_key, extent, spread, bound, split=(), kind=jnp.bfloat16):
    values = spread * jax.random.normal(own_key, extent, jnp.float32)
    if split:
        values = values * block_scale(own_key, extent, split, -0.22, 0.18)
    return jnp.clip(values, -bound, bound).astype(kind)


def setup_inputs(seed: int = 0) -> dict:
    seeds = jax.random.split(jax.random.key(seed), 31)
    tokens = noise(seeds[0], (TOKENS, D), 1.0, 6.0, ((0, 32),))
    cotangent = noise(seeds[1], (TOKENS, D), 1.0, 6.0, ((0, 32),))
    gain_first = jnp.clip(1.0 + 0.1 * jax.random.normal(seeds[2], (D,), jnp.float32), 0.5, 1.5).astype(jnp.bfloat16)
    gain_second = jnp.clip(1.0 + 0.1 * jax.random.normal(seeds[3], (D,), jnp.float32), 0.5, 1.5).astype(jnp.bfloat16)
    router_attn = noise(seeds[4], (D, ATT_EXPERTS), (2 * D) ** -0.5, 0.09375)
    router_mlp = noise(seeds[5], (D, EXPERTS), (2 * D) ** -0.5, 0.09375)
    query_w = noise(seeds[6], (ATT_EXPERTS, D, HEADS * HD), D ** -0.5, 0.125, ((2, 4),))
    key_w = noise(seeds[7], (D, HEADS * HD), D ** -0.5, 0.125, ((1, 4),))
    value_w = noise(seeds[8], (D, HEADS * HD), D ** -0.5, 0.125, ((1, 4),))
    output_w = noise(seeds[9], (ATT_EXPERTS, HEADS * HD, D), (HEADS * HD // 32) ** -0.5, 0.75, ((1, 4),))
    gate_w = noise(seeds[10], (D, EXPERTS * FF), D ** -0.5, 0.125, ((1, 8),))
    up_w = noise(seeds[11], (D, EXPERTS * FF), D ** -0.5, 0.125, ((1, 8),))
    down_w = noise(seeds[12], (EXPERTS * FF, D), FF ** -0.5, 0.078125, ((0, 8),))
    query_a = noise(seeds[13], (ATT_EXPERTS, ADAPTERS, D, RANK), D ** -0.5, 0.125)
    query_b = noise(seeds[14], (ATT_EXPERTS, ADAPTERS, RANK, HEADS * HD), (4 * RANK) ** -0.5, 0.75, ((3, 4),))
    key_a = noise(seeds[15], (ADAPTERS, D, RANK), D ** -0.5, 0.125)
    key_b = noise(seeds[16], (ADAPTERS, RANK, HEADS * HD), (4 * RANK) ** -0.5, 0.75, ((2, 4),))
    value_a = noise(seeds[17], (ADAPTERS, D, RANK), D ** -0.5, 0.125)
    value_b = noise(seeds[18], (ADAPTERS, RANK, HEADS * HD), (4 * RANK) ** -0.5, 0.75, ((2, 4),))
    output_a = noise(seeds[19], (ATT_EXPERTS, ADAPTERS, HEADS * HD, RANK), (HEADS * HD // 32) ** -0.5, 0.75, ((2, 4),))
    output_b = noise(seeds[20], (ATT_EXPERTS, ADAPTERS, RANK, D), (4 * RANK) ** -0.5, 0.75)
    gate_a = noise(seeds[21], (EXPERTS, ADAPTERS, D, RANK), D ** -0.5, 0.125)
    gate_b = noise(seeds[22], (ADAPTERS, RANK, EXPERTS * FF), (4 * RANK) ** -0.5, 0.75, ((2, 8),))
    up_a = noise(seeds[23], (EXPERTS, ADAPTERS, D, RANK), D ** -0.5, 0.125)
    up_b = noise(seeds[24], (ADAPTERS, RANK, EXPERTS * FF), (4 * RANK) ** -0.5, 0.75, ((2, 8),))
    down_a = noise(seeds[25], (ADAPTERS, EXPERTS * FF, RANK), FF ** -0.5, 0.078125, ((1, 8),))
    down_b = noise(seeds[26], (EXPERTS, ADAPTERS, RANK, D), (4 * RANK) ** -0.5, 0.75)
    adapter_ids = set_ends(jax.random.randint(seeds[27], (SEQS,), 0, ADAPTERS), jax.random.fold_in(seeds[27], 1), 0, ADAPTERS - 1).astype(jnp.int32)
    attn_routes_keys = jax.random.split(jax.random.fold_in(seeds[28], 1), TOKENS // LEN)
    attn_routes_turns = jax.random.permutation(jax.random.fold_in(seeds[28], 3), TOKENS // LEN)
    attn_routes = jax.vmap(lambda own, number: shared_out(jax.random.fold_in(seeds[28], 2), own, number, LEN, ATT_EXPERTS, TOPK, CAP_ATT, 1))(attn_routes_keys, attn_routes_turns).reshape((TOKENS, TOPK))
    mlp_routes_keys = jax.random.split(jax.random.fold_in(seeds[29], 1), TOKENS // TOK_DEV)
    mlp_routes_turns = jax.random.permutation(jax.random.fold_in(seeds[29], 3), TOKENS // TOK_DEV)
    mlp_routes = jax.vmap(lambda own, number: shared_out(jax.random.fold_in(seeds[29], 2), own, number, TOK_DEV, EXPERTS, TOPK, CAP_MLP, 1))(mlp_routes_keys, mlp_routes_turns).reshape((TOKENS, TOPK))
    return dict(tokens=tokens, cotangent=cotangent, gain_first=gain_first, gain_second=gain_second, router_attn=router_attn, router_mlp=router_mlp, query_w=query_w, key_w=key_w, value_w=value_w, output_w=output_w, gate_w=gate_w, up_w=up_w, down_w=down_w, query_a=query_a, query_b=query_b, key_a=key_a, key_b=key_b, value_a=value_a, value_b=value_b, output_a=output_a, output_b=output_b, gate_a=gate_a, gate_b=gate_b, up_a=up_a, up_b=up_b, down_a=down_a, down_b=down_b, adapter_ids=adapter_ids, attn_routes=attn_routes, mlp_routes=mlp_routes)


precise = lax.Precision.HIGHEST
eps = 1e-05

@jax.custom_vjp
def low(v):
    return lax.optimization_barrier(v.astype(jnp.bfloat16)).astype(jnp.float32)

@jax.custom_vjp
def low_back(v):
    return v

def low_keep(v):
    return (low(v), None)

def low_pass(kept, grad):
    return (grad,)

def back_keep(v):
    return (v, None)

def back_low(kept, grad):
    return (low(grad),)
low.defvjp(low_keep, low_pass)
low_back.defvjp(back_keep, back_low)

def matmul_high(left, right):
    return jnp.dot(left, right, precision=precise, preferred_element_type=jnp.float32)

def rms_norm(values, gain_vector):
    return values * lax.rsqrt(lax.optimization_barrier(jnp.mean(values * values, axis=-1, keepdims=True)) + eps) * gain_vector

def rotate(values, positions):
    half_width = values.shape[-1] // 2
    freq_table = jnp.exp(jnp.arange(half_width, dtype=jnp.float32) * (-2.0 * math.log(10000.0) / values.shape[-1]))
    angles = positions.astype(jnp.float32)[..., None] * freq_table
    cosine_table = jnp.cos(angles)[..., None, :]
    sine_table = jnp.sin(angles)[..., None, :]
    first_half = values[..., :half_width]
    second_half = values[..., half_width:]
    return jnp.concatenate([first_half * cosine_table - second_half * sine_table, second_half * cosine_table + first_half * sine_table], axis=-1)

def pair_gates(logits, routes):
    chosen = jnp.take_along_axis(logits, routes, axis=1)
    peak_logit = lax.optimization_barrier(jnp.max(chosen, axis=1, keepdims=True))
    weights = jnp.exp(chosen - peak_logit)
    return weights / lax.optimization_barrier(jnp.sum(weights, axis=1, keepdims=True))

def member_slots(routes, expert, capacity):
    member = jnp.any(routes == expert, axis=1)
    count_rows = jnp.sum(member.astype(jnp.int32))
    token_ids = jnp.nonzero(member, size=capacity, fill_value=0)[0].astype(jnp.int32)
    slot_valid = jnp.arange(capacity, dtype=jnp.int32) < count_rows
    return (token_ids, slot_valid)

def expert_weight(gate_values, routes, expert, token_ids, slot_valid):
    per_token = lax.optimization_barrier(jnp.sum(jnp.where(routes == expert, gate_values, 0.0), axis=1))
    return jnp.where(slot_valid, per_token[token_ids], 0.0)

def sequence_attention(normed, routes, adapter, frozen, trained):
    seq_len = normed.shape[0]
    positions = jnp.arange(seq_len, dtype=jnp.int32)
    gate_values = pair_gates(matmul_high(normed, frozen['router_attn']), routes)
    key_low = matmul_high(normed, trained['key_a'][adapter])
    key_pre = matmul_high(normed, frozen['key_w']) + matmul_high(key_low, trained['key_b'][adapter])
    key_rows = low(rotate(low_back(key_pre).reshape(seq_len, HEADS, HD), positions))
    value_low = matmul_high(normed, trained['value_a'][adapter])
    value_pre = matmul_high(normed, frozen['value_w']) + matmul_high(value_low, trained['value_b'][adapter])
    value_rows = low(low_back(value_pre)).reshape(seq_len, HEADS, HD)
    score_scale = HD ** (-0.5)

    def one_expert(expert):
        token_ids, slot_valid = member_slots(routes, expert, CAP_ATT)
        query_rows = normed[token_ids]
        query_low = matmul_high(query_rows, trained['query_a'][expert, adapter])
        query_pre = matmul_high(query_rows, frozen['query_w'][expert]) + matmul_high(query_low, trained['query_b'][expert, adapter])
        queries = low(rotate(low_back(query_pre).reshape(CAP_ATT, HEADS, HD), token_ids))
        scores = jnp.einsum('qhd,khd->hqk', queries, key_rows, precision=precise) * score_scale
        scores = low_back(scores)
        allowed = positions[None, None, :] <= token_ids[None, :, None]
        scores = jnp.where(allowed, scores, -1e+30)
        peak_score = lax.optimization_barrier(jnp.max(scores, axis=-1, keepdims=True))
        exp_scores = jnp.exp(scores - peak_score)
        probabilities = low(exp_scores / lax.optimization_barrier(jnp.sum(exp_scores, axis=-1, keepdims=True)))
        mixed = jnp.einsum('hqk,khd->qhd', probabilities, value_rows, precision=precise)
        mixed = low(low_back(mixed)).reshape(CAP_ATT, HEADS * HD)
        out_low = matmul_high(mixed, trained['output_a'][expert, adapter])
        result = low_back(matmul_high(mixed, frozen['output_w'][expert]) + matmul_high(out_low, trained['output_b'][expert, adapter]))
        weight_rows = expert_weight(gate_values, routes, expert, token_ids, slot_valid)
        return jnp.zeros((seq_len, D), jnp.float32).at[token_ids].add(weight_rows[:, None] * result)
    parts = lax.map(jax.checkpoint(one_expert), jnp.arange(ATT_EXPERTS, dtype=jnp.int32))
    return lax.optimization_barrier(jnp.sum(parts, axis=0))

def mlp_block(mlp_in, routes, row_adapters, frozen, trained):
    total_rows = mlp_in.shape[0]
    gate_values = pair_gates(matmul_high(mlp_in, frozen['router_mlp']), routes)
    room = CAP_MLP * (total_rows // TOK_DEV)

    def one_expert(expert):
        token_ids, slot_valid = member_slots(routes, expert, room)
        expert_rows = mlp_in[token_ids]
        choose = (row_adapters[token_ids][:, None] == jnp.arange(ADAPTERS, dtype=jnp.int32)[None, :]).astype(jnp.float32)

        def spread_low(low_part):
            return (choose[:, :, None] * low_part[:, None, :]).reshape(room, ADAPTERS * RANK)

        def select_low(wide):
            return lax.optimization_barrier(jnp.sum(wide.reshape(room, ADAPTERS, RANK) * choose[:, :, None], axis=1))

        def first_factor(table):
            wide = matmul_high(expert_rows, jnp.transpose(table, (1, 0, 2)).reshape(D, ADAPTERS * RANK))
            return low(select_low(wide))
        gate_low = first_factor(trained['gate_a'][expert])
        up_low = first_factor(trained['up_a'][expert])
        gate_cols = lax.dynamic_slice_in_dim(frozen['gate_w'], expert * FF, FF, 1)
        up_cols = lax.dynamic_slice_in_dim(frozen['up_w'], expert * FF, FF, 1)
        gate_second = lax.dynamic_slice_in_dim(trained['gate_b'], expert * FF, FF, 2).reshape(ADAPTERS * RANK, FF)
        up_second = lax.dynamic_slice_in_dim(trained['up_b'], expert * FF, FF, 2).reshape(ADAPTERS * RANK, FF)
        gate_pre = low_back(matmul_high(expert_rows, gate_cols) + matmul_high(spread_low(gate_low), gate_second))
        up_pre = low_back(matmul_high(expert_rows, up_cols) + matmul_high(spread_low(up_low), up_second))
        hidden_act = low(jax.nn.silu(gate_pre) * up_pre)
        down_rows = lax.dynamic_slice_in_dim(frozen['down_w'], expert * FF, FF, 0)
        down_first = lax.dynamic_slice_in_dim(trained['down_a'], expert * FF, FF, 1)
        main_out = low_back(matmul_high(hidden_act, down_rows))
        down_wide = matmul_high(hidden_act, jnp.transpose(down_first, (1, 0, 2)).reshape(FF, ADAPTERS * RANK))
        down_low = low_back(select_low(down_wide))
        result = main_out + matmul_high(spread_low(down_low), trained['down_b'][expert].reshape(ADAPTERS * RANK, D))
        weight_rows = expert_weight(gate_values, routes, expert, token_ids, slot_valid)
        return jnp.zeros((total_rows, D), jnp.float32).at[token_ids].add(weight_rows[:, None] * result)
    parts = lax.map(jax.checkpoint(one_expert), jnp.arange(EXPERTS, dtype=jnp.int32))
    return lax.optimization_barrier(jnp.sum(parts, axis=0))

def layer(inputs, trained, frozen, attn_routes, mlp_routes, adapter_ids):
    normed = low(rms_norm(inputs, frozen['gain_first']))
    seq_rows = normed.reshape(SEQS, LEN, D)
    seq_routes = attn_routes.reshape(SEQS, LEN, TOPK)

    def one_sequence(block_items):
        return sequence_attention(block_items[0], block_items[1], block_items[2], frozen, trained)
    attn = lax.map(one_sequence, (seq_rows, seq_routes, adapter_ids)).reshape(TOKENS, D)
    hidden_first = inputs + low_back(attn)
    mlp_in = low(rms_norm(hidden_first, frozen['gain_second']))
    row_adapters = jnp.repeat(adapter_ids, LEN, total_repeat_length=TOKENS).astype(jnp.int32)
    return hidden_first + mlp_block(mlp_in, mlp_routes, row_adapters, frozen, trained)

def reference(tokens, cotangent, gain_first, gain_second, router_attn, router_mlp, query_w, key_w, value_w, output_w, gate_w, up_w, down_w, query_a, query_b, key_a, key_b, value_a, value_b, output_a, output_b, gate_a, gate_b, up_a, up_b, down_a, down_b, adapter_ids, attn_routes, mlp_routes):
    frozen = {'gain_first': gain_first, 'gain_second': gain_second, 'router_attn': router_attn, 'router_mlp': router_mlp, 'query_w': query_w, 'key_w': key_w, 'value_w': value_w, 'output_w': output_w, 'gate_w': gate_w, 'up_w': up_w, 'down_w': down_w}
    frozen = jax.tree.map(lambda weight: weight.astype(jnp.float32), frozen)
    trained = {'query_a': query_a, 'query_b': query_b, 'key_a': key_a, 'key_b': key_b, 'value_a': value_a, 'value_b': value_b, 'output_a': output_a, 'output_b': output_b, 'gate_a': gate_a, 'gate_b': gate_b, 'up_a': up_a, 'up_b': up_b, 'down_a': down_a, 'down_b': down_b}
    trained = jax.tree.map(lambda weight: weight.astype(jnp.float32), trained)

    def run(inputs, trained_now):
        return layer(inputs, trained_now, frozen, attn_routes, mlp_routes, adapter_ids)
    output_value, pullback = jax.vjp(run, tokens.astype(jnp.float32), trained)
    grad_inputs, grad_trained = pullback(cotangent.astype(jnp.float32))
    return (output_value.astype(jnp.bfloat16), grad_inputs, grad_trained['query_a'], grad_trained['query_b'], grad_trained['key_a'], grad_trained['key_b'], grad_trained['value_a'], grad_trained['value_b'], grad_trained['output_a'], grad_trained['output_b'], grad_trained['gate_a'], grad_trained['gate_b'], grad_trained['up_a'], grad_trained['up_b'], grad_trained['down_a'], grad_trained['down_b'])
```

```python
import math

import jax
import jax.numpy as jnp
from jax import lax
from jax.sharding import PartitionSpec as P

D = 2048
HD = 128
EXPERTS = 8
ATT_EXPERTS = 8
ADAPTERS = 8
RANK = 16


precise = lax.Precision.HIGHEST
eps = 1e-05


def inverse_rms(values):
    return lax.rsqrt(jnp.mean(values * values, axis=-1, keepdims=True) + eps)


def rotary_tables(positions, head_width):
    half_width = head_width // 2
    freq_table = jnp.exp(
        jnp.arange(half_width, dtype=jnp.float32) * (-2.0 * math.log(10000.0) / head_width)
    )
    angles = positions.astype(jnp.float32)[..., None] * freq_table
    return (jnp.cos(angles), jnp.sin(angles))


def rotate(values, cosine_table, sine_table):
    half_width = values.shape[-1] // 2
    first_half = values[..., :half_width]
    second_half = values[..., half_width:]
    return jnp.concatenate(
        [
            first_half * cosine_table - second_half * sine_table,
            second_half * cosine_table + first_half * sine_table,
        ],
        axis=-1,
    )


def unrotate(values, cosine_table, sine_table):
    half_width = values.shape[-1] // 2
    first_half = values[..., :half_width]
    second_half = values[..., half_width:]
    return jnp.concatenate(
        [
            first_half * cosine_table + second_half * sine_table,
            second_half * cosine_table - first_half * sine_table,
        ],
        axis=-1,
    )


def pair_gates(logits, routes):
    chosen = jnp.take_along_axis(logits, routes, axis=1)
    peak_logit = jnp.max(chosen, axis=1, keepdims=True)
    weights = jnp.exp(chosen - peak_logit)
    return weights / jnp.sum(weights, axis=1, keepdims=True)


def gate_backward(gate_values, grad_gates):
    return gate_values * (grad_gates - jnp.sum(gate_values * grad_gates, axis=1, keepdims=True))


def norm_backward(values, inverse, gain_vector, grad_normed):
    weighted = gain_vector.astype(jnp.float32) * grad_normed
    return inverse * weighted - values * inverse**3 * jnp.mean(
        values * weighted, axis=-1, keepdims=True
    )


def slot_table(routes, expert_count, capacity):
    choose = (routes[:, :, None] == jnp.arange(expert_count, dtype=jnp.int32)).astype(jnp.int32)
    member = jnp.sum(choose, axis=1)
    slot_numbers = jnp.cumsum(member, axis=0) - member
    target = jnp.where(member > 0, slot_numbers, capacity)
    token_ids = jnp.broadcast_to(
        jnp.arange(routes.shape[0], dtype=jnp.int32)[:, None], member.shape
    )
    expert_ids = jnp.broadcast_to(jnp.arange(expert_count, dtype=jnp.int32)[None, :], member.shape)
    token_table = (
        jnp.zeros((expert_count, capacity), jnp.int32)
        .at[expert_ids, target]
        .set(token_ids, mode="drop")
    )
    slot_valid = jnp.arange(capacity, dtype=jnp.int32)[None, :] < jnp.sum(member, axis=0)[:, None]
    pair_slots = jnp.take_along_axis(slot_numbers, routes, axis=1)
    return (token_table, slot_valid, pair_slots, choose.astype(jnp.float32))


def on_device(
    tokens,
    cotangent,
    gain_first,
    gain_second,
    router_attn,
    router_mlp,
    query_w,
    key_w,
    value_w,
    output_w,
    gate_w,
    up_w,
    down_w,
    query_a,
    query_b,
    key_a,
    key_b,
    value_a,
    value_b,
    output_a,
    output_b,
    gate_a,
    gate_b,
    up_a,
    up_b,
    down_a,
    down_b,
    adapter_ids,
    attn_routes,
    mlp_routes,
):
    shard_count = lax.axis_size("shard")
    group_count = lax.axis_size("dp")
    tok_rows = tokens.shape[0]
    seq_len = tok_rows * shard_count
    cap_att = seq_len // 4 + seq_len // 16
    cap_mlp = tok_rows // 4 + tok_rows // 16
    slice_count = group_count // EXPERTS
    ff_local = gate_w.shape[1]
    width_local = key_w.shape[1]
    heads_local = width_local // HD
    adapter_now = adapter_ids[lax.axis_index("dp")]
    first_row = lax.axis_index("shard") * tok_rows
    score_scale = HD ** (-0.5)
    key_w_heads = key_w.reshape(D, heads_local, HD)
    value_w_heads = value_w.reshape(D, heads_local, HD)
    query_w_heads = query_w.reshape(ATT_EXPERTS, D, heads_local, HD)
    output_w_heads = output_w.reshape(ATT_EXPERTS, heads_local, HD, D)
    inputs = tokens.astype(jnp.float32)
    inverse_first = inverse_rms(inputs)
    normed = (inputs * inverse_first * gain_first.astype(jnp.float32)).astype(jnp.bfloat16)
    normed_all = lax.all_gather(normed, "shard", axis=0, tiled=True)
    attn_gates = pair_gates(
        jnp.dot(normed_all, router_attn, preferred_element_type=jnp.float32), attn_routes
    )
    attn_table, attn_valid, attn_slots, attn_choose = slot_table(attn_routes, ATT_EXPERTS, cap_att)
    gate_by_expert = jnp.sum(attn_gates[:, :, None] * attn_choose, axis=1)
    expert_range = jnp.arange(ATT_EXPERTS, dtype=jnp.int32)[:, None]
    attn_weight = jnp.where(attn_valid, gate_by_expert[attn_table, expert_range], 0.0)
    positions = jnp.arange(seq_len, dtype=jnp.int32)
    key_cos, key_sin = rotary_tables(positions, HD)
    key_first = key_a[adapter_now]
    key_second = key_b[adapter_now]
    value_first = value_a[adapter_now]
    value_second = value_b[adapter_now]
    key_second_heads = key_second.reshape(RANK, heads_local, HD)
    value_second_heads = value_second.reshape(RANK, heads_local, HD)
    key_low = jnp.dot(normed_all, key_first, preferred_element_type=jnp.float32)
    key_pre = jnp.einsum(
        "sd,dhj->hsj", normed_all, key_w_heads, preferred_element_type=jnp.float32
    ) + jnp.einsum("sr,rhj->hsj", key_low, key_second_heads.astype(jnp.float32), precision=precise)
    key_rows = rotate(key_pre, key_cos, key_sin).astype(jnp.bfloat16)
    value_low = jnp.dot(normed_all, value_first, preferred_element_type=jnp.float32)
    value_pre = jnp.einsum(
        "sd,dhj->hsj", normed_all, value_w_heads, preferred_element_type=jnp.float32
    ) + jnp.einsum(
        "sr,rhj->hsj", value_low, value_second_heads.astype(jnp.float32), precision=precise
    )
    value_rows = value_pre.astype(jnp.bfloat16)
    query_rows = normed_all[attn_table]
    query_first = query_a[:, adapter_now]
    query_second = query_b[:, adapter_now]
    query_second_heads = query_second.reshape(ATT_EXPERTS, RANK, heads_local, HD)
    query_low = jnp.einsum(
        "ecd,edr->ecr", query_rows, query_first, preferred_element_type=jnp.float32
    )
    query_pre = jnp.einsum(
        "ecd,edhj->ehcj", query_rows, query_w_heads, preferred_element_type=jnp.float32
    ) + jnp.einsum(
        "ecr,erhj->ehcj", query_low, query_second_heads.astype(jnp.float32), precision=precise
    )
    query_cos, query_sin = rotary_tables(attn_table, HD)
    query_cos = query_cos[:, None]
    query_sin = query_sin[:, None]
    queries = rotate(query_pre, query_cos, query_sin).astype(jnp.bfloat16)

    def scores_for(query_block, query_pos):
        raw_scores = (
            jnp.einsum("hqd,hkd->hqk", query_block, key_rows, preferred_element_type=jnp.float32)
            * score_scale
        )
        allowed = positions[None, None, :] <= query_pos[None, :, None]
        return jnp.where(allowed, raw_scores, -1e30)

    def attend(block_items):
        query_block, query_pos = block_items
        scores = scores_for(query_block, query_pos)
        peak_score = jnp.max(scores, axis=-1, keepdims=True)
        exp_scores = jnp.exp(scores - peak_score)
        total_weight = jnp.sum(exp_scores, axis=-1, keepdims=True)
        probabilities = (exp_scores / total_weight).astype(jnp.bfloat16)
        mixed = jnp.einsum(
            "hqk,hkd->hqd", probabilities, value_rows, preferred_element_type=jnp.float32
        ).astype(jnp.bfloat16)
        return (mixed, peak_score[..., 0] + jnp.log(total_weight[..., 0]))

    mixed_heads, log_totals = lax.map(attend, (queries, attn_table))
    out_first = output_a[:, adapter_now]
    out_second = output_b[:, adapter_now]
    out_first_heads = out_first.reshape(ATT_EXPERTS, heads_local, HD, RANK)
    out_low = jnp.einsum(
        "ehcj,ehjr->ecr", mixed_heads, out_first_heads, preferred_element_type=jnp.float32
    )
    out_part = jnp.einsum(
        "ehcj,ehjd->ecd", mixed_heads, output_w_heads, preferred_element_type=jnp.float32
    ) + jnp.einsum("ecr,erd->ecd", out_low, out_second.astype(jnp.float32), precision=precise)
    attn_part = (
        jnp.zeros((seq_len, D), jnp.float32).at[attn_table].add(attn_weight[..., None] * out_part)
    )
    attn_local = lax.psum_scatter(
        attn_part.astype(jnp.bfloat16), "shard", scatter_dimension=0, tiled=True
    ).astype(jnp.float32)
    hidden_first = inputs + attn_local
    inverse_second = inverse_rms(hidden_first)
    mlp_in = (hidden_first * inverse_second * gain_second.astype(jnp.float32)).astype(jnp.bfloat16)
    mlp_gates = pair_gates(
        jnp.dot(mlp_in, router_mlp, preferred_element_type=jnp.float32), mlp_routes
    )
    mlp_table, mlp_valid, mlp_slots, mlp_choose = slot_table(mlp_routes, EXPERTS, cap_mlp)
    mlp_by_expert = jnp.sum(mlp_gates[:, :, None] * mlp_choose, axis=1)
    mlp_range = jnp.arange(EXPERTS, dtype=jnp.int32)[:, None]
    mlp_weight = jnp.where(mlp_valid, mlp_by_expert[mlp_table, mlp_range], 0.0)
    sent_rows = jnp.where(mlp_valid[..., None], mlp_in[mlp_table], jnp.zeros((), jnp.bfloat16))
    gate_first = gate_a[:, adapter_now]
    up_first = up_a[:, adapter_now]
    low_gate = jnp.einsum("td,edr->ter", mlp_in, gate_first, preferred_element_type=jnp.float32)
    low_up = jnp.einsum("td,edr->ter", mlp_in, up_first, preferred_element_type=jnp.float32)
    low_both = jnp.concatenate([low_gate, low_up], axis=-1)
    sent_low = jnp.where(mlp_valid[..., None], low_both[mlp_table, mlp_range], 0.0).astype(
        jnp.bfloat16
    )
    send_rows_all = jnp.repeat(sent_rows, slice_count, axis=0)
    send_low_all = jnp.repeat(sent_low, slice_count, axis=0)
    pick_source = (adapter_ids[:, None] == jnp.arange(ADAPTERS, dtype=jnp.int32)[None, :]).astype(
        jnp.float32
    )
    gate_table = gate_b.reshape(ADAPTERS * RANK, ff_local)
    up_table = up_b.reshape(ADAPTERS * RANK, ff_local)
    down_table = jnp.transpose(down_a, (1, 0, 2)).reshape(ff_local, ADAPTERS * RANK)

    def spread_low(low_part):
        expanded = pick_source[:, None, :, None] * low_part[:, :, None, :]
        return expanded.reshape(low_part.shape[0], low_part.shape[1], ADAPTERS * RANK).astype(
            jnp.bfloat16
        )

    def select_low(wide):
        split_wide = wide.reshape(wide.shape[0], wide.shape[1], ADAPTERS, RANK)
        return jnp.sum(split_wide * pick_source[:, None, :, None], axis=2)

    def expert_inner(recv_rows, recv_low):
        gate_wide = spread_low(recv_low[..., :RANK].astype(jnp.float32))
        up_wide = spread_low(recv_low[..., RANK:].astype(jnp.float32))
        gate_pre = jnp.einsum(
            "scd,df->scf", recv_rows, gate_w, preferred_element_type=jnp.float32
        ) + jnp.einsum("scq,qf->scf", gate_wide, gate_table, preferred_element_type=jnp.float32)
        up_pre = jnp.einsum(
            "scd,df->scf", recv_rows, up_w, preferred_element_type=jnp.float32
        ) + jnp.einsum("scq,qf->scf", up_wide, up_table, preferred_element_type=jnp.float32)
        return (gate_pre, up_pre, gate_wide, up_wide)

    recv_rows = lax.all_to_all(send_rows_all, "dp", split_axis=0, concat_axis=0, tiled=True)
    recv_low = lax.all_to_all(send_low_all, "dp", split_axis=0, concat_axis=0, tiled=True)
    gate_pre, up_pre, gate_wide, up_wide = expert_inner(recv_rows, recv_low)
    hidden_act = (jax.nn.silu(gate_pre) * up_pre).astype(jnp.bfloat16)
    main_out = jnp.einsum("scf,fd->scd", hidden_act, down_w, preferred_element_type=jnp.float32)
    down_low = select_low(
        jnp.einsum("scf,fq->scq", hidden_act, down_table, preferred_element_type=jnp.float32)
    )
    main_out, down_low, kept_rows, kept_low = (main_out, down_low, recv_rows, recv_low)
    returned = (
        lax.all_to_all(
            main_out.astype(jnp.bfloat16), "dp", split_axis=0, concat_axis=0, tiled=True
        ).astype(main_out.dtype),
        lax.all_to_all(
            down_low.astype(jnp.bfloat16), "dp", split_axis=0, concat_axis=0, tiled=True
        ).astype(down_low.dtype),
    )
    main_sum = jnp.sum(returned[0].reshape(EXPERTS, slice_count, cap_mlp, D), axis=1)
    low_sum = jnp.sum(returned[1].reshape(EXPERTS, slice_count, cap_mlp, RANK), axis=1)
    down_second = down_b[:, adapter_now].astype(jnp.float32)
    expert_out = main_sum + jnp.einsum("ecr,erd->ecd", low_sum, down_second, precision=precise)
    pair_out = expert_out[mlp_routes, mlp_slots]
    mlp_out = jnp.sum(mlp_gates[..., None] * pair_out, axis=1)
    layer_out = (hidden_first + mlp_out).astype(jnp.bfloat16)
    grad_out = cotangent.astype(jnp.float32)
    grad_pair_gate = jnp.sum(grad_out[:, None, :] * pair_out, axis=-1)
    grad_mlp_logits = gate_backward(mlp_gates, grad_pair_gate)
    grad_mlp_cols = jnp.sum(grad_mlp_logits[:, :, None] * mlp_choose, axis=1)
    grad_mlp_in = jnp.dot(grad_mlp_cols, router_mlp.astype(jnp.float32).T, precision=precise)
    grad_expert = mlp_weight[..., None] * grad_out[mlp_table]
    grad_main = grad_expert.astype(jnp.bfloat16)
    grad_down_low = jnp.einsum("ecd,erd->ecr", grad_expert, down_second, precision=precise).astype(
        jnp.bfloat16
    )
    grad_down_b_own = jnp.einsum("ecr,ecd->erd", low_sum, grad_expert, precision=precise)
    send_grad = jnp.repeat(grad_main, slice_count, axis=0)
    send_grad_low = jnp.repeat(grad_down_low, slice_count, axis=0)
    recv_grad, recv_grad_low, owner_rows, owner_low = (
        lax.all_to_all(send_grad, "dp", split_axis=0, concat_axis=0, tiled=True),
        lax.all_to_all(send_grad_low, "dp", split_axis=0, concat_axis=0, tiled=True),
        lax.all_to_all(send_rows_all, "dp", split_axis=0, concat_axis=0, tiled=True),
        lax.all_to_all(send_low_all, "dp", split_axis=0, concat_axis=0, tiled=True),
    )
    gate_pre, up_pre, gate_wide, up_wide = expert_inner(owner_rows, owner_low)
    sigmoid_gate = jax.nn.sigmoid(gate_pre)
    activated = gate_pre * sigmoid_gate
    hidden_act = (activated * up_pre).astype(jnp.bfloat16)
    grad_low_wide = spread_low(recv_grad_low.astype(jnp.float32))
    grad_hidden = jnp.einsum(
        "scd,fd->scf", recv_grad, down_w, preferred_element_type=jnp.float32
    ) + jnp.einsum("scq,fq->scf", grad_low_wide, down_table, preferred_element_type=jnp.float32)
    grad_down_table = jnp.einsum(
        "scq,scf->qf", grad_low_wide, hidden_act, preferred_element_type=jnp.float32
    )
    grad_gate_pre = (
        grad_hidden * up_pre * sigmoid_gate * (1.0 + gate_pre * (1.0 - sigmoid_gate))
    ).astype(jnp.bfloat16)
    grad_up_pre = (grad_hidden * activated).astype(jnp.bfloat16)
    grad_rows = jnp.einsum(
        "scf,df->scd", grad_gate_pre, gate_w, preferred_element_type=jnp.float32
    ) + jnp.einsum("scf,df->scd", grad_up_pre, up_w, preferred_element_type=jnp.float32)
    grad_gate_low = select_low(
        jnp.einsum("scf,qf->scq", grad_gate_pre, gate_table, preferred_element_type=jnp.float32)
    )
    grad_up_low = select_low(
        jnp.einsum("scf,qf->scq", grad_up_pre, up_table, preferred_element_type=jnp.float32)
    )
    grad_gate_table = jnp.einsum(
        "scq,scf->qf", gate_wide, grad_gate_pre, preferred_element_type=jnp.float32
    )
    grad_up_table = jnp.einsum(
        "scq,scf->qf", up_wide, grad_up_pre, preferred_element_type=jnp.float32
    )
    grad_back = (
        lax.all_to_all(
            grad_rows.astype(jnp.bfloat16), "dp", split_axis=0, concat_axis=0, tiled=True
        ).astype(grad_rows.dtype),
        lax.all_to_all(
            jnp.concatenate([grad_gate_low, grad_up_low], axis=-1).astype(jnp.bfloat16),
            "dp",
            split_axis=0,
            concat_axis=0,
            tiled=True,
        ).astype(jnp.float32),
    )
    rows_back = jnp.sum(grad_back[0].reshape(EXPERTS, slice_count, cap_mlp, D), axis=1)
    lows_back = jnp.sum(grad_back[1].reshape(EXPERTS, slice_count, cap_mlp, 2 * RANK), axis=1)
    grad_gate_lows = lows_back[..., :RANK]
    grad_up_lows = lows_back[..., RANK:]
    grad_buffer = (
        rows_back
        + jnp.einsum(
            "ecr,edr->ecd", grad_gate_lows, gate_first.astype(jnp.float32), precision=precise
        )
        + jnp.einsum("ecr,edr->ecd", grad_up_lows, up_first.astype(jnp.float32), precision=precise)
    )
    grad_mlp_in = grad_mlp_in + jnp.zeros((tok_rows, D), jnp.float32).at[mlp_table].add(
        jnp.where(mlp_valid[..., None], grad_buffer, 0.0)
    )
    sent_rows_wide = sent_rows.astype(jnp.float32)
    grad_gate_a_own = jnp.einsum("ecd,ecr->erd", sent_rows_wide, grad_gate_lows, precision=precise)
    grad_up_a_own = jnp.einsum("ecd,ecr->erd", sent_rows_wide, grad_up_lows, precision=precise)
    grad_first = grad_out + norm_backward(hidden_first, inverse_second, gain_second, grad_mlp_in)
    grad_all = lax.all_gather(grad_first.astype(jnp.bfloat16), "shard", axis=0, tiled=True)
    grad_at_pairs = grad_all[attn_table].astype(jnp.float32)
    grad_gate_part = jnp.where(attn_valid, jnp.sum(grad_at_pairs * out_part, axis=-1), 0.0)
    grad_result = (attn_weight[..., None] * grad_at_pairs).astype(jnp.bfloat16)
    grad_out_low = jnp.einsum(
        "ecd,erd->ecr", grad_result, out_second, preferred_element_type=jnp.float32
    )
    grad_output_a_own = jnp.einsum(
        "ecr,ehcj->erhj", grad_out_low, mixed_heads.astype(jnp.float32), precision=precise
    ).reshape(ATT_EXPERTS, RANK, width_local)
    grad_mixed = jnp.einsum(
        "ecd,ehjd->ehcj", grad_result, output_w_heads, preferred_element_type=jnp.float32
    ) + jnp.einsum(
        "ecr,ehjr->ehcj", grad_out_low, out_first_heads.astype(jnp.float32), precision=precise
    )
    grad_mixed = grad_mixed.astype(jnp.bfloat16)

    def attend_back(running, block_items):
        key_sum, value_sum = running
        query_block, query_pos, grad_block, log_block = block_items
        scores = scores_for(query_block, query_pos)
        probabilities = jnp.exp(scores - log_block[..., None])
        grad_probs = jnp.einsum(
            "hqd,hkd->hqk", grad_block, value_rows, preferred_element_type=jnp.float32
        )
        centre = jnp.sum(probabilities * grad_probs, axis=-1, keepdims=True)
        grad_scores = (probabilities * (grad_probs - centre)).astype(jnp.bfloat16)
        grad_query = (
            jnp.einsum("hqk,hkd->hqd", grad_scores, key_rows, preferred_element_type=jnp.float32)
            * score_scale
        )
        key_sum = (
            key_sum
            + jnp.einsum(
                "hqk,hqd->hkd", grad_scores, query_block, preferred_element_type=jnp.float32
            )
            * score_scale
        )
        value_sum = value_sum + jnp.einsum(
            "hqk,hqd->hkd",
            probabilities.astype(jnp.bfloat16),
            grad_block,
            preferred_element_type=jnp.float32,
        )
        return ((key_sum, value_sum), grad_query)

    zero_rows = jnp.zeros((heads_local, seq_len, HD), jnp.float32)
    (grad_keys, grad_values), grad_queries = lax.scan(
        attend_back, (zero_rows, zero_rows), (queries, attn_table, grad_mixed, log_totals)
    )
    grad_query_pre = unrotate(grad_queries, query_cos, query_sin).astype(jnp.bfloat16)
    grad_key_pre = unrotate(grad_keys, key_cos, key_sin).astype(jnp.bfloat16)
    grad_value_pre = grad_values.astype(jnp.bfloat16)
    grad_query_low = jnp.einsum(
        "ehcj,erhj->ecr", grad_query_pre, query_second_heads, preferred_element_type=jnp.float32
    )
    grad_query_rows = jnp.einsum(
        "ehcj,edhj->ecd", grad_query_pre, query_w_heads, preferred_element_type=jnp.float32
    ) + jnp.einsum(
        "ecr,edr->ecd", grad_query_low, query_first.astype(jnp.float32), precision=precise
    )
    grad_query_b_own = jnp.einsum(
        "ecr,ehcj->erhj", query_low, grad_query_pre.astype(jnp.float32), precision=precise
    ).reshape(ATT_EXPERTS, RANK, width_local)
    grad_normed = (
        jnp.zeros((seq_len, D), jnp.float32)
        .at[attn_table]
        .add(jnp.where(attn_valid[..., None], grad_query_rows, 0.0))
    )
    grad_key_low = jnp.einsum(
        "hsj,rhj->sr", grad_key_pre, key_second_heads, preferred_element_type=jnp.float32
    )
    grad_value_low = jnp.einsum(
        "hsj,rhj->sr", grad_value_pre, value_second_heads, preferred_element_type=jnp.float32
    )
    grad_normed = (
        grad_normed
        + jnp.einsum("hsj,dhj->sd", grad_key_pre, key_w_heads, preferred_element_type=jnp.float32)
        + jnp.einsum(
            "hsj,dhj->sd", grad_value_pre, value_w_heads, preferred_element_type=jnp.float32
        )
    )
    grad_normed = (
        grad_normed
        + jnp.dot(grad_key_low, key_first.astype(jnp.float32).T, precision=precise)
        + jnp.dot(grad_value_low, value_first.astype(jnp.float32).T, precision=precise)
    )
    grad_key_b_own = jnp.einsum(
        "sr,hsj->rhj", key_low, grad_key_pre.astype(jnp.float32), precision=precise
    ).reshape(RANK, width_local)
    grad_value_b_own = jnp.einsum(
        "sr,hsj->rhj", value_low, grad_value_pre.astype(jnp.float32), precision=precise
    ).reshape(RANK, width_local)
    gate_rows_part = (
        jnp.zeros((seq_len, ATT_EXPERTS), jnp.float32)
        .at[attn_table, expert_range]
        .add(grad_gate_part)
    )
    grad_normed_local, grad_gate_local = (
        lax.psum_scatter(
            grad_normed.astype(jnp.bfloat16), "shard", scatter_dimension=0, tiled=True
        ).astype(jnp.float32),
        lax.psum_scatter(
            gate_rows_part.astype(jnp.bfloat16), "shard", scatter_dimension=0, tiled=True
        ).astype(jnp.float32),
    )
    local_gates = lax.dynamic_slice_in_dim(attn_gates, first_row, tok_rows, 0)
    local_routes = lax.dynamic_slice_in_dim(attn_routes, first_row, tok_rows, 0)
    local_choose = lax.dynamic_slice_in_dim(attn_choose, first_row, tok_rows, 0)
    grad_pair = jnp.take_along_axis(grad_gate_local, local_routes, axis=1)
    grad_attn_logits = gate_backward(local_gates, grad_pair)
    grad_attn_cols = jnp.sum(grad_attn_logits[:, :, None] * local_choose, axis=1)
    grad_normed_local = grad_normed_local + jnp.dot(
        grad_attn_cols, router_attn.astype(jnp.float32).T, precision=precise
    )
    input_grad = grad_first + norm_backward(inputs, inverse_first, gain_first, grad_normed_local)
    block = D // (group_count * shard_count)
    lows = jnp.concatenate(
        [
            out_low.reshape(-1, RANK),
            grad_query_low.reshape(-1, RANK),
            grad_key_low,
            grad_value_low,
        ],
        axis=0,
    )
    lows = lax.psum(lows, "shard")
    pair_count = ATT_EXPERTS * cap_att
    out_low_full = lows[:pair_count].reshape(ATT_EXPERTS, cap_att, RANK)
    query_low_full = lows[pair_count : 2 * pair_count].reshape(ATT_EXPERTS, cap_att, RANK)
    kv_low_full = jnp.concatenate(
        [lows[2 * pair_count : 2 * pair_count + seq_len], lows[2 * pair_count + seq_len :]], axis=1
    )

    def own_columns(rows):
        split = rows.reshape(rows.shape[:-1] + (group_count, shard_count, block))
        own = lax.dynamic_index_in_dim(
            split, lax.axis_index("shard"), axis=split.ndim - 2, keepdims=False
        )
        return own.reshape(rows.shape[:-1] + (group_count * block,))

    grad_query_a_own = jnp.einsum(
        "ecr,ecd->erd",
        query_low_full,
        own_columns(query_rows).astype(jnp.float32),
        preferred_element_type=jnp.float32,
    )
    grad_output_b_own = jnp.einsum(
        "ecr,ecd->erd",
        out_low_full,
        own_columns(grad_result).astype(jnp.float32),
        preferred_element_type=jnp.float32,
    )
    grad_kv_a_own = jnp.einsum(
        "sr,sd->rd",
        kv_low_full,
        own_columns(normed_all).astype(jnp.float32),
        preferred_element_type=jnp.float32,
    ).reshape(2, RANK, group_count * block)
    mlp_parts = jnp.concatenate([grad_gate_a_own, grad_up_a_own, grad_down_b_own], axis=0)
    mlp_parts = (
        mlp_parts.reshape(3 * EXPERTS * RANK, group_count, shard_count, block)
        .transpose(2, 0, 1, 3)
        .reshape(shard_count, 3 * EXPERTS * RANK, group_count * block)
        .astype(jnp.bfloat16)
    )
    mlp_parts = lax.psum_scatter(mlp_parts, "shard", scatter_dimension=0, tiled=True)[0]

    def to_owner_columns(part):
        return part.reshape(-1, group_count, block).transpose(1, 0, 2).reshape(group_count, -1)

    def to_owner_ranks(part):
        rows = part.reshape(-1, group_count, RANK // group_count, width_local)
        return rows.transpose(1, 0, 2, 3).reshape(group_count, -1)

    pieces = [
        to_owner_columns(grad_query_a_own.astype(jnp.bfloat16)),
        to_owner_columns(grad_output_b_own.astype(jnp.bfloat16)),
        to_owner_columns(grad_kv_a_own.astype(jnp.bfloat16)),
        to_owner_columns(mlp_parts),
        to_owner_ranks(grad_query_b_own.astype(jnp.bfloat16)),
        to_owner_ranks(grad_output_a_own.astype(jnp.bfloat16)),
        to_owner_ranks(jnp.stack([grad_key_b_own, grad_value_b_own]).astype(jnp.bfloat16)),
    ]
    sizes = [piece.shape[1] for piece in pieces]
    sent = jnp.concatenate(pieces, axis=1).reshape(group_count, -1, 128)
    got = lax.all_to_all(sent, "dp", split_axis=0, concat_axis=0, tiled=True)
    got = got.reshape(group_count, -1).astype(jnp.float32)
    placed_sums = jnp.einsum("sa,sn->an", pick_source, got, precision=precise)
    parts = []
    start = 0
    for size in sizes:
        parts.append(placed_sums[:, start : start + size])
        start += size
    ranks_own = RANK // group_count

    def columns_out(part, count):
        return part.reshape(ADAPTERS, count, RANK, block)

    def ranks_out(part, count):
        return part.reshape(ADAPTERS, count, ranks_own, width_local)

    query_a_sum = columns_out(parts[0], ATT_EXPERTS).transpose(1, 0, 3, 2)
    output_b_sum = columns_out(parts[1], ATT_EXPERTS).transpose(1, 0, 2, 3)
    kv_a_sum = columns_out(parts[2], 2).transpose(1, 0, 3, 2)
    mlp_sum = columns_out(parts[3], 3 * EXPERTS).transpose(1, 0, 2, 3)
    gate_a_sum = mlp_sum[:EXPERTS].transpose(0, 1, 3, 2)
    up_a_sum = mlp_sum[EXPERTS : 2 * EXPERTS].transpose(0, 1, 3, 2)
    down_b_sum = mlp_sum[2 * EXPERTS :]
    query_b_sum = ranks_out(parts[4], ATT_EXPERTS).transpose(1, 0, 2, 3)
    output_a_sum = ranks_out(parts[5], ATT_EXPERTS).transpose(1, 0, 3, 2)
    kv_b_sum = ranks_out(parts[6], 2).transpose(1, 0, 2, 3)

    def slice_sum(table):
        return lax.psum_scatter(
            table.astype(jnp.bfloat16), "shard", scatter_dimension=1, tiled=True
        ).astype(jnp.float32)

    gate_b_sum = slice_sum(grad_gate_table).reshape(ADAPTERS, RANK, -1)
    up_b_sum = slice_sum(grad_up_table).reshape(ADAPTERS, RANK, -1)
    down_a_sum = slice_sum(grad_down_table).reshape(ADAPTERS, RANK, -1).transpose(0, 2, 1)
    return (
        layer_out,
        input_grad,
        query_a_sum,
        query_b_sum,
        kv_a_sum[0],
        kv_b_sum[0],
        kv_a_sum[1],
        kv_b_sum[1],
        output_a_sum,
        output_b_sum,
        gate_a_sum,
        gate_b_sum,
        up_a_sum,
        up_b_sum,
        down_a_sum,
        down_b_sum,
    )


def solution(mesh):
    placed = (
        P(("dp", "shard"), None),
        P(("dp", "shard"), None),
        P(),
        P(),
        P(),
        P(),
        P(None, None, "shard"),
        P(None, "shard"),
        P(None, "shard"),
        P(None, "shard", None),
        P(None, "dp"),
        P(None, "dp"),
        P("dp", None),
        P(),
        P(None, None, None, "shard"),
        P(),
        P(None, None, "shard"),
        P(),
        P(None, None, "shard"),
        P(None, None, "shard", None),
        P(),
        P(),
        P(None, None, "dp"),
        P(),
        P(None, None, "dp"),
        P(None, "dp", None),
        P(),
        P(),
        P("dp", None),
        P(("dp", "shard"), None),
    )
    return jax.shard_map(
        on_device,
        mesh=mesh,
        in_specs=placed,
        out_specs=(
            P(("dp", "shard"), None),
            P(("dp", "shard"), None),
            P(None, None, ("dp", "shard"), None),
            P(None, None, "dp", "shard"),
            P(None, ("dp", "shard"), None),
            P(None, "dp", "shard"),
            P(None, ("dp", "shard"), None),
            P(None, "dp", "shard"),
            P(None, None, "shard", "dp"),
            P(None, None, None, ("dp", "shard")),
            P(None, None, ("dp", "shard"), None),
            P(None, None, ("dp", "shard")),
            P(None, None, ("dp", "shard"), None),
            P(None, None, ("dp", "shard")),
            P(None, ("dp", "shard"), None),
            P(None, None, None, ("dp", "shard")),
        ),
        check_vma=False,
    )
```

```python
import math

import jax
import jax.numpy as jnp
from jax import lax
from jax.experimental import pallas as pl
from jax.experimental.pallas import tpu as pltpu
from jax.sharding import PartitionSpec as P

D = 2048
HD = 128
EXPERTS = 8
ATT_EXPERTS = 8
ADAPTERS = 8
RANK = 16
LOW = 128
CHUNK = 128
GATE_LANE = 64
ROUTE_LANE = 96
ROUTER_ROW = 32


f32 = jnp.float32
bf16 = jnp.bfloat16
precise = lax.Precision.HIGHEST
eps = 1e-05
score_scale = HD ** (-0.5)


def nn(a, b):
    return lax.dot_general(a, b, (((1,), (0,)), ((), ())), preferred_element_type=f32)


def nt(a, b):
    return lax.dot_general(a, b, (((1,), (1,)), ((), ())), preferred_element_type=f32)


def tn(a, b):
    return lax.dot_general(a, b, (((0,), (0,)), ((), ())), preferred_element_type=f32)


def iota(shape, axis):
    return lax.broadcasted_iota(jnp.int32, shape, axis)


def ones_where(condition):
    return jnp.where(condition, 1.0, 0.0).astype(bf16)


def inverse_rms(values):
    return lax.rsqrt(jnp.mean(values * values, axis=-1, keepdims=True) + eps)


def norm_backward(values, inverse, gain_vector, grad_normed):
    weighted = gain_vector * grad_normed
    return inverse * weighted - values * (inverse * inverse * inverse) * jnp.mean(
        values * weighted, axis=-1, keepdims=True
    )


def softmax_pair(first, second):
    peak = jnp.maximum(first, second)
    one, two = jnp.exp(first - peak), jnp.exp(second - peak)
    total = one + two
    return one / total, two / total


def in_lane(column, lane, width=LOW):
    shape = (column.shape[0], width)
    return jnp.where(iota(shape, 1) == lane, column, 0.0)


def lane_of(values, lane):
    return jnp.sum(jnp.where(iota(values.shape, 1) == lane, values, 0.0), axis=1, keepdims=True)


def expert_lanes(dest, capacity, shape, group):
    lane = iota(shape, 1)
    low = (lane // group) * capacity
    return (dest >= low) & (dest < low + capacity)


def whole():
    return pl.BlockSpec(memory_space=pltpu.VMEM)


def sds(shape, dtype):
    return jax.ShapeDtypeStruct(shape, dtype)


def call(kernel, grid, in_specs, out_specs, out_shape, scratch, flops, moved):
    return pl.pallas_call(
        kernel,
        grid=grid,
        in_specs=in_specs,
        out_specs=out_specs,
        out_shape=out_shape,
        scratch_shapes=scratch,
        compiler_params=pltpu.CompilerParams(
            vmem_limit_bytes=60 * 1024 * 1024,
            dimension_semantics=("arbitrary",) * len(grid) if grid else None,
        ),
        cost_estimate=pl.CostEstimate(
            flops=4 * flops, bytes_accessed=4 * moved, transcendentals=0
        ),
    )


def rope(values, cosine, sine):
    return values * cosine + pltpu.roll(values, HD // 2, 1) * sine


def unrope(values, cosine, sine):
    return values * cosine - pltpu.roll(values, HD // 2, 1) * sine


def routed(route, shape):
    return (iota(shape, 1) // RANK) == route


def qkv_kernel(
    xn, wq, wk, wv, aq, amisc, bcat, kb, vb, routes, cosf, sinf,
    q_out, k_out, v_out, ga_out, low_out, misc_out, qsum,
):
    e = pl.program_id(0)
    s, width = k_out.shape
    heads = width // HD

    @pl.when(e == 0)
    def _():
        x = xn[...]
        low_out[...] = nt(x, aq[...]).astype(bf16)
        misc = nt(x, amisc[...])
        misc_out[...] = misc.astype(bf16)
        lane = iota((s, LOW), 1) - ROUTER_ROW
        gates = [
            jnp.sum(jnp.where(lane == routes[:, k : k + 1], misc, 0.0), axis=1, keepdims=True)
            for k in range(2)
        ]
        one, two = softmax_pair(*gates)
        ga_out[...] = in_lane(one, 0) + in_lane(two, 1)
        keys = nn(x, wk[...]) + nn(misc_out[...], kb[...])
        for h in range(heads):
            hs = slice(h * HD, (h + 1) * HD)
            k_out[:, hs] = rope(keys[:, hs], cosf[...], sinf[...]).astype(bf16)
        v_out[...] = (nn(x, wv[...]) + nn(misc_out[...], vb[...])).astype(bf16)
        for k in range(2):
            mine = routed(routes[:, k : k + 1], (s, LOW))
            low = jnp.where(mine, low_out[...], jnp.zeros((), bf16))
            qsum[k * s : (k + 1) * s, :] = nn(low, bcat[...])

    part = nn(xn[...], wq[0])
    for k in range(2):
        qsum[k * s : (k + 1) * s, :] += jnp.where(routes[:, k : k + 1] == e, part, 0.0)

    @pl.when(e == pl.num_programs(0) - 1)
    def _():
        for k in range(2):
            for h in range(heads):
                hs = slice(h * HD, (h + 1) * HD)
                at = slice(k * s, (k + 1) * s)
                q_out[at, hs] = rope(qsum[at, hs], cosf[...], sinf[...]).astype(bf16)


def causal(i, shape):
    row = (iota(shape, 0) & (CHUNK - 1)) + i * CHUNK
    return iota(shape, 1) <= row


def attend_kernel(q, k, v, ga, o_out, og_out, lse_out):
    s, width = k.shape
    for i in range(s // CHUNK):
        end = (i + 1) * CHUNK
        first, second = slice(i * CHUNK, end), slice(s + i * CHUNK, s + end)
        gates = [lane_of(ga[first, :], 0), lane_of(ga[first, :], 1)]
        log_totals = jnp.zeros((2 * CHUNK, LOW), f32)
        for h in range(width // HD):
            hs = slice(h * HD, (h + 1) * HD)
            queries = jnp.concatenate([q[first, hs], q[second, hs]], axis=0)
            scores = nt(queries, k[0:end, hs]) * score_scale
            scores = jnp.where(causal(i, scores.shape), scores, -1e30)
            peak = jnp.max(scores, axis=1, keepdims=True)
            weights = jnp.exp(scores - peak)
            total = jnp.sum(weights, axis=1, keepdims=True)
            mixed = nn(weights.astype(bf16), v[0:end, hs]) / total
            o_out[first, hs] = mixed[:CHUNK].astype(bf16)
            o_out[second, hs] = mixed[CHUNK:].astype(bf16)
            og_out[first, hs] = (mixed[:CHUNK] * gates[0]).astype(bf16)
            og_out[second, hs] = (mixed[CHUNK:] * gates[1]).astype(bf16)
            log_totals = log_totals + in_lane(peak + jnp.log(total), h)
        lse_out[first, :] = log_totals[:CHUNK]
        lse_out[second, :] = log_totals[CHUNK:]


def of_expert_rows(rows, routes, expert, s):
    return rows[0:s, :] * ones_where(routes[:, 0:1] == expert) + rows[s : 2 * s, :] * ones_where(
        routes[:, 1:2] == expert
    )


def out_kernel(og, wo, oa, ob, routes, attn_out, low_out, total):
    step = pl.program_id(0)
    s = attn_out.shape[0]
    batch = wo.shape[0]

    @pl.when(step == 0)
    def _():
        low = jnp.zeros((s, LOW), f32)
        for k in range(2):
            part = nt(og[k * s : (k + 1) * s, :], oa[...])
            low = low + jnp.where(routed(routes[:, k : k + 1], (s, LOW)), part, 0.0)
        low_out[...] = low.astype(bf16)
        total[...] = nn(low_out[...], ob[...])

    part = None
    for j in range(batch):
        new = nn(of_expert_rows(og, routes, step * batch + j, s), wo[j])
        part = new if part is None else part + new
    total[...] += part

    @pl.when(step == pl.num_programs(0) - 1)
    def _():
        attn_out[...] = total[...].astype(bf16)


def second_norm(attn, tokens, gain):
    hidden = tokens[...].astype(f32) + attn[...].astype(f32)
    inverse = inverse_rms(hidden)
    return hidden, inverse, gain[...].astype(f32)


def dispatch_kernel(cap, attn, tokens, cot, gain, router, mrow, mcol, rows_out, grads_out, gm_out, m_out):
    hidden, inverse, scale = second_norm(attn, tokens, gain)
    m = (hidden * inverse * scale).astype(bf16)
    m_out[...] = m
    logits = nt(m, router[...])
    gates = softmax_pair(
        *[
            jnp.sum(
                jnp.where(
                    expert_lanes(mcol[:, k : k + 1], cap, logits.shape, 1),
                    logits,
                    0.0,
                ),
                axis=1,
                keepdims=True,
            )
            for k in range(2)
        ]
    )
    gm_out[...] = in_lane(gates[0], 0) + in_lane(gates[1], 1)
    slot = iota((rows_out.shape[0], mrow.shape[1]), 0)
    picks = [ones_where(mrow[k : k + 1, :] == slot) for k in range(2)]
    rows_out[...] = nn(picks[0] + picks[1], m).astype(bf16)
    grad = cot[...].astype(f32)
    grads_out[...] = (
        nn(picks[0], (gates[0] * grad).astype(bf16)) + nn(picks[1], (gates[1] * grad).astype(bf16))
    ).astype(bf16)


def fold(first_lane):
    row, column = iota((LOW, LOW), 0), iota((LOW, LOW), 1)
    return ones_where(column == (row & (RANK - 1)) + first_lane)


def spread(first_lane):
    row, column = iota((LOW, LOW), 0), iota((LOW, LOW), 1)
    return ones_where(row == (column & (RANK - 1)) + first_lane)


def combine_kernel(cap, ze, attn, tokens, cot, gm, mcol, layer_out, dlm_out, low_out):
    hidden = tokens[...].astype(f32) + attn[...].astype(f32)
    grad = cot[...].astype(f32)
    lane = iota((mcol.shape[0], ze.shape[0]), 1)
    gates, slopes, lows = [], [], []
    for k in range(2):
        gates.append(lane_of(gm[...], k))
        pick = ones_where(mcol[:, k : k + 1] == lane)
        expert_out = nn(pick, ze[:, 0:D])
        lows.append(gates[k] * nn(pick, ze[:, D : D + LOW]))
        slopes.append(jnp.sum(grad * expert_out, axis=1, keepdims=True))
        hidden = hidden + gates[k] * expert_out
    layer_out[...] = hidden.astype(bf16)
    low_out[...] = lows[0] + pltpu.roll(lows[1], 3 * RANK, 1)
    mean = gates[0] * slopes[0] + gates[1] * slopes[1]
    total = jnp.zeros(dlm_out.shape, f32)
    for k in range(2):
        mine = expert_lanes(mcol[:, k : k + 1], cap, dlm_out.shape, 1)
        total = total + jnp.where(mine, gates[k] * (slopes[k] - mean), 0.0)
    dlm_out[...] = total.astype(bf16)


def hidden_grad_kernel(
    rows, dlm, low, attn, tokens, cot, gain, router, mcol, routes, dh1_out, da_out, low_out
):
    hidden, inverse, scale = second_norm(attn, tokens, gain)
    lane = iota((mcol.shape[0], rows.shape[0]), 1)
    picks = [ones_where(mcol[:, k : k + 1] == lane) for k in range(2)]
    grad_m = nn(picks[0] + picks[1], rows[:, 0:D]) + nn(dlm[...], router[...])
    lows = [nn(pick, rows[:, D : D + LOW]) for pick in picks]
    total = low[...] + lows[0] + pltpu.roll(lows[1], 3 * RANK, 1)
    for k in range(2):
        total = total + in_lane(routes[:, k : k + 1].astype(f32), ROUTE_LANE + k)
    low_out[...] = total.astype(bf16)
    grad = cot[...].astype(f32) + norm_backward(hidden, inverse, scale, grad_m)
    dh1_out[...] = grad
    da_out[...] = grad.astype(bf16)


def factor_kernel(low, columns, out):
    own = columns.shape[1] // 2
    count = low.shape[0]
    lane = (iota((count, LOW), 1) // RANK).astype(f32)
    lows = low[...]
    mine = [lane_of(lows.astype(f32), ROUTE_LANE + k) == lane for k in range(2)]
    for part in range(3):
        dense = jnp.zeros((count, LOW), f32)
        for k in range(2):
            wide = nn(lows, spread((3 * k + part) * RANK))
            dense = dense + jnp.where(mine[k], wide, 0.0)
        at = slice(own, 2 * own) if part == 2 else slice(0, own)
        out[part * LOW : (part + 1) * LOW, :] = tn(dense.astype(bf16), columns[:, at]).astype(bf16)


def expert_kernel(
    x, mask, ga, ua, db, gate_w, up_w, down_w, gate_b, up_b, down_a,
    ze_out, g_out, u_out, h_out, lg_out, lu_out, pd_out, total, pd,
):
    f = pl.program_id(0)

    @pl.when(f == 0)
    def _():
        lg_out[...] = nt(x[...], ga[...]).astype(bf16) * mask[...]
        lu_out[...] = nt(x[...], ua[...]).astype(bf16) * mask[...]
        total[...] = jnp.zeros_like(total)
        pd[...] = jnp.zeros_like(pd)

    gate = nn(x[...], gate_w[...]) + nn(lg_out[...], gate_b[...])
    up = nn(x[...], up_w[...]) + nn(lu_out[...], up_b[...])
    g_out[...] = gate.astype(bf16)
    u_out[...] = up.astype(bf16)
    hidden = (gate * jax.nn.sigmoid(gate) * up).astype(bf16)
    h_out[...] = hidden
    total[...] += nn(hidden, down_w[...])
    pd[...] += nt(hidden, down_a[...])

    @pl.when(f == pl.num_programs(0) - 1)
    def _():
        pd_out[...] = pd[...].astype(bf16) * mask[...]
        ze_out[:, 0:D] = (total[...] + nn(pd_out[...], db[...])).astype(bf16)
        ze_out[:, D : D + LOW] = nn(pd_out[...], fold(2 * RANK)).astype(bf16)


def identity():
    return ones_where(iota((LOW, LOW), 0) == iota((LOW, LOW), 1))


def down_grads_kernel(dy, mask, db, h, dpd_out, table_out, dpd_t):
    @pl.when(pl.program_id(0) == 0)
    def _():
        dpd_out[...] = nt(dy[...], db[...]).astype(bf16) * mask[...]
        dpd_t[...] = nt(identity(), dpd_out[...]).astype(bf16)

    table_out[0] = nn(dpd_t[...], h[...]).astype(bf16)


def expert_back_kernel(
    first, last,
    dy, mask, ga, ua, dpd, lg, lu, total_in, dlg_in, dlu_in,
    g, u, gate_w, up_w, down_w, gate_b, up_b, down_a,
    total, dlg, dlu, dm_out, tables_out, lg_t, lu_t,
):
    f = pl.program_id(0)

    @pl.when(f == 0)
    def _():
        lg_t[...] = nt(identity(), lg[...]).astype(bf16)
        lu_t[...] = nt(identity(), lu[...]).astype(bf16)
        if first:
            total[...] = jnp.zeros_like(total)
            dlg[...] = jnp.zeros_like(dlg)
            dlu[...] = jnp.zeros_like(dlu)
        else:
            total[...] = total_in[...]
            dlg[...] = dlg_in[...]
            dlu[...] = dlu_in[...]

    dh = nt(dy[...], down_w[...]) + nn(dpd[...], down_a[...])
    gate = g[...].astype(f32)
    up = u[...].astype(f32)
    sig = jax.nn.sigmoid(gate)
    act = gate * sig
    dgate = (dh * up * (sig + act * (1.0 - sig))).astype(bf16)
    dup = (dh * act).astype(bf16)
    total[...] += nt(dgate, gate_w[...]) + nt(dup, up_w[...])
    dlg[...] += nt(dgate, gate_b[...])
    dlu[...] += nt(dup, up_b[...])
    tables_out[0, 0:LOW, :] = nn(lg_t[...], dgate).astype(bf16)
    tables_out[0, LOW : 2 * LOW, :] = nn(lu_t[...], dup).astype(bf16)

    if last:

        @pl.when(f == pl.num_programs(0) - 1)
        def _():
            dlg_m = dlg[...].astype(bf16) * mask[...]
            dlu_m = dlu[...].astype(bf16) * mask[...]
            total_grad = total[...] + nn(dlg_m, ga[...]) + nn(dlu_m, ua[...])
            dm_out[:, 0:D] = total_grad.astype(bf16)
            dm_out[:, D : D + LOW] = (nn(dlg_m, fold(0)) + nn(dlu_m, fold(RANK))).astype(bf16)


def out_back_kernel(
    da, wo, oa, ob, routes, ga, o, do_out, stats_out, grad_oa_out, dzl, dosum
):
    e = pl.program_id(0)
    s = da.shape[0]
    width = o.shape[1]

    @pl.when(e == 0)
    def _():
        dzl[...] = nt(da[...], ob[...])
        for k in range(2):
            mine = routed(routes[:, k : k + 1], (s, LOW))
            low = jnp.where(mine, dzl[...], 0.0).astype(bf16)
            dosum[k * s : (k + 1) * s, :] = nn(low, oa[...])

    part = nt(da[...], wo[0])
    for k in range(2):
        dosum[k * s : (k + 1) * s, :] += jnp.where(routes[:, k : k + 1] == e, part, 0.0)

    @pl.when(e == pl.num_programs(0) - 1)
    def _():
        grad_oa = jnp.zeros((LOW, width), f32)
        for k in range(2):
            at = slice(k * s, (k + 1) * s)
            gate = lane_of(ga[...], k)
            mine = routed(routes[:, k : k + 1], (s, LOW))
            low = jnp.where(mine, gate * dzl[...], 0.0).astype(bf16)
            grad_oa = grad_oa + tn(low, o[at, :])
            stats = jnp.zeros((s, LOW), f32)
            slope = jnp.zeros((s, 1), f32)
            for h in range(width // HD):
                hs = slice(h * HD, (h + 1) * HD)
                before = dosum[at, hs]
                part = jnp.sum(o[at, hs].astype(f32) * before, axis=1, keepdims=True)
                slope = slope + part
                stats = stats + in_lane(gate * part, h)
                do_out[at, hs] = (gate * before).astype(bf16)
            stats_out[at, :] = stats + in_lane(slope, GATE_LANE)
        grad_oa_out[...] = grad_oa.astype(bf16)


def attend_back_kernel(
    q, k, v, do, lse, stats, cosf, sinf, bcat, kb, vb, low, misc, routes,
    dq_out, dk_out, dv_out, lows_out, misc_back_out, grad_qb_out, grad_kv_out, dk_sum, dv_sum,
):
    s, width = k.shape
    for h in range(width // HD):
        hs = slice(h * HD, (h + 1) * HD)
        dk_sum[...] = jnp.zeros_like(dk_sum)
        dv_sum[...] = jnp.zeros_like(dv_sum)
        for i in range(s // CHUNK):
            end = (i + 1) * CHUNK
            first, second = slice(i * CHUNK, end), slice(s + i * CHUNK, s + end)
            queries = jnp.concatenate([q[first, hs], q[second, hs]], axis=0)
            grads = jnp.concatenate([do[first, hs], do[second, hs]], axis=0)
            logs = jnp.concatenate(
                [lane_of(lse[first, :], h), lane_of(lse[second, :], h)], axis=0
            )
            centre = jnp.concatenate(
                [lane_of(stats[first, :], h), lane_of(stats[second, :], h)], axis=0
            )
            scores = nt(queries, k[0:end, hs]) * score_scale
            weights = jnp.where(causal(i, scores.shape), jnp.exp(scores - logs), 0.0)
            dscores = (weights * (nt(grads, v[0:end, hs]) - centre)).astype(bf16)
            dq = nn(dscores, k[0:end, hs]) * score_scale
            cosine, sine = cosf[first, :], sinf[first, :]
            dq_out[first, hs] = unrope(dq[:CHUNK], cosine, sine).astype(bf16)
            dq_out[second, hs] = unrope(dq[CHUNK:], cosine, sine).astype(bf16)
            dk_sum[0:end, :] += tn(dscores, queries)
            dv_sum[0:end, :] += tn(weights.astype(bf16), grads)
        dk_out[:, hs] = unrope(dk_sum[...] * score_scale, cosf[...], sinf[...]).astype(bf16)
        dv_out[:, hs] = dv_sum[...].astype(bf16)
    row, column = iota((LOW, LOW), 0), iota((LOW, LOW), 1)
    grad_qb = jnp.zeros((LOW, width), f32)
    for i in range(s // CHUNK):
        rs = slice(i * CHUNK, (i + 1) * CHUNK)
        misc_back = (nt(dk_out[rs, :], kb[...]) + nt(dv_out[rs, :], vb[...])).astype(bf16)
        lows = nn(misc_back, ones_where((column == row + 2 * RANK) & (row < 2 * RANK)))
        dense = jnp.zeros((CHUNK, LOW), f32)
        for j in range(2):
            at = slice(j * s + i * CHUNK, j * s + (i + 1) * CHUNK)
            mine = routed(routes[rs, j : j + 1], (CHUNK, LOW))
            part = jnp.where(mine, nt(dq_out[at, :], bcat[...]), 0.0).astype(bf16)
            dense = dense + part.astype(f32)
            fold = ones_where((column == (row & (RANK - 1)) + j * RANK) & (column < 2 * RANK))
            lows = lows + nn(part, fold)
            lows = lows + in_lane(lane_of(stats[at, :], GATE_LANE), GATE_LANE + j)
            grad_qb = grad_qb + tn(
                jnp.where(mine, low[rs, :], jnp.zeros((), bf16)), dq_out[at, :]
            )
        lows_out[rs, :] = lows.astype(bf16)
        misc_back_out[rs, 0:LOW] = dense.astype(bf16)
        misc_back_out[rs, LOW : 2 * LOW] = misc_back
    grad_qb_out[...] = grad_qb.astype(bf16)
    grad_kv_out[0:LOW, :] = tn(misc[...], dk_out[...]).astype(bf16)
    grad_kv_out[LOW : 2 * LOW, :] = tn(misc[...], dv_out[...]).astype(bf16)


def rows_back_kernel(dq, wq, dk, dv, wk, wv, aq, amisc, lows, routes, dx_out, total):
    step = pl.program_id(0)
    s = dk.shape[0]
    batch = wq.shape[0]

    @pl.when(step == 0)
    def _():
        total[...] = (
            nn(lows[:, 0:LOW], aq[...])
            + nn(lows[:, LOW : 2 * LOW], amisc[...])
            + nt(dk[...], wk[...])
            + nt(dv[...], wv[...])
        )

    part = None
    for j in range(batch):
        new = nt(of_expert_rows(dq, routes, step * batch + j, s), wq[j])
        part = new if part is None else part + new
    total[...] += part

    @pl.when(step == pl.num_programs(0) - 1)
    def _():
        dx_out[...] = total[...].astype(bf16)


def input_grad_kernel(dx, slopes, ga, tokens, gain, amisc, dh1, routes, out):
    x = tokens[...].astype(f32)
    gates = [lane_of(ga[...], k) for k in range(2)]
    slope = [lane_of(slopes[...].astype(f32), GATE_LANE + k) for k in range(2)]
    mean = gates[0] * slope[0] + gates[1] * slope[1]
    total = jnp.zeros(ga.shape, f32)
    lane = iota(ga.shape, 1) - ROUTER_ROW
    for k in range(2):
        mine = lane == routes[:, k : k + 1]
        total = total + jnp.where(mine, gates[k] * (slope[k] - mean), 0.0)
    grad = dx[...].astype(f32) + nn(total.astype(bf16), amisc[...])
    out[...] = dh1[...] + norm_backward(x, inverse_rms(x), gain[...].astype(f32), grad)


def after(value, *earlier):
    return lax.optimization_barrier((value, *earlier))[0]


def slot_places(routes, expert_count, capacity):
    choose = (routes[:, :, None] == jnp.arange(expert_count, dtype=jnp.int32)).astype(bf16)
    member = choose[:, 0] + choose[:, 1]
    count = routes.shape[0]
    before = (iota((count, count), 1) < iota((count, count), 0)).astype(bf16)
    slots = nn(before, member)
    mine = jnp.sum(slots[:, None, :] * choose.astype(f32), axis=2)
    return routes * capacity + mine.astype(jnp.int32)


def rotary_tables(count):
    half = HD // 2
    freq = jnp.exp(jnp.arange(half, dtype=f32) * (-2.0 * math.log(10000.0) / HD))
    angles = jnp.arange(count, dtype=jnp.int32).astype(f32)[:, None] * freq
    cosine, sine = jnp.cos(angles), jnp.sin(angles)
    return (
        jnp.concatenate([cosine, cosine], axis=1),
        jnp.concatenate([-sine, sine], axis=1),
    )


def on_device(
    tokens, cotangent, gain_first, gain_second, router_attn, router_mlp, query_w, key_w, value_w,
    output_w, gate_w, up_w, down_w, query_a, query_b, key_a, key_b, value_a, value_b, output_a,
    output_b, gate_a, gate_b, up_a, up_b, down_a, down_b, adapter_ids, attn_routes, mlp_routes,
):
    shards = lax.axis_size("shard")
    groups = lax.axis_size("dp")
    shard_at = lax.axis_index("shard")
    group_at = lax.axis_index("dp")
    rows = tokens.shape[0]
    seq = rows * shards
    cap_mlp = rows // 4 + rows // 16
    slices = groups // EXPERTS
    ff = gate_w.shape[1]
    width = key_w.shape[1]
    block = D // (groups * shards)
    own = groups * block
    adapter = adapter_ids[group_at]
    expert = group_at // slices

    x = tokens.astype(f32)
    normed = (x * inverse_rms(x) * gain_first.astype(f32)).astype(bf16)
    xn = lax.all_gather(normed, "shard", axis=0, tiled=True)

    mcol = slot_places(mlp_routes, EXPERTS, cap_mlp)
    mrow = mcol.T
    cosf, sinf = rotary_tables(seq)

    def ranks_first(factor):
        return jnp.swapaxes(factor, -1, -2)

    def of_adapter(factor, axis):
        return lax.dynamic_index_in_dim(factor, adapter, axis, keepdims=False)

    def pad_rows(parts, count=LOW):
        have = sum(p.shape[0] for p in parts)
        fill = jnp.zeros((count - have, parts[0].shape[1]), bf16)
        return jnp.concatenate(list(parts) + [fill], axis=0)

    aq = of_adapter(ranks_first(query_a), 1).reshape(LOW, D)
    amisc = pad_rows(
        [of_adapter(ranks_first(key_a), 0), of_adapter(ranks_first(value_a), 0), router_attn.T]
    )
    bcat = of_adapter(query_b, 1).reshape(LOW, width)
    key_second, value_second = of_adapter(key_b, 0), of_adapter(value_b, 0)
    kb = pad_rows([key_second])
    vb = pad_rows([jnp.zeros_like(value_second), value_second])
    oa = of_adapter(ranks_first(output_a), 1).reshape(LOW, width)
    ob = of_adapter(output_b, 1).reshape(LOW, D)
    router = pad_rows([router_mlp.T])
    gain1, gain2 = gain_first.reshape(1, D), gain_second.reshape(1, D)

    def of_expert(factor):
        return lax.dynamic_index_in_dim(factor, expert, 0, keepdims=False).reshape(LOW, D)

    gate_first = of_expert(ranks_first(gate_a))
    up_first = of_expert(ranks_first(up_a))
    down_second = of_expert(down_b)
    gate_table = gate_b.reshape(LOW, ff)
    up_table = up_b.reshape(LOW, ff)
    down_table = ranks_first(down_a).reshape(LOW, ff)
    expert_rows = groups * cap_mlp
    source_adapter = jnp.repeat(adapter_ids, cap_mlp)
    mask = (
        source_adapter[:, None] == (jnp.arange(LOW, dtype=jnp.int32) // RANK)[None, :]
    ).astype(bf16)

    experts = (ATT_EXPERTS,)
    batch = 2
    batches = (ATT_EXPERTS // batch,)
    projection = pl.BlockSpec((1, D, width), lambda e: (e, 0, 0))
    projections = pl.BlockSpec((batch, D, width), lambda e: (e, 0, 0))
    out_projection = pl.BlockSpec((1, width, D), lambda e: (e, 0, 0))
    out_projections = pl.BlockSpec((batch, width, D), lambda e: (e, 0, 0))
    project_flops = 2 * ATT_EXPERTS * seq * D * width
    weight_bytes = 2 * ATT_EXPERTS * D * width

    q, k, v, ga, low, misc = call(
        qkv_kernel,
        experts,
        [whole(), projection] + [whole()] * 10,
        [whole()] * 6,
        [
            sds((2 * seq, width), bf16),
            sds((seq, width), bf16),
            sds((seq, width), bf16),
            sds((seq, LOW), f32),
            sds((seq, LOW), bf16),
            sds((seq, LOW), bf16),
        ],
        [pltpu.VMEM((2 * seq, width), f32)],
        project_flops,
        weight_bytes,
    )(xn, query_w, key_w, value_w, aq, amisc, bcat, kb, vb, attn_routes, cosf, sinf)

    o, og, lse = call(
        attend_kernel,
        (),
        [whole()] * 4,
        [whole()] * 3,
        [
            sds((2 * seq, width), bf16),
            sds((2 * seq, width), bf16),
            sds((2 * seq, LOW), f32),
        ],
        [],
        8 * seq * seq * width,
        16 * seq * width,
    )(q, k, v, ga)

    attn_part, low_part = call(
        out_kernel,
        batches,
        [whole(), out_projections] + [whole()] * 3,
        [whole()] * 2,
        [sds((seq, D), bf16), sds((seq, LOW), bf16)],
        [pltpu.VMEM((seq, D), f32)],
        project_flops,
        weight_bytes,
    )(og, output_w, oa, ob, attn_routes)

    attn = lax.psum_scatter(attn_part, "shard", scatter_dimension=0, tiled=True)

    sent_rows = EXPERTS * cap_mlp
    rows_sent, grads_sent, gm, m = call(
        lambda *refs: dispatch_kernel(cap_mlp, *refs),
        (),
        [whole()] * 7,
        [whole()] * 4,
        [
            sds((sent_rows, D), bf16),
            sds((sent_rows, D), bf16),
            sds((rows, LOW), f32),
            sds((rows, D), bf16),
        ],
        [],
        6 * sent_rows * rows * D,
        8 * sent_rows * D,
    )(attn, tokens, cotangent, gain2, router, mrow, mcol)

    def to_experts(sent):
        sent = jnp.repeat(sent.reshape(EXPERTS, cap_mlp, D), slices, axis=0)
        got = lax.all_to_all(sent, "dp", split_axis=0, concat_axis=0, tiled=True)
        return got.reshape(expert_rows, D)

    def from_experts(made):
        got = lax.all_to_all(
            made.reshape(groups, cap_mlp, D + LOW), "dp", split_axis=0, concat_axis=0, tiled=True
        )
        if slices > 1:
            parts = got.reshape(EXPERTS, slices, cap_mlp, D + LOW).astype(f32)
            got = jnp.sum(parts, axis=1).astype(bf16)
        return got.reshape(sent_rows, D + LOW)

    def shifted(part, step):
        pairs = [(i, (i + step) % shards) for i in range(shards)]
        return lax.ppermute(part, "shard", pairs)

    def by_column_owner(part):
        split = part.reshape(rows, groups, shards, block)
        return split.transpose(2, 0, 1, 3).reshape(shards, rows, own)

    columns_sent = jnp.concatenate([by_column_owner(m), by_column_owner(cotangent)], axis=2)
    low_lanes = low_part.reshape(shards, rows, LOW).transpose(1, 0, 2).reshape(rows, shards * LOW)
    arrived = []
    for step in range(shards):
        piece = lax.dynamic_index_in_dim(
            columns_sent, lax.rem(shard_at + step, shards), 0, keepdims=False
        )
        piece = jnp.concatenate([piece, low_lanes], axis=1)
        arrived.append(shifted(piece, step) if step else piece)

    rows_in = to_experts(rows_sent)
    grads_in = to_experts(grads_sent)

    steps = 11
    each = ff // shards
    aligned = each % LOW == 0

    def spans(offset, span):
        if aligned:
            count, span = shards, span
            at = lambda f: pl.multiple_of(f * each + offset, LOW)
        else:
            count, span = steps, ff // steps
            at = lambda f: pl.multiple_of(f * (ff // steps), LOW)
        columns = pl.BlockSpec((pl.Element(D), pl.Element(span)), lambda f: (0, at(f)))
        weight_rows = pl.BlockSpec((pl.Element(span), pl.Element(D)), lambda f: (at(f), 0))
        table = pl.BlockSpec((pl.Element(LOW), pl.Element(span)), lambda f: (0, at(f)))
        kept = pl.BlockSpec((pl.Element(expert_rows), pl.Element(span)), lambda f: (0, at(f)))
        return count, span, columns, weight_rows, table, kept

    def by_shard(table):
        if aligned:
            return table
        return table.transpose(1, 0, 2).reshape(-1, shards, each).transpose(1, 0, 2)

    fb = ff // steps
    columns = pl.BlockSpec((D, fb), lambda f: (0, f))
    weight_rows = pl.BlockSpec((fb, D), lambda f: (f, 0))
    table = pl.BlockSpec((LOW, fb), lambda f: (0, f))
    kept = pl.BlockSpec((expert_rows, fb), lambda f: (0, f))
    expert_flops = 6 * expert_rows * D * ff
    expert_bytes = 6 * D * ff

    low_shape = sds((expert_rows, LOW), bf16)
    ze, g, u, hid, lg, lu, _ = call(
        expert_kernel,
        (steps,),
        [whole()] * 5 + [columns, columns, weight_rows, table, table, table],
        [whole(), kept, kept, kept, whole(), whole(), whole()],
        [sds((expert_rows, D + LOW), bf16)]
        + [sds((expert_rows, ff), bf16)] * 3
        + [low_shape, low_shape, low_shape],
        [pltpu.VMEM((expert_rows, D), f32), pltpu.VMEM((expert_rows, LOW), f32)],
        expert_flops,
        expert_bytes,
    )(rows_in, mask, gate_first, up_first, down_second, gate_w, up_w, down_w, gate_table, up_table, down_table)

    ze_back = from_experts(ze)

    hid, *arrived = lax.optimization_barrier((hid, *arrived))
    arrived = jnp.concatenate(arrived, axis=0)
    mlp_columns = arrived[:, : 2 * own]
    out_lows = jnp.sum(
        arrived[:, 2 * own :].reshape(shards, rows, shards, LOW).astype(f32), axis=0
    )
    out_lows = out_lows.astype(bf16).transpose(1, 0, 2).reshape(seq, LOW)

    count, span, _, _, _, kept = spans(0, each)
    dpd, down_part = call(
        down_grads_kernel,
        (count,),
        [whole()] * 3 + [kept],
        [whole(), pl.BlockSpec((1, LOW, span), lambda f: (f, 0, 0))],
        [low_shape, sds((count, LOW, span), bf16)],
        [pltpu.VMEM((LOW, expert_rows), bf16)],
        2 * expert_rows * LOW * ff,
        2 * expert_rows * ff,
    )(grads_in, mask, down_second, hid)

    def table_sum(part):
        part = by_shard(part)
        part = part.reshape(-1, part.shape[-1])
        return lax.psum_scatter(part, "shard", scatter_dimension=0, tiled=True)

    down_sum = table_sum(down_part)

    head = ((each // LOW + 1) // 2) * LOW
    pieces = [(0, head), (head, each - head)] if aligned else [(0, each)]
    low_sum = sds((expert_rows, LOW), f32)
    running = (jnp.zeros((8, LOW), f32),) * 3
    pair_parts = []
    for at, size in pieces:
        first, last = at == 0, at + size == each
        if not first:
            running = after(running, down_sum, ze_back)
        count, span, columns, weight_rows, table, kept = spans(at, size)
        made = call(
            lambda *refs, first=first, last=last: expert_back_kernel(first, last, *refs),
            (count,),
            [whole()] * 10
            + [kept, kept, columns, columns, weight_rows, table, table, table],
            [whole()] * 4 + [pl.BlockSpec((1, 2 * LOW, span), lambda f: (f, 0, 0))],
            [
                sds((expert_rows, D), f32),
                low_sum,
                low_sum,
                sds((expert_rows, D + LOW) if last else (16, LOW), bf16),
                sds((count, 2 * LOW, span), bf16),
            ],
            [pltpu.VMEM((LOW, expert_rows), bf16), pltpu.VMEM((LOW, expert_rows), bf16)],
            expert_flops * size // each,
            expert_bytes * size // each,
        )(grads_in, mask, gate_first, up_first, dpd, lg, lu, *running, g, u, gate_w, up_w, down_w, gate_table, up_table, down_table)
        running = made[:3]
        dm = made[3]
        pair_parts.append(made[4])

    dm_back = from_experts(dm)
    head_tables = table_sum(pair_parts[0])

    layer_out, dlm, low_down = call(
        lambda *refs: combine_kernel(cap_mlp, *refs),
        (),
        [whole()] * 6,
        [whole()] * 3,
        [sds((rows, D), bf16), sds((rows, LOW), bf16), sds((rows, LOW), f32)],
        [],
        4 * sent_rows * rows * D,
        4 * sent_rows * D,
    )(ze_back, attn, tokens, cotangent, gm, mcol)

    dm_back = after(dm_back, head_tables)
    dh1, da_own, low_mlp = call(
        hidden_grad_kernel,
        (),
        [whole()] * 10,
        [whole()] * 3,
        [sds((rows, D), f32), sds((rows, D), bf16), sds((rows, LOW), bf16)],
        [],
        2 * sent_rows * rows * D,
        4 * sent_rows * D,
    )(dm_back, dlm, low_down, attn, tokens, cotangent, gain2, router, mcol, mlp_routes)

    da = lax.all_gather(da_own, "shard", axis=0, tiled=True)
    mlp_lows = jnp.concatenate(
        [low_mlp] + [shifted(low_mlp, step) for step in range(1, shards)], axis=0
    )
    mlp_lows = after(mlp_lows, da)
    pair_tables = [head_tables] + [table_sum(after(part, da)) for part in pair_parts[1:]]
    factors = call(
        factor_kernel,
        (),
        [whole()] * 2,
        whole(),
        sds((3 * LOW, own), bf16),
        [],
        6 * seq * LOW * own,
        4 * seq * own,
    )(mlp_lows, mlp_columns)

    do, stats, grad_oa = call(
        out_back_kernel,
        experts,
        [whole(), out_projection] + [whole()] * 5,
        [whole()] * 3,
        [
            sds((2 * seq, width), bf16),
            sds((2 * seq, LOW), f32),
            sds((LOW, width), bf16),
        ],
        [pltpu.VMEM((seq, LOW), f32), pltpu.VMEM((2 * seq, width), f32)],
        project_flops,
        weight_bytes,
    )(da, output_w, oa, ob, attn_routes, ga, o)

    dq, dk, dv, lows, lows_dense, grad_qb, grad_kv = call(
        attend_back_kernel,
        (),
        [whole()] * 14,
        [whole()] * 7,
        [
            sds((2 * seq, width), bf16),
            sds((seq, width), bf16),
            sds((seq, width), bf16),
            sds((seq, LOW), bf16),
            sds((seq, 2 * LOW), bf16),
            sds((LOW, width), bf16),
            sds((2 * LOW, width), bf16),
        ],
        [pltpu.VMEM((seq, HD), f32), pltpu.VMEM((seq, HD), f32)],
        20 * seq * seq * width,
        16 * seq * width,
    )(q, k, v, do, lse, stats, cosf, sinf, bcat, kb, vb, low, misc, attn_routes)

    dx_part = call(
        rows_back_kernel,
        batches,
        [whole(), projections] + [whole()] * 8,
        whole(),
        sds((seq, D), bf16),
        [pltpu.VMEM((seq, D), f32)],
        project_flops,
        weight_bytes,
    )(dq, query_w, dk, dv, key_w, value_w, aq, amisc, lows_dense, attn_routes)

    column = jnp.arange(own, dtype=jnp.int32)
    own_at = (column // block) * (shards * block) + column % block
    dx_part, *pair_tables, grad_qb = lax.optimization_barrier((dx_part, *pair_tables, grad_qb))
    lows_parts = [lows] + [shifted(lows, step) for step in range(1, shards)]
    dx_part, *lows_parts = lax.optimization_barrier((dx_part, *lows_parts))
    lows_all = sum(part.astype(f32) for part in lows_parts).astype(bf16)
    dx = lax.psum_scatter(dx_part, "shard", scatter_dimension=0, tiled=True)

    own_rows = lambda array: lax.dynamic_slice_in_dim(array, shard_at * rows, rows, 0)

    input_grad = call(
        input_grad_kernel,
        (),
        [whole()] * 8,
        whole(),
        sds((rows, D), f32),
        [],
        2 * rows * LOW * D,
        24 * rows * D,
    )(dx, own_rows(lows_all), own_rows(ga), tokens, gain1, amisc, dh1, own_rows(attn_routes))

    select_own = (iota((D, own), 0) == (own_at + shard_at * block)[None, :]).astype(bf16)
    xn_own = nn(xn, select_own).astype(bf16)
    da_cols = nn(da, select_own).astype(bf16)
    lane = jnp.arange(LOW, dtype=jnp.int32)
    dense = jnp.zeros((seq, LOW), f32)
    for j in range(2):
        spread = (iota((LOW, LOW), 0) == (lane % RANK + j * RANK)[None, :]).astype(bf16)
        chosen = attn_routes[:, j : j + 1] == (lane // RANK)[None, :]
        dense = dense + jnp.where(chosen, nn(lows_all, spread), 0.0)
    grad_qa_own = tn(dense.astype(bf16), xn_own)
    grad_ob_own = tn(out_lows, da_cols)
    grad_kva_own = tn(lows_all[:, 2 * RANK : 4 * RANK], xn_own)

    def to_owner_columns(part):
        return part.reshape(-1, groups, block).transpose(1, 0, 2).reshape(groups, -1)

    def to_owner_ranks(part):
        parts = part.reshape(-1, groups, RANK // groups, width)
        return parts.transpose(1, 0, 2, 3).reshape(groups, -1)

    sending = [
        to_owner_columns(grad_qa_own.astype(bf16)),
        to_owner_columns(grad_ob_own.astype(bf16)),
        to_owner_columns(grad_kva_own.astype(bf16)),
        to_owner_ranks(grad_qb),
        to_owner_ranks(grad_oa),
        to_owner_ranks(jnp.concatenate([grad_kv[:RANK], grad_kv[LOW + RANK : LOW + 2 * RANK]])),
        to_owner_columns(factors),
    ]
    sizes = [piece.shape[1] for piece in sending]
    sent = jnp.concatenate(sending, axis=1).reshape(groups, -1, LOW)
    got = lax.all_to_all(sent, "dp", split_axis=0, concat_axis=0, tiled=True)
    got = got.reshape(groups, -1).astype(f32)
    pick_source = (adapter_ids[:, None] == jnp.arange(ADAPTERS, dtype=jnp.int32)[None, :]).astype(
        f32
    )
    placed_sums = jnp.einsum("sa,sn->an", pick_source, got, precision=precise)
    parts = []
    start = 0
    for size in sizes:
        parts.append(placed_sums[:, start : start + size])
        start += size
    ranks_own = RANK // groups

    def columns_out(part, count):
        return part.reshape(ADAPTERS, count, RANK, block)

    def ranks_out(part, count):
        return part.reshape(ADAPTERS, count, ranks_own, width)

    query_a_sum = columns_out(parts[0], ATT_EXPERTS).transpose(1, 0, 3, 2)
    output_b_sum = columns_out(parts[1], ATT_EXPERTS).transpose(1, 0, 2, 3)
    kv_a_sum = columns_out(parts[2], 2).transpose(1, 0, 3, 2)
    query_b_sum = ranks_out(parts[3], ATT_EXPERTS).transpose(1, 0, 2, 3)
    output_a_sum = ranks_out(parts[4], ATT_EXPERTS).transpose(1, 0, 3, 2)
    kv_b_sum = ranks_out(parts[5], 2).transpose(1, 0, 2, 3)
    factor_sum = columns_out(parts[6], 3 * EXPERTS).transpose(1, 0, 2, 3)
    gate_a_sum = factor_sum[:EXPERTS].transpose(0, 1, 3, 2)
    up_a_sum = factor_sum[EXPERTS : 2 * EXPERTS].transpose(0, 1, 3, 2)
    down_b_sum = factor_sum[2 * EXPERTS :]

    def widen(*parts):
        table = jnp.concatenate(parts, axis=1) if len(parts) > 1 else parts[0]
        return table.astype(f32).reshape(ADAPTERS, RANK, each)

    return (
        layer_out,
        input_grad,
        query_a_sum,
        query_b_sum,
        kv_a_sum[0],
        kv_b_sum[0],
        kv_a_sum[1],
        kv_b_sum[1],
        output_a_sum,
        output_b_sum,
        gate_a_sum,
        widen(*[t[:LOW] for t in pair_tables]),
        up_a_sum,
        widen(*[t[LOW:] for t in pair_tables]),
        ranks_first(widen(down_sum)),
        down_b_sum,
    )


def solution(mesh):
    placed = (
        P(("dp", "shard"), None),
        P(("dp", "shard"), None),
        P(),
        P(),
        P(),
        P(),
        P(None, None, "shard"),
        P(None, "shard"),
        P(None, "shard"),
        P(None, "shard", None),
        P(None, "dp"),
        P(None, "dp"),
        P("dp", None),
        P(),
        P(None, None, None, "shard"),
        P(),
        P(None, None, "shard"),
        P(),
        P(None, None, "shard"),
        P(None, None, "shard", None),
        P(),
        P(),
        P(None, None, "dp"),
        P(),
        P(None, None, "dp"),
        P(None, "dp", None),
        P(),
        P(),
        P("dp", None),
        P(("dp", "shard"), None),
    )
    return jax.shard_map(
        on_device,
        mesh=mesh,
        in_specs=placed,
        out_specs=(
            P(("dp", "shard"), None),
            P(("dp", "shard"), None),
            P(None, None, ("dp", "shard"), None),
            P(None, None, "dp", "shard"),
            P(None, ("dp", "shard"), None),
            P(None, "dp", "shard"),
            P(None, ("dp", "shard"), None),
            P(None, "dp", "shard"),
            P(None, None, "shard", "dp"),
            P(None, None, None, ("dp", "shard")),
            P(None, None, ("dp", "shard"), None),
            P(None, None, ("dp", "shard")),
            P(None, None, ("dp", "shard"), None),
            P(None, None, ("dp", "shard")),
            P(None, ("dp", "shard"), None),
            P(None, None, None, ("dp", "shard")),
        ),
        check_vma=False,
    )
```

```python
import math

import jax
import jax.numpy as jnp
from jax import lax
from jax.experimental import pallas as pl
from jax.experimental.pallas import tpu as pltpu
from jax.sharding import PartitionSpec as P

D = 2048
HD = 128
EXPERTS = 8
ATT_EXPERTS = 8
ADAPTERS = 8
RANK = 16
LOW = 128
CHUNK = 128
GATE_LANE = 64
ROUTE_LANE = 96
ROUTER_ROW = 32


f32 = jnp.float32
bf16 = jnp.bfloat16
precise = lax.Precision.HIGHEST
eps = 1e-05
score_scale = HD ** (-0.5)


def nn(a, b):
    return lax.dot_general(a, b, (((1,), (0,)), ((), ())), preferred_element_type=f32)


def nt(a, b):
    return lax.dot_general(a, b, (((1,), (1,)), ((), ())), preferred_element_type=f32)


def tn(a, b):
    return lax.dot_general(a, b, (((0,), (0,)), ((), ())), preferred_element_type=f32)


def iota(shape, axis):
    return lax.broadcasted_iota(jnp.int32, shape, axis)


def ones_where(condition):
    return jnp.where(condition, 1.0, 0.0).astype(bf16)


def inverse_rms(values):
    return lax.rsqrt(jnp.mean(values * values, axis=-1, keepdims=True) + eps)


def norm_backward(values, inverse, gain_vector, grad_normed):
    weighted = gain_vector * grad_normed
    return inverse * weighted - values * (inverse * inverse * inverse) * jnp.mean(
        values * weighted, axis=-1, keepdims=True
    )


def softmax_pair(first, second):
    peak = jnp.maximum(first, second)
    one, two = jnp.exp(first - peak), jnp.exp(second - peak)
    total = one + two
    return one / total, two / total


def in_lane(column, lane, width=LOW):
    shape = (column.shape[0], width)
    return jnp.where(iota(shape, 1) == lane, column, 0.0)


def lane_of(values, lane):
    return jnp.sum(jnp.where(iota(values.shape, 1) == lane, values, 0.0), axis=1, keepdims=True)


def expert_lanes(dest, capacity, shape, group):
    lane = iota(shape, 1)
    low = (lane // group) * capacity
    return (dest >= low) & (dest < low + capacity)


def whole():
    return pl.BlockSpec(memory_space=pltpu.VMEM)


def sds(shape, dtype):
    return jax.ShapeDtypeStruct(shape, dtype)


def call(kernel, grid, in_specs, out_specs, out_shape, scratch, flops, moved):
    return pl.pallas_call(
        kernel,
        grid=grid,
        in_specs=in_specs,
        out_specs=out_specs,
        out_shape=out_shape,
        scratch_shapes=scratch,
        compiler_params=pltpu.CompilerParams(
            vmem_limit_bytes=60 * 1024 * 1024,
            dimension_semantics=("arbitrary",) * len(grid) if grid else None,
        ),
        cost_estimate=pl.CostEstimate(
            flops=4 * flops, bytes_accessed=4 * moved, transcendentals=0
        ),
    )


def rope(values, cosine, sine):
    return values * cosine + pltpu.roll(values, HD // 2, 1) * sine


def unrope(values, cosine, sine):
    return values * cosine - pltpu.roll(values, HD // 2, 1) * sine


def routed(route, shape):
    return (iota(shape, 1) // RANK) == route


def select_add(total, part, routes, expert):
    s = part.shape[0]
    for k in range(2):
        total[k * s : (k + 1) * s, :] += jnp.where(routes[:, k : k + 1] == expert, part, 0.0)


def copies(sources, targets, sems):
    return [
        pltpu.make_async_copy(source, target, sems.at[j])
        for j, (source, target) in enumerate(zip(sources, targets, strict=True))
    ]


def join_rows(places, left, parts, out):
    split, rows = left.shape[1], parts[0].shape[0]
    out[:, 0:split] = left[...]
    for j, part in enumerate(parts):
        at = pl.ds(pl.multiple_of(places[j] * rows, 16), rows)
        out[at, split:] = part[:, 0 : out.shape[1] - split]


def attention_kernel(shards, places, left, *refs):
    parts, refs = refs[:shards], refs[shards:]
    *refs, xn = refs

    @pl.when(pl.program_id(0) == 0)
    def _():
        join_rows(places, left, parts, xn)

    attention_steps(xn, *refs)


def attention_steps(
    xn, wq, wo, ob, wk_far, wv_far, aq, amisc, bcat, kb, vb, routes, cosf, sinf, oa,
    attn_out, out_low, q_far, k_far, v_far, ga_far, low_far, misc_far, o_far, lse_far,
    q, k, v, ga, low, misc, o, lse, qsum, og, chosen, wk, wv, load_sems, save_sems,
):
    step = pl.program_id(0)
    s, width = k.shape
    loads = copies((wk_far, wv_far), (wk, wv), load_sems)
    saves = copies(
        (q, k, v, ga, low, misc, o, lse),
        (q_far, k_far, v_far, ga_far, low_far, misc_far, o_far, lse_far),
        save_sems,
    )

    @pl.when(step == 0)
    def _():
        for load in loads:
            load.start()
        x = xn[...]
        low[...] = nt(x, aq[...]).astype(bf16)
        scores = nt(x, amisc[...])
        misc[...] = scores.astype(bf16)
        lane = iota((s, LOW), 1) - ROUTER_ROW
        gates = [
            jnp.sum(jnp.where(lane == routes[:, j : j + 1], scores, 0.0), axis=1, keepdims=True)
            for j in range(2)
        ]
        one, two = softmax_pair(*gates)
        ga[...] = in_lane(one, 0) + in_lane(two, 1)
        for j in range(2):
            mine = routed(routes[:, j : j + 1], (s, LOW))
            part = jnp.where(mine, low[...], jnp.zeros((), bf16))
            qsum[j * s : (j + 1) * s, :] = nn(part, bcat[...])

    @pl.when(step < ATT_EXPERTS)
    def _():
        select_add(qsum, nn(xn[...], wq[0]), routes, step)

    @pl.when(step == ATT_EXPERTS - 1)
    def _():
        for load in loads:
            load.wait()
        x = xn[...]
        keys = nn(x, wk[...]) + nn(misc[...], kb[...])
        for h in range(width // HD):
            hs = slice(h * HD, (h + 1) * HD)
            k[:, hs] = rope(keys[:, hs], cosf[...], sinf[...]).astype(bf16)
            for j in range(2):
                at = slice(j * s, (j + 1) * s)
                q[at, hs] = rope(qsum[at, hs], cosf[...], sinf[...]).astype(bf16)
        v[...] = (nn(x, wv[...]) + nn(misc[...], vb[...])).astype(bf16)
        attend(q, k, v, ga, o, og, lse)
        for save in saves:
            save.start()
        total = jnp.zeros((s, LOW), f32)
        for j in range(2):
            part = nt(og[j * s : (j + 1) * s, :], oa[...])
            total = total + jnp.where(routed(routes[:, j : j + 1], (s, LOW)), part, 0.0)
        out_low[...] = total.astype(bf16)
        spread_rows(og, routes, chosen)

    @pl.when(step >= ATT_EXPERTS)
    def _():
        weights = wo[...].reshape(chosen.shape[1], wo.shape[2])
        attn_out[...] = (nn(chosen[...], weights) + nn(out_low[...], ob[...])).astype(bf16)

    @pl.when(step == pl.num_programs(0) - 1)
    def _():
        for save in saves:
            save.wait()


def spread_rows(pair, routes, chosen):
    s, width = chosen.shape[0], pair.shape[1]
    for e in range(ATT_EXPERTS):
        chosen[:, e * width : (e + 1) * width] = of_expert_rows(pair, routes, e, s)


def causal(i, shape):
    row = (iota(shape, 0) & (CHUNK - 1)) + i * CHUNK
    return iota(shape, 1) <= row


def attend(q, k, v, ga, o_out, og_out, lse_out):
    s, width = k.shape
    for i in range(s // CHUNK):
        end = (i + 1) * CHUNK
        first, second = slice(i * CHUNK, end), slice(s + i * CHUNK, s + end)
        gates = [lane_of(ga[first, :], 0), lane_of(ga[first, :], 1)]
        log_totals = jnp.zeros((2 * CHUNK, LOW), f32)
        for h in range(width // HD):
            hs = slice(h * HD, (h + 1) * HD)
            queries = jnp.concatenate([q[first, hs], q[second, hs]], axis=0)
            scores = nt(queries, k[0:end, hs]) * score_scale
            scores = jnp.where(causal(i, scores.shape), scores, -1e30)
            peak = jnp.max(scores, axis=1, keepdims=True)
            weights = jnp.exp(scores - peak)
            total = jnp.sum(weights, axis=1, keepdims=True)
            mixed = nn(weights.astype(bf16), v[0:end, hs]) / total
            o_out[first, hs] = mixed[:CHUNK].astype(bf16)
            o_out[second, hs] = mixed[CHUNK:].astype(bf16)
            og_out[first, hs] = (mixed[:CHUNK] * gates[0]).astype(bf16)
            og_out[second, hs] = (mixed[CHUNK:] * gates[1]).astype(bf16)
            log_totals = log_totals + in_lane(peak + jnp.log(total), h)
        lse_out[first, :] = log_totals[:CHUNK]
        lse_out[second, :] = log_totals[CHUNK:]


def of_expert_rows(rows, routes, expert, s):
    return rows[0:s, :] * ones_where(routes[:, 0:1] == expert) + rows[s : 2 * s, :] * ones_where(
        routes[:, 1:2] == expert
    )


def second_norm(attn, tokens, gain):
    hidden = tokens[...].astype(f32) + attn[...].astype(f32)
    inverse = inverse_rms(hidden)
    return hidden, inverse, gain[...].astype(f32)


def dispatch_kernel(cap, attn, tokens, gain, router, mrow, mcol, rows_out, gm_out, m_out):
    hidden, inverse, scale = second_norm(attn, tokens, gain)
    m = (hidden * inverse * scale).astype(bf16)
    m_out[...] = m
    logits = nt(m, router[...])
    gates = softmax_pair(
        *[
            jnp.sum(
                jnp.where(
                    expert_lanes(mcol[:, k : k + 1], cap, logits.shape, 1),
                    logits,
                    0.0,
                ),
                axis=1,
                keepdims=True,
            )
            for k in range(2)
        ]
    )
    gm_out[...] = in_lane(gates[0], 0) + in_lane(gates[1], 1)
    slot = iota((rows_out.shape[0], mrow.shape[1]), 0)
    picks = [ones_where(mrow[k : k + 1, :] == slot) for k in range(2)]
    rows_out[:, 0:D] = nn(picks[0] + picks[1], m).astype(bf16)
    total = jnp.zeros((rows_out.shape[0], LOW), f32)
    for k in range(2):
        high = gates[k].astype(bf16).astype(f32)
        middle = (gates[k] - high).astype(bf16).astype(f32)
        both = in_lane(high, 0) + in_lane(middle, 1)
        total = total + nn(picks[k], both.astype(bf16))
    rows_out[:, D : D + LOW] = total.astype(bf16)


def fold(first_lane):
    row, column = iota((LOW, LOW), 0), iota((LOW, LOW), 1)
    return ones_where(column == (row & (RANK - 1)) + first_lane)


def spread(first_lane):
    row, column = iota((LOW, LOW), 0), iota((LOW, LOW), 1)
    return ones_where(row == (column & (RANK - 1)) + first_lane)


def combine_kernel(cap, ze, attn, tokens, cot, gm, mcol, layer_out, dlm_out, low_out):
    hidden = tokens[...].astype(f32) + attn[...].astype(f32)
    grad = cot[...].astype(f32)
    lane = iota((mcol.shape[0], ze.shape[0]), 1)
    gates, slopes, lows = [], [], []
    for k in range(2):
        gates.append(lane_of(gm[...], k))
        pick = ones_where(mcol[:, k : k + 1] == lane)
        expert_out = nn(pick, ze[:, 0:D])
        lows.append(gates[k] * nn(pick, ze[:, D : D + LOW]))
        slopes.append(jnp.sum(grad * expert_out, axis=1, keepdims=True))
        hidden = hidden + gates[k] * expert_out
    layer_out[...] = hidden.astype(bf16)
    low_out[...] = lows[0] + pltpu.roll(lows[1], 3 * RANK, 1)
    mean = gates[0] * slopes[0] + gates[1] * slopes[1]
    total = jnp.zeros(dlm_out.shape, f32)
    for k in range(2):
        mine = expert_lanes(mcol[:, k : k + 1], cap, dlm_out.shape, 1)
        total = total + jnp.where(mine, gates[k] * (slopes[k] - mean), 0.0)
    dlm_out[...] = total.astype(bf16)


def hidden_grad_kernel(
    rows, dlm, low, attn, tokens, cot, gain, router, mcol, routes, dh1_out, da_left, da_right
):
    hidden, inverse, scale = second_norm(attn, tokens, gain)
    lane = iota((mcol.shape[0], rows.shape[0]), 1)
    picks = [ones_where(mcol[:, k : k + 1] == lane) for k in range(2)]
    grad_m = nn(picks[0] + picks[1], rows[:, 0:D]) + nn(dlm[:, 0 : router.shape[0]], router[...])
    lows = [nn(pick, rows[:, D : D + LOW]) for pick in picks]
    total = low[...] + lows[0] + pltpu.roll(lows[1], 3 * RANK, 1)
    for k in range(2):
        total = total + in_lane(routes[:, k : k + 1].astype(f32), ROUTE_LANE + k)
    grad = cot[...].astype(f32) + norm_backward(hidden, inverse, scale, grad_m)
    dh1_out[...] = grad
    split = da_left.shape[1]
    da_left[...] = grad[:, :split].astype(bf16)
    da_right[:, 0 : D - split] = grad[:, split:].astype(bf16)
    da_right[:, D - split :] = total.astype(bf16)


def select_columns(places, shards, select):
    row, column = iota(select.shape, 0), iota(select.shape, 1)
    size = places[shards]
    group = lax.div(column, size)
    source = group * (size * shards) + places[0] * size + (column - group * size)
    select[...] = ones_where(row == source)


def own_columns_kernel(shards, places, *refs):
    parts, (out, gathered, select) = refs[: shards + 1], refs[shards + 1 :]
    select_columns(places, shards, select)
    join_rows(places, parts[0], parts[1:], gathered)
    out[...] = nn(gathered[...], select[...]).astype(bf16)


def owner_kernel(shards, places, *refs):
    da_refs, refs = refs[: shards + 1], refs[shards + 1 :]
    out_lows, columns, factors, grad_ob, da_own, gathered, select = refs
    own = da_own.shape[1]
    select_columns(places, shards, select)
    join_rows(places, da_refs[0], da_refs[1:], gathered)
    da_own[...] = nn(gathered[...], select[...]).astype(bf16)
    grad_ob[...] = tn(out_lows[...], da_own[...]).astype(bf16)
    right = D - da_refs[0].shape[1]
    lows = jnp.concatenate([ref[:, right : right + LOW] for ref in da_refs[1:]], axis=0)
    lane = (iota(lows.shape, 1) // RANK).astype(f32)
    mine = [lane_of(lows.astype(f32), ROUTE_LANE + k) == lane for k in range(2)]
    for part in range(3):
        dense = jnp.zeros(lows.shape, f32)
        for k in range(2):
            wide = nn(lows, spread((3 * k + part) * RANK))
            dense = dense + jnp.where(mine[k], wide, 0.0)
        at = slice(own, 2 * own) if part == 2 else slice(0, own)
        factors[part * LOW : (part + 1) * LOW, :] = tn(dense.astype(bf16), columns[:, at]).astype(
            bf16
        )


def identity():
    return ones_where(iota((LOW, LOW), 0) == iota((LOW, LOW), 1))


def expert_up_kernel(
    x, mask, ga, ua, gate_w, up_w, gate_b, up_b, g_out, u_out, lg_out, lu_out
):
    x = x.at[:, 0:D]

    @pl.when(pl.program_id(0) == 0)
    def _():
        lg_out[...] = nt(x[...], ga[...]).astype(bf16) * mask[...]
        lu_out[...] = nt(x[...], ua[...]).astype(bf16) * mask[...]

    g_out[...] = (nn(x[...], gate_w[...]) + nn(lg_out[...], gate_b[...])).astype(bf16)
    u_out[...] = (nn(x[...], up_w[...]) + nn(lu_out[...], up_b[...])).astype(bf16)


def expert_down_kernel(
    grads, x, mask, db, lg, lu, g, u, down_w, gate_b, up_b, down_a,
    ze_out, dg_out, du_out, dlg_out, dlu_out, *rest,
):
    *tables_out, dy, total, pd, dlg, dlu, dpd, lg_t, lu_t, dpd_t, tables = rest
    f = pl.program_id(0)
    width = down_w.shape[0]

    @pl.when(f == 0)
    def _():
        gate = x[:, D : D + LOW].astype(f32)
        gate = lane_of(gate, 0) + lane_of(gate, 1)
        dy[...] = (gate * grads[...].astype(f32)).astype(bf16)
        dpd[...] = nt(dy[...], db[...]).astype(bf16) * mask[...]
        lg_t[...] = nt(identity(), lg[...]).astype(bf16)
        lu_t[...] = nt(identity(), lu[...]).astype(bf16)
        dpd_t[...] = nt(identity(), dpd[...]).astype(bf16)
        for sums in (total, pd, dlg, dlu):
            sums[...] = jnp.zeros_like(sums)

    dh = nt(dy[...], down_w[...]) + nn(dpd[...], down_a[...])
    gate = g[...].astype(f32)
    up = u[...].astype(f32)
    sig = jax.nn.sigmoid(gate)
    act = gate * sig
    hidden = (act * up).astype(bf16)
    dgate = (dh * up * (sig + act * (1.0 - sig))).astype(bf16)
    dup = (dh * act).astype(bf16)
    dg_out[...] = dgate
    du_out[...] = dup
    total[...] += nn(hidden, down_w[...])
    pd[...] += nt(hidden, down_a[...])
    dlg[...] += nt(dgate, gate_b[...])
    dlu[...] += nt(dup, up_b[...])
    at = pl.ds(pl.multiple_of(f * width, LOW), width)
    tables[0:LOW, at] = nn(lg_t[...], dgate).astype(bf16)
    tables[LOW : 2 * LOW, at] = nn(lu_t[...], dup).astype(bf16)
    tables[2 * LOW : 3 * LOW, at] = nn(dpd_t[...], hidden).astype(bf16)

    @pl.when(f == pl.num_programs(0) - 1)
    def _():
        low = pd[...].astype(bf16) * mask[...]
        ze_out[:, 0:D] = (total[...] + nn(low, db[...])).astype(bf16)
        ze_out[:, D : D + LOW] = nn(low, fold(2 * RANK)).astype(bf16)
        dlg_out[...] = dlg[...].astype(bf16) * mask[...]
        dlu_out[...] = dlu[...].astype(bf16) * mask[...]
        first = 0
        for out in tables_out:
            parts, _, size = out.shape
            for z in range(parts):
                start = z * (tables.shape[1] // parts) + first
                out[z] = tables[:, start : start + size]
            first += size


def expert_rows_kernel(dg, du, dlg, dlu, gate_w, up_w, ga, ua, dm_out):
    n = pl.program_id(0)
    width = gate_w.shape[0]

    @pl.when(n == 0)
    def _():
        low = nn(dlg[...], fold(0)) + nn(dlu[...], fold(RANK))
        dm_out[:, D : D + LOW] = low.astype(bf16)

    total = nt(dg[...], gate_w[...]) + nt(du[...], up_w[...])
    total = total + nn(dlg[...], ga[...]) + nn(dlu[...], ua[...])
    dm_out[:, pl.ds(pl.multiple_of(n * width, LOW), width)] = total.astype(bf16)


def attention_back_kernel(shards, places, left, *refs):
    parts, refs = refs[:shards], refs[shards:]
    *refs, da = refs

    @pl.when(pl.program_id(0) == 0)
    def _():
        join_rows(places, left, parts, da)

    attention_back_steps(da, *refs)


def attention_back_steps(
    da, wo, wq, wk, wv, aq, amisc, bcat, kb, vb, oa, ob, routes,
    ga_far, o_far, q_far, k_far, v_far, lse_far, low_far, misc_far, cosf_far, sinf_far,
    dx_out, lows_out, grad_oa_out, grad_qb_out, grad_kv_out,
    ga, o, q, k, v, lse, low, misc, cosf, sinf, sems,
    dzl, dosum, do, stats, dq, dk, dv, lows_dense, dk_sum, dv_sum, chosen,
):
    step = pl.program_id(0)
    s, width = k.shape
    loads = copies(
        (ga_far, o_far, q_far, k_far, v_far, lse_far, low_far, misc_far, cosf_far, sinf_far),
        (ga, o, q, k, v, lse, low, misc, cosf, sinf),
        sems,
    )

    @pl.when(step == 0)
    def _():
        for load in loads:
            load.start()
        dzl[...] = nt(da[...], ob[...])
        for j in range(2):
            mine = routed(routes[:, j : j + 1], (s, LOW))
            part = jnp.where(mine, dzl[...], 0.0).astype(bf16)
            dosum[j * s : (j + 1) * s, :] = nn(part, oa[...])

    @pl.when(step < ATT_EXPERTS)
    def _():
        select_add(dosum, nt(da[...], wo[0]), routes, step)

    @pl.when(step == ATT_EXPERTS - 1)
    def _():
        for load in loads:
            load.wait()
        out_back(routes, ga, o, dzl, dosum, do, stats, grad_oa_out)
        attend_back(
            q, k, v, do, lse, stats, cosf, sinf, bcat, kb, vb, low, misc, routes,
            dq, dk, dv, lows_out, lows_dense, grad_qb_out, grad_kv_out, dk_sum, dv_sum,
        )
        spread_rows(dq, routes, chosen)

    @pl.when(step >= ATT_EXPERTS)
    def _():
        total = (
            nn(lows_dense[:, 0:LOW], aq[...])
            + nn(lows_dense[:, LOW : 2 * LOW], amisc[...])
            + nt(dk[...], wk[...])
            + nt(dv[...], wv[...])
        )
        for e in range(ATT_EXPERTS):
            total = total + nt(chosen[:, e * width : (e + 1) * width], wq[e])
        dx_out[...] = total.astype(bf16)


def out_back(routes, ga, o, dzl, dosum, do_out, stats_out, grad_oa_out):
    s, width = o.shape[0] // 2, o.shape[1]
    grad_oa = jnp.zeros((LOW, width), f32)
    for k in range(2):
        at = slice(k * s, (k + 1) * s)
        gate = lane_of(ga[...], k)
        mine = routed(routes[:, k : k + 1], (s, LOW))
        low = jnp.where(mine, gate * dzl[...], 0.0).astype(bf16)
        grad_oa = grad_oa + tn(low, o[at, :])
        stats = jnp.zeros((s, LOW), f32)
        slope = jnp.zeros((s, 1), f32)
        for h in range(width // HD):
            hs = slice(h * HD, (h + 1) * HD)
            before = dosum[at, hs]
            part = jnp.sum(o[at, hs].astype(f32) * before, axis=1, keepdims=True)
            slope = slope + part
            stats = stats + in_lane(gate * part, h)
            do_out[at, hs] = (gate * before).astype(bf16)
        stats_out[at, :] = stats + in_lane(slope, GATE_LANE)
    grad_oa_out[...] = grad_oa.astype(bf16)


def attend_back(
    q, k, v, do, lse, stats, cosf, sinf, bcat, kb, vb, low, misc, routes,
    dq_out, dk_out, dv_out, lows_out, misc_back_out, grad_qb_out, grad_kv_out, dk_sum, dv_sum,
):
    s, width = k.shape
    for h in range(width // HD):
        hs = slice(h * HD, (h + 1) * HD)
        dk_sum[...] = jnp.zeros_like(dk_sum)
        dv_sum[...] = jnp.zeros_like(dv_sum)
        for i in range(s // CHUNK):
            end = (i + 1) * CHUNK
            first, second = slice(i * CHUNK, end), slice(s + i * CHUNK, s + end)
            queries = jnp.concatenate([q[first, hs], q[second, hs]], axis=0)
            grads = jnp.concatenate([do[first, hs], do[second, hs]], axis=0)
            logs = jnp.concatenate(
                [lane_of(lse[first, :], h), lane_of(lse[second, :], h)], axis=0
            )
            centre = jnp.concatenate(
                [lane_of(stats[first, :], h), lane_of(stats[second, :], h)], axis=0
            )
            scores = nt(queries, k[0:end, hs]) * score_scale
            weights = jnp.where(causal(i, scores.shape), jnp.exp(scores - logs), 0.0)
            dscores = (weights * (nt(grads, v[0:end, hs]) - centre)).astype(bf16)
            dq = nn(dscores, k[0:end, hs]) * score_scale
            cosine, sine = cosf[first, :], sinf[first, :]
            dq_out[first, hs] = unrope(dq[:CHUNK], cosine, sine).astype(bf16)
            dq_out[second, hs] = unrope(dq[CHUNK:], cosine, sine).astype(bf16)
            dk_sum[0:end, :] += tn(dscores, queries)
            dv_sum[0:end, :] += tn(weights.astype(bf16), grads)
        dk_out[:, hs] = unrope(dk_sum[...] * score_scale, cosf[...], sinf[...]).astype(bf16)
        dv_out[:, hs] = dv_sum[...].astype(bf16)
    row, column = iota((LOW, LOW), 0), iota((LOW, LOW), 1)
    grad_qb = jnp.zeros((LOW, width), f32)
    chunks = s // CHUNK
    half = chunks // 2
    packed = [None] * half
    slopes = jnp.zeros((16, LOW), f32)
    line, at_lane = iota((16, LOW), 0), iota((16, LOW), 1) == GATE_LANE
    for i in range(chunks):
        rs = slice(i * CHUNK, (i + 1) * CHUNK)
        misc_back = (nt(dk_out[rs, :], kb[...]) + nt(dv_out[rs, :], vb[...])).astype(bf16)
        lows = nn(misc_back, ones_where((column == row + 2 * RANK) & (row < 2 * RANK)))
        dense = jnp.zeros((CHUNK, LOW), f32)
        for j in range(2):
            at = slice(j * s + i * CHUNK, j * s + (i + 1) * CHUNK)
            mine = routed(routes[rs, j : j + 1], (CHUNK, LOW))
            part = jnp.where(mine, nt(dq_out[at, :], bcat[...]), 0.0).astype(bf16)
            dense = dense + part.astype(f32)
            fold_pair = ones_where((column == (row & (RANK - 1)) + j * RANK) & (column < 2 * RANK))
            lows = lows + nn(part, fold_pair)
            mark = ones_where((line == j * chunks + i) & at_lane)
            slopes = slopes + nt(mark, stats[at, :].astype(bf16))
            grad_qb = grad_qb + tn(
                jnp.where(mine, low[rs, :], jnp.zeros((), bf16)), dq_out[at, :]
            )
        if i < half:
            packed[i] = lows
        else:
            together = packed[i - half] + pltpu.roll(lows, LOW // 2, 1)
            lows_out[(i - half) * CHUNK : (i - half + 1) * CHUNK, :] = together.astype(bf16)
        misc_back_out[rs, 0:LOW] = dense.astype(bf16)
        misc_back_out[rs, LOW : 2 * LOW] = misc_back
    lows_out[half * CHUNK : half * CHUNK + 16, :] = slopes.astype(bf16)
    grad_qb_out[...] = grad_qb.astype(bf16)
    grad_kv_out[0:LOW, :] = tn(misc[...], dk_out[...]).astype(bf16)
    grad_kv_out[LOW : 2 * LOW, :] = tn(misc[...], dv_out[...]).astype(bf16)


def input_grad_kernel(dx, slopes, ga, tokens, gain, router, dh1, routes, out):
    x = tokens[...].astype(f32)
    gates = [lane_of(ga[...], k) for k in range(2)]
    slope = [slopes[:, k : k + 1] for k in range(2)]
    mean = gates[0] * slope[0] + gates[1] * slope[1]
    total = jnp.zeros(ga.shape, f32)
    lane = iota(ga.shape, 1)
    for k in range(2):
        mine = lane == routes[:, k : k + 1]
        total = total + jnp.where(mine, gates[k] * (slope[k] - mean), 0.0)
    grad = dx[...].astype(f32) + nn(total[:, 0 : router.shape[0]].astype(bf16), router[...])
    out[...] = dh1[...] + norm_backward(x, inverse_rms(x), gain[...].astype(f32), grad)


def after(value, *earlier):
    return lax.optimization_barrier((value, *earlier))[0]


def slot_places(routes, expert_count, capacity):
    choose = (routes[:, :, None] == jnp.arange(expert_count, dtype=jnp.int32)).astype(bf16)
    member = choose[:, 0] + choose[:, 1]
    count = routes.shape[0]
    before = (iota((count, count), 1) < iota((count, count), 0)).astype(bf16)
    slots = nn(before, member)
    mine = jnp.sum(slots[:, None, :] * choose.astype(f32), axis=2)
    return routes * capacity + mine.astype(jnp.int32)


def rotary_tables(count):
    half = HD // 2
    freq = jnp.exp(jnp.arange(half, dtype=f32) * (-2.0 * math.log(10000.0) / HD))
    angles = jnp.arange(count, dtype=jnp.int32).astype(f32)[:, None] * freq
    cosine, sine = jnp.cos(angles), jnp.sin(angles)
    return (
        jnp.concatenate([cosine, cosine], axis=1),
        jnp.concatenate([-sine, sine], axis=1),
    )


def on_device(
    tokens, cotangent, gain_first, gain_second, router_attn, router_mlp, query_w, key_w, value_w,
    output_w, gate_w, up_w, down_w, query_a, query_b, key_a, key_b, value_a, value_b, output_a,
    output_b, gate_a, gate_b, up_a, up_b, down_a, down_b, adapter_ids, attn_routes, mlp_routes,
):
    shards = lax.axis_size("shard")
    groups = lax.axis_size("dp")
    shard_at = lax.axis_index("shard")
    group_at = lax.axis_index("dp")
    rows = tokens.shape[0]
    seq = rows * shards
    cap_mlp = rows // 4 + rows // 16
    slices = groups // EXPERTS
    ff = gate_w.shape[1]
    width = key_w.shape[1]
    block = D // (groups * shards)
    own = groups * block
    adapter = adapter_ids[group_at]
    expert = group_at // slices

    x = tokens.astype(f32)
    normed = (x * inverse_rms(x) * gain_first.astype(f32)).astype(bf16)
    split = (D // LOW * 9 // 16) * LOW
    places = lax.rem(shard_at + shards - jnp.arange(shards, dtype=jnp.int32), shards)

    def shifted(part, step):
        pairs = [(i, (i + step) % shards) for i in range(shards)]
        return lax.ppermute(part, "shard", pairs) if step else part

    def gathered(left, right):
        return [lax.all_gather(left, "shard", axis=0, tiled=True)] + [
            shifted(right, step) for step in range(shards)
        ]

    xn_parts = gathered(normed[:, :split], normed[:, split:])

    mcol = slot_places(mlp_routes, EXPERTS, cap_mlp)
    mrow = mcol.T
    cosf, sinf = rotary_tables(seq)

    def ranks_first(factor):
        return jnp.swapaxes(factor, -1, -2)

    def of_adapter(factor, axis):
        return lax.dynamic_index_in_dim(factor, adapter, axis, keepdims=False)

    def pad_rows(parts, count=LOW):
        have = sum(p.shape[0] for p in parts)
        fill = jnp.zeros((count - have, parts[0].shape[1]), bf16)
        return jnp.concatenate(list(parts) + [fill], axis=0)

    aq = of_adapter(ranks_first(query_a), 1).reshape(LOW, D)
    amisc = pad_rows(
        [of_adapter(ranks_first(key_a), 0), of_adapter(ranks_first(value_a), 0), router_attn.T]
    )
    bcat = of_adapter(query_b, 1).reshape(LOW, width)
    key_second, value_second = of_adapter(key_b, 0), of_adapter(value_b, 0)
    kb = pad_rows([key_second])
    vb = pad_rows([jnp.zeros_like(value_second), value_second])
    oa = of_adapter(ranks_first(output_a), 1).reshape(LOW, width)
    ob = of_adapter(output_b, 1).reshape(LOW, D)
    router = pad_rows([router_mlp.T], 2 * EXPERTS)
    router_first = pad_rows([router_attn.T], 2 * ATT_EXPERTS)
    gain1, gain2 = gain_first.reshape(1, D), gain_second.reshape(1, D)

    def of_expert(factor):
        return lax.dynamic_index_in_dim(factor, expert, 0, keepdims=False).reshape(LOW, D)

    gate_first = of_expert(ranks_first(gate_a))
    up_first = of_expert(ranks_first(up_a))
    down_second = of_expert(down_b)
    gate_table = gate_b.reshape(LOW, ff)
    up_table = up_b.reshape(LOW, ff)
    down_table = ranks_first(down_a).reshape(LOW, ff)
    expert_rows = groups * cap_mlp
    source_adapter = jnp.repeat(adapter_ids, cap_mlp)
    mask = (
        source_adapter[:, None] == (jnp.arange(LOW, dtype=jnp.int32) // RANK)[None, :]
    ).astype(bf16)

    experts = (ATT_EXPERTS,)
    batch = 2
    batches = (ATT_EXPERTS // batch,)
    def to_experts(sent):
        wide = sent.shape[1]
        sent = jnp.repeat(sent.reshape(EXPERTS, cap_mlp, wide), slices, axis=0)
        got = lax.all_to_all(sent, "dp", split_axis=0, concat_axis=0, tiled=True)
        return got.reshape(expert_rows, wide)

    sent_rows = EXPERTS * cap_mlp
    picked = (mrow[0][None, :] == iota((sent_rows, rows), 0)) | (
        mrow[1][None, :] == iota((sent_rows, rows), 0)
    )
    grads_in = to_experts(nn(picked.astype(bf16), cotangent).astype(bf16))
    own_rows = lambda array: lax.dynamic_slice_in_dim(array, shard_at * rows, rows, 0)
    routes_own = own_rows(attn_routes)
    early_made = (router, router_first, gain1, gain2, mask, mrow, mcol, routes_own)
    early_made += (gate_first, up_first, down_second)
    early_made, xn_parts, grads_in = lax.optimization_barrier((early_made, xn_parts, grads_in))
    router, router_first, gain1, gain2, mask, mrow, mcol, routes_own, *firsts = early_made
    gate_first, up_first, down_second = firsts

    column_parts = 8
    width_d = D // column_parts
    steps_attn = ATT_EXPERTS + column_parts
    early = lambda e: (jnp.minimum(e, ATT_EXPERTS - 1), 0, 0)
    late = lambda e: jnp.maximum(e - ATT_EXPERTS, 0)
    column_block = pl.BlockSpec((LOW, width_d), lambda e: (0, late(e)))
    out_block = pl.BlockSpec((seq, width_d), lambda e: (0, late(e)))
    key_block = pl.BlockSpec((width_d, width), lambda e: (late(e), 0))
    far = pl.BlockSpec(memory_space=pl.ANY)
    project_flops = 4 * ATT_EXPERTS * seq * D * width
    weight_bytes = 4 * ATT_EXPERTS * D * width
    pair, row = ((2 * seq, width), bf16), ((seq, width), bf16)
    narrow, stat = ((seq, LOW), bf16), ((2 * seq, LOW), f32)
    saved = [pair, row, row, ((seq, LOW), f32), narrow, narrow, pair, stat]

    attn_part, low_part, q, k, v, ga, low, misc, o, lse = call(
        lambda *refs: attention_kernel(shards, *refs),
        (steps_attn,),
        [pl.BlockSpec(memory_space=pltpu.SMEM)]
        + [whole()] * (1 + shards)
        + [
            pl.BlockSpec((1, D, width), early),
            pl.BlockSpec((ATT_EXPERTS, width, width_d), lambda e: (0, 0, late(e))),
            column_block,
            far,
            far,
        ]
        + [whole()] * 9,
        [out_block, whole()] + [far] * 8,
        [sds((seq, D), bf16), sds(*narrow)] + [sds(*shape) for shape in saved],
        [pltpu.VMEM(*shape) for shape in saved]
        + [
            pltpu.VMEM((2 * seq, width), f32),
            pltpu.VMEM(*pair),
            pltpu.VMEM((seq, ATT_EXPERTS * width), bf16),
            pltpu.VMEM((D, width), bf16),
            pltpu.VMEM((D, width), bf16),
            pltpu.SemaphoreType.DMA((2,)),
            pltpu.SemaphoreType.DMA((8,)),
            pltpu.VMEM((seq, D), bf16),
        ],
        project_flops,
        weight_bytes,
    )(places, *xn_parts, query_w, output_w, ob, key_w, value_w, aq, amisc, bcat, kb, vb, attn_routes, cosf, sinf, oa)

    attn = lax.psum_scatter(attn_part, "shard", scatter_dimension=0, tiled=True)

    rows_sent, gm, m = call(
        lambda *refs: dispatch_kernel(cap_mlp, *refs),
        (),
        [whole()] * 6,
        [whole()] * 3,
        [
            sds((sent_rows, D + LOW), bf16),
            sds((rows, LOW), f32),
            sds((rows, D), bf16),
        ],
        [],
        6 * sent_rows * rows * D,
        8 * sent_rows * D,
    )(attn, tokens, gain2, router, mrow, mcol)

    def from_experts(made):
        got = lax.all_to_all(
            made.reshape(groups, cap_mlp, D + LOW), "dp", split_axis=0, concat_axis=0, tiled=True
        )
        if slices > 1:
            parts = got.reshape(EXPERTS, slices, cap_mlp, D + LOW).astype(f32)
            got = jnp.sum(parts, axis=1).astype(bf16)
        return got.reshape(sent_rows, D + LOW)

    def by_column_owner(part):
        split = part.reshape(rows, groups, shards, block)
        return split.transpose(2, 0, 1, 3).reshape(shards, rows, own)

    columns_sent = jnp.concatenate([by_column_owner(m), by_column_owner(cotangent)], axis=2)
    low_lanes = low_part.reshape(shards, rows, LOW).transpose(1, 0, 2).reshape(rows, shards * LOW)
    arrived = []
    for step in range(shards):
        piece = lax.dynamic_index_in_dim(
            columns_sent, lax.rem(shard_at + step, shards), 0, keepdims=False
        )
        piece = jnp.concatenate([piece, low_lanes], axis=1)
        arrived.append(shifted(piece, step))

    rows_in = to_experts(rows_sent)

    steps = 11
    fb = ff // steps
    columns = pl.BlockSpec((D, fb), lambda f: (0, f))
    weight_rows = pl.BlockSpec((fb, D), lambda f: (f, 0))
    table = pl.BlockSpec((LOW, fb), lambda f: (0, f))
    kept = pl.BlockSpec((expert_rows, fb), lambda f: (0, f))
    weight_flops = 2 * expert_rows * D * ff
    weight_moved = 2 * D * ff
    low_shape = sds((expert_rows, LOW), bf16)
    wide_shape = sds((expert_rows, ff), bf16)
    out_shape = sds((expert_rows, D + LOW), bf16)

    g, u, lg, lu = call(
        expert_up_kernel,
        (steps,),
        [whole()] * 4 + [columns, columns, table, table],
        [kept, kept, whole(), whole()],
        [wide_shape, wide_shape, low_shape, low_shape],
        [],
        2 * weight_flops,
        2 * weight_moved,
    )(rows_in, mask, gate_first, up_first, gate_w, up_w, gate_table, up_table)

    g, *arrived = lax.optimization_barrier((g, *arrived))
    arrived = jnp.concatenate(arrived, axis=0)
    mlp_columns = arrived[:, : 2 * own]
    out_lows = jnp.sum(
        arrived[:, 2 * own :].reshape(shards, rows, shards, LOW).astype(f32), axis=0
    )
    out_lows = out_lows.astype(bf16).transpose(1, 0, 2).reshape(seq, LOW)

    each = ff // shards
    head = ((each // LOW + 1) // 2) * LOW
    spans = [head, each - head] if each % LOW == 0 else [each]
    low_sum = pltpu.VMEM((expert_rows, LOW), f32)
    low_turned = pltpu.VMEM((LOW, expert_rows), bf16)
    ze, dg, du, dlg, dlu, *tables = call(
        expert_down_kernel,
        (steps,),
        [whole()] * 6 + [kept, kept, weight_rows, table, table, table],
        [whole(), kept, kept, whole(), whole()] + [whole() for _ in spans],
        [out_shape, wide_shape, wide_shape, low_shape, low_shape]
        + [sds((shards, 3 * LOW, span), bf16) for span in spans],
        [pltpu.VMEM((expert_rows, D), bf16)]
        + [pltpu.VMEM((expert_rows, D), f32), low_sum, low_sum, low_sum]
        + [pltpu.VMEM((expert_rows, LOW), bf16)]
        + [low_turned] * 3
        + [pltpu.VMEM((3 * LOW, ff), bf16)],
        2 * weight_flops,
        weight_moved,
    )(grads_in, rows_in, mask, down_second, lg, lu, g, u, down_w, gate_table, up_table, down_table)

    ze_back = from_experts(ze)

    def table_sum(part):
        part = part.reshape(-1, part.shape[-1])
        return lax.psum_scatter(part, "shard", scatter_dimension=0, tiled=True)

    head_tables = table_sum(tables[0])

    parts = 8
    db = D // parts
    row_block = pl.BlockSpec((db, ff), lambda n: (n, 0))
    low_block = pl.BlockSpec((LOW, db), lambda n: (0, n))
    dm = call(
        expert_rows_kernel,
        (parts,),
        [whole()] * 4 + [row_block, row_block, low_block, low_block],
        whole(),
        out_shape,
        [],
        2 * weight_flops,
        2 * weight_moved,
    )(dg, du, dlg, dlu, gate_w, up_w, gate_first, up_first)

    dm_back = from_experts(dm)

    layer_out, dlm, low_down = call(
        lambda *refs: combine_kernel(cap_mlp, *refs),
        (),
        [whole()] * 6,
        [whole()] * 3,
        [sds((rows, D), bf16), sds((rows, LOW), bf16), sds((rows, LOW), f32)],
        [],
        4 * sent_rows * rows * D,
        4 * sent_rows * D,
    )(ze_back, attn, tokens, cotangent, gm, mcol)

    dm_back = after(dm_back, head_tables)
    dh1, da_left, da_right = call(
        hidden_grad_kernel,
        (),
        [whole()] * 10,
        [whole()] * 3,
        [
            sds((rows, D), f32),
            sds((rows, split), bf16),
            sds((rows, D - split + LOW), bf16),
        ],
        [],
        2 * sent_rows * rows * D,
        4 * sent_rows * D,
    )(dm_back, dlm, low_down, attn, tokens, cotangent, gain2, router, mcol, mlp_routes)

    da_parts = gathered(da_left, da_right)
    owner_places = jnp.concatenate([places, jnp.full((1,), block, jnp.int32)])
    xn_own = call(
        lambda *refs: own_columns_kernel(shards, *refs),
        (),
        [pl.BlockSpec(memory_space=pltpu.SMEM)] + [whole()] * (shards + 1),
        whole(),
        sds((seq, own), bf16),
        [pltpu.VMEM((seq, D), bf16), pltpu.VMEM((D, own), bf16)],
        0,
        0,
    )(owner_places, *after(xn_parts, da_left))
    *da_parts, xn_own = lax.optimization_barrier((*da_parts, xn_own))
    tables_sum = [head_tables] + [table_sum(after(part, *da_parts)) for part in tables[1:]]

    loaded = [((seq, LOW), f32), pair, pair, row, row, stat, narrow, narrow]
    loaded += [((seq, HD), f32), ((seq, HD), f32)]
    dx_part, lows, grad_oa, grad_qb, grad_kv = call(
        lambda *refs: attention_back_kernel(shards, *refs),
        (steps_attn,),
        [pl.BlockSpec(memory_space=pltpu.SMEM)]
        + [whole()] * (1 + shards)
        + [
            pl.BlockSpec((1, width, D), early),
            pl.BlockSpec((ATT_EXPERTS, width_d, width), lambda e: (0, late(e), 0)),
            key_block,
            key_block,
            column_block,
            column_block,
        ]
        + [whole()] * 6
        + [far] * 10,
        [out_block] + [whole()] * 4,
        [
            sds((seq, D), bf16),
            sds((seq // 2 + 16, LOW), bf16),
            sds((LOW, width), bf16),
            sds((LOW, width), bf16),
            sds((2 * LOW, width), bf16),
        ],
        [pltpu.VMEM(*shape) for shape in loaded]
        + [
            pltpu.SemaphoreType.DMA((10,)),
            pltpu.VMEM((seq, LOW), f32),
            pltpu.VMEM((2 * seq, width), f32),
            pltpu.VMEM(*pair),
            pltpu.VMEM(*stat),
            pltpu.VMEM(*pair),
            pltpu.VMEM(*row),
            pltpu.VMEM(*row),
            pltpu.VMEM((seq, 2 * LOW), bf16),
            pltpu.VMEM((seq, HD), f32),
            pltpu.VMEM((seq, HD), f32),
            pltpu.VMEM((seq, ATT_EXPERTS * width), bf16),
            pltpu.VMEM((seq, D), bf16),
        ],
        project_flops,
        weight_bytes,
    )(places, *da_parts, output_w, query_w, key_w, value_w, aq, amisc, bcat, kb, vb, oa, ob, attn_routes, ga, o, q, k, v, lse, low, misc, cosf, sinf)

    held = (dx_part, lows, grad_oa, grad_qb, grad_kv, *da_parts, *tables_sum)
    dx_part, lows, grad_oa, grad_qb, grad_kv, *held = lax.optimization_barrier(held)
    da_parts, tables_sum = held[: shards + 1], held[shards + 1 :]
    lows_parts = [lows] + [shifted(lows, step) for step in range(1, shards)]
    chain = (*lows_parts, *da_parts)
    chain = lax.optimization_barrier(chain)
    lows_parts, da_parts = chain[:shards], chain[shards:]
    factors, grad_ob_own = call(
        lambda *refs: owner_kernel(shards, *refs),
        (),
        [pl.BlockSpec(memory_space=pltpu.SMEM)] + [whole()] * (shards + 3),
        [whole()] * 2,
        [sds((3 * LOW, own), bf16), sds((LOW, own), bf16)],
        [
            pltpu.VMEM((seq, own), bf16),
            pltpu.VMEM((seq, D), bf16),
            pltpu.VMEM((D, own), bf16),
        ],
        0,
        0,
    )(owner_places, *da_parts, out_lows, mlp_columns)
    lows_sum = sum(part.astype(f32) for part in lows_parts)
    half = LOW // 2
    lows_all = jnp.concatenate([lows_sum[: seq // 2, :half], lows_sum[: seq // 2, half:]], axis=0)
    lows_all = lows_all.astype(bf16)
    slopes = lows_sum[seq // 2 : seq // 2 + 2 * (seq // CHUNK)].reshape(2, seq).T
    dx = lax.psum_scatter(dx_part, "shard", scatter_dimension=0, tiled=True)

    input_grad = call(
        input_grad_kernel,
        (),
        [whole()] * 8,
        whole(),
        sds((rows, D), f32),
        [],
        2 * rows * LOW * D,
        24 * rows * D,
    )(dx, own_rows(slopes), own_rows(ga), tokens, gain1, router_first, dh1, routes_own)

    lane = jnp.arange(LOW, dtype=jnp.int32)
    dense = jnp.zeros((seq, LOW), f32)
    for j in range(2):
        spread = (iota((half, LOW), 0) == (lane % RANK + j * RANK)[None, :]).astype(bf16)
        chosen = attn_routes[:, j : j + 1] == (lane // RANK)[None, :]
        dense = dense + jnp.where(chosen, nn(lows_all, spread), 0.0)
    grad_qa_own = tn(dense.astype(bf16), xn_own)
    grad_kva_own = tn(lows_all[:, 2 * RANK : 4 * RANK], xn_own)

    def to_owner_columns(part):
        return part.reshape(-1, groups, block).transpose(1, 0, 2).reshape(groups, -1)

    def to_owner_ranks(part):
        parts = part.reshape(-1, groups, RANK // groups, width)
        return parts.transpose(1, 0, 2, 3).reshape(groups, -1)

    sending = [
        to_owner_columns(grad_qa_own.astype(bf16)),
        to_owner_columns(grad_ob_own),
        to_owner_columns(grad_kva_own.astype(bf16)),
        to_owner_ranks(grad_qb),
        to_owner_ranks(grad_oa),
        to_owner_ranks(jnp.concatenate([grad_kv[:RANK], grad_kv[LOW + RANK : LOW + 2 * RANK]])),
        to_owner_columns(factors),
    ]
    sizes = [piece.shape[1] for piece in sending]
    sent = jnp.concatenate(sending, axis=1).reshape(groups, -1, LOW)
    got = lax.all_to_all(sent, "dp", split_axis=0, concat_axis=0, tiled=True)
    got = got.reshape(groups, -1).astype(f32)
    pick_source = (adapter_ids[:, None] == jnp.arange(ADAPTERS, dtype=jnp.int32)[None, :]).astype(
        f32
    )
    placed_sums = jnp.einsum("sa,sn->an", pick_source, got, precision=precise)
    parts = []
    start = 0
    for size in sizes:
        parts.append(placed_sums[:, start : start + size])
        start += size
    ranks_own = RANK // groups

    def columns_out(part, count):
        return part.reshape(ADAPTERS, count, RANK, block)

    def ranks_out(part, count):
        return part.reshape(ADAPTERS, count, ranks_own, width)

    query_a_sum = columns_out(parts[0], ATT_EXPERTS).transpose(1, 0, 3, 2)
    output_b_sum = columns_out(parts[1], ATT_EXPERTS).transpose(1, 0, 2, 3)
    kv_a_sum = columns_out(parts[2], 2).transpose(1, 0, 3, 2)
    query_b_sum = ranks_out(parts[3], ATT_EXPERTS).transpose(1, 0, 2, 3)
    output_a_sum = ranks_out(parts[4], ATT_EXPERTS).transpose(1, 0, 3, 2)
    kv_b_sum = ranks_out(parts[5], 2).transpose(1, 0, 2, 3)
    factor_sum = columns_out(parts[6], 3 * EXPERTS).transpose(1, 0, 2, 3)
    gate_a_sum = factor_sum[:EXPERTS].transpose(0, 1, 3, 2)
    up_a_sum = factor_sum[EXPERTS : 2 * EXPERTS].transpose(0, 1, 3, 2)
    down_b_sum = factor_sum[2 * EXPERTS :]

    joined = jnp.concatenate(tables_sum, axis=1) if len(tables_sum) > 1 else tables_sum[0]
    joined = joined.astype(f32).reshape(3, ADAPTERS, RANK, each)

    return (
        layer_out,
        input_grad,
        query_a_sum,
        query_b_sum,
        kv_a_sum[0],
        kv_b_sum[0],
        kv_a_sum[1],
        kv_b_sum[1],
        output_a_sum,
        output_b_sum,
        gate_a_sum,
        joined[0],
        up_a_sum,
        joined[1],
        ranks_first(joined[2]),
        down_b_sum,
    )


def solution(mesh):
    placed = (
        P(("dp", "shard"), None),
        P(("dp", "shard"), None),
        P(),
        P(),
        P(),
        P(),
        P(None, None, "shard"),
        P(None, "shard"),
        P(None, "shard"),
        P(None, "shard", None),
        P(None, "dp"),
        P(None, "dp"),
        P("dp", None),
        P(),
        P(None, None, None, "shard"),
        P(),
        P(None, None, "shard"),
        P(),
        P(None, None, "shard"),
        P(None, None, "shard", None),
        P(),
        P(),
        P(None, None, "dp"),
        P(),
        P(None, None, "dp"),
        P(None, "dp", None),
        P(),
        P(),
        P("dp", None),
        P(("dp", "shard"), None),
    )
    return jax.shard_map(
        on_device,
        mesh=mesh,
        in_specs=placed,
        out_specs=(
            P(("dp", "shard"), None),
            P(("dp", "shard"), None),
            P(None, None, ("dp", "shard"), None),
            P(None, None, "dp", "shard"),
            P(None, ("dp", "shard"), None),
            P(None, "dp", "shard"),
            P(None, ("dp", "shard"), None),
            P(None, "dp", "shard"),
            P(None, None, "shard", "dp"),
            P(None, None, None, ("dp", "shard")),
            P(None, None, ("dp", "shard"), None),
            P(None, None, ("dp", "shard")),
            P(None, None, ("dp", "shard"), None),
            P(None, None, ("dp", "shard")),
            P(None, ("dp", "shard"), None),
            P(None, None, None, ("dp", "shard")),
        ),
        check_vma=False,
    )
```

```python
import math

import jax
import jax.numpy as jnp
from jax import lax
from jax.experimental import pallas as pl
from jax.experimental.pallas import tpu as pltpu
from jax.sharding import PartitionSpec as P

D = 2048
HD = 128
EXPERTS = 8
ATT_EXPERTS = 8
ADAPTERS = 8
RANK = 16
LOW = 128
CHUNK = 128
GATE_LANE = 64
ROUTE_LANE = 96
ROUTER_ROW = 32
DEPTH = 3


f32 = jnp.float32
bf16 = jnp.bfloat16
precise = lax.Precision.HIGHEST
eps = 1e-05
score_scale = HD ** (-0.5)


def nn(a, b):
    return lax.dot_general(a, b, (((1,), (0,)), ((), ())), preferred_element_type=f32)


def nt(a, b):
    return lax.dot_general(a, b, (((1,), (1,)), ((), ())), preferred_element_type=f32)


def tn(a, b):
    return lax.dot_general(a, b, (((0,), (0,)), ((), ())), preferred_element_type=f32)


def iota(shape, axis):
    return lax.broadcasted_iota(jnp.int32, shape, axis)


def ones_where(condition):
    return jnp.where(condition, 1.0, 0.0).astype(bf16)


def inverse_rms(values):
    return lax.rsqrt(jnp.mean(values * values, axis=-1, keepdims=True) + eps)


def norm_backward(values, inverse, gain_vector, grad_normed):
    weighted = gain_vector * grad_normed
    return inverse * weighted - values * (inverse * inverse * inverse) * jnp.mean(
        values * weighted, axis=-1, keepdims=True
    )


def softmax_pair(first, second):
    peak = jnp.maximum(first, second)
    one, two = jnp.exp(first - peak), jnp.exp(second - peak)
    total = one + two
    return one / total, two / total


def in_lane(column, lane, width=LOW):
    shape = (column.shape[0], width)
    return jnp.where(iota(shape, 1) == lane, column, 0.0)


def lane_of(values, lane):
    return jnp.sum(jnp.where(iota(values.shape, 1) == lane, values, 0.0), axis=1, keepdims=True)


def expert_lanes(dest, capacity, shape, group):
    lane = iota(shape, 1)
    low = (lane // group) * capacity
    return (dest >= low) & (dest < low + capacity)


def whole():
    return pl.BlockSpec(memory_space=pltpu.VMEM)


def sds(shape, dtype):
    return jax.ShapeDtypeStruct(shape, dtype)


def call(kernel, grid, in_specs, out_specs, out_shape, scratch, flops, moved):
    return pl.pallas_call(
        kernel,
        grid=grid,
        in_specs=in_specs,
        out_specs=out_specs,
        out_shape=out_shape,
        scratch_shapes=scratch,
        compiler_params=pltpu.CompilerParams(
            vmem_limit_bytes=60 * 1024 * 1024,
            dimension_semantics=("arbitrary",) * len(grid) if grid else None,
        ),
        cost_estimate=pl.CostEstimate(
            flops=4 * flops, bytes_accessed=4 * moved, transcendentals=0
        ),
    )


def rope(values, cosine, sine):
    return values * cosine + pltpu.roll(values, HD // 2, 1) * sine


def unrope(values, cosine, sine):
    return values * cosine - pltpu.roll(values, HD // 2, 1) * sine


def routed(route, shape):
    return (iota(shape, 1) // RANK) == route


def select_add(total, part, routes, expert):
    s = part.shape[0]
    for k in range(2):
        total[k * s : (k + 1) * s, :] += jnp.where(routes[:, k : k + 1] == expert, part, 0.0)


def weight_stream(n, count, fetch):
    def prime():
        for j in range(min(DEPTH - 1, count)):
            for copy in fetch(j, j):
                copy.start()

    def advance():
        later = n + DEPTH - 1

        @pl.when(later < count)
        def _():
            for copy in fetch(later, lax.rem(later, DEPTH)):
                copy.start()

        for copy in fetch(n, lax.rem(n, DEPTH)):
            copy.wait()

    return prime, advance


def block_at(n, width):
    return pl.ds(pl.multiple_of(n * width, LOW), width)


def copies(sources, targets, sems):
    return [
        pltpu.make_async_copy(source, target, sems.at[j])
        for j, (source, target) in enumerate(zip(sources, targets, strict=True))
    ]


def join_rows(places, left, parts, out):
    split, rows = left.shape[1], parts[0].shape[0]
    out[:, 0:split] = left[...]
    for j, part in enumerate(parts):
        at = pl.ds(pl.multiple_of(places[j] * rows, 16), rows)
        out[at, split:] = part[:, 0 : out.shape[1] - split]


def attention_kernel(shards, places, left, *refs):
    parts, refs = refs[:shards], refs[shards:]
    *refs, xn = refs

    @pl.when(pl.program_id(0) == 0)
    def _():
        join_rows(places, left, parts, xn)

    attention_steps(xn, *refs)


def attention_steps(
    xn, wq_far, wo_far, ob, wk_far, wv_far, aq, amisc, bcat, kb, vb, routes, cosf, sinf, oa,
    attn_out, out_low, q_far, k_far, v_far, ga_far, low_far, misc_far, o_far, lse_far,
    q, k, v, ga, low, misc, o, lse, qsum, og, chosen, wk, wv, load_sems, save_sems, wq, wo, wq_sems, wo_sems,
):
    step = pl.program_id(0)
    s, width = k.shape
    loads = copies((wk_far, wv_far), (wk, wv), load_sems)
    width_d = wo.shape[3]
    prime_q, next_q = weight_stream(
        step,
        ATT_EXPERTS,
        lambda n, slot: [
            pltpu.make_async_copy(wq_far.at[n], wq.at[slot], wq_sems.at[slot]),
        ],
    )
    prime_o, next_o = weight_stream(
        step - ATT_EXPERTS,
        D // width_d,
        lambda n, slot: [
            pltpu.make_async_copy(
                wo_far.at[:, :, block_at(n, width_d)], wo.at[slot], wo_sems.at[slot]
            ),
        ],
    )
    saves = copies(
        (q, k, v, ga, low, misc, o, lse),
        (q_far, k_far, v_far, ga_far, low_far, misc_far, o_far, lse_far),
        save_sems,
    )

    @pl.when(step == 0)
    def _():
        prime_q()
        for load in loads:
            load.start()
        x = xn[...]
        low[...] = nt(x, aq[...]).astype(bf16)
        scores = nt(x, amisc[...])
        misc[...] = scores.astype(bf16)
        lane = iota((s, LOW), 1) - ROUTER_ROW
        gates = [
            jnp.sum(jnp.where(lane == routes[:, j : j + 1], scores, 0.0), axis=1, keepdims=True)
            for j in range(2)
        ]
        one, two = softmax_pair(*gates)
        ga[...] = in_lane(one, 0) + in_lane(two, 1)
        for j in range(2):
            mine = routed(routes[:, j : j + 1], (s, LOW))
            part = jnp.where(mine, low[...], jnp.zeros((), bf16))
            qsum[j * s : (j + 1) * s, :] = nn(part, bcat[...])

    @pl.when(step < ATT_EXPERTS)
    def _():
        next_q()
        select_add(qsum, nn(xn[...], wq[lax.rem(step, DEPTH)]), routes, step)

    @pl.when(step == ATT_EXPERTS - 1)
    def _():
        prime_o()
        for load in loads:
            load.wait()
        x = xn[...]
        keys = nn(x, wk[...]) + nn(misc[...], kb[...])
        for h in range(width // HD):
            hs = slice(h * HD, (h + 1) * HD)
            k[:, hs] = rope(keys[:, hs], cosf[...], sinf[...]).astype(bf16)
            for j in range(2):
                at = slice(j * s, (j + 1) * s)
                q[at, hs] = rope(qsum[at, hs], cosf[...], sinf[...]).astype(bf16)
        v[...] = (nn(x, wv[...]) + nn(misc[...], vb[...])).astype(bf16)
        attend(q, k, v, ga, o, og, lse)
        for save in saves:
            save.start()
        total = jnp.zeros((s, LOW), f32)
        for j in range(2):
            part = nt(og[j * s : (j + 1) * s, :], oa[...])
            total = total + jnp.where(routed(routes[:, j : j + 1], (s, LOW)), part, 0.0)
        out_low[...] = total.astype(bf16)
        spread_rows(og, routes, chosen)

    @pl.when(step >= ATT_EXPERTS)
    def _():
        next_o()
        weights = wo[lax.rem(step - ATT_EXPERTS, DEPTH)].reshape(chosen.shape[1], width_d)
        attn_out[...] = (nn(chosen[...], weights) + nn(out_low[...], ob[...])).astype(bf16)

    @pl.when(step == pl.num_programs(0) - 1)
    def _():
        for save in saves:
            save.wait()


def spread_rows(pair, routes, chosen):
    s, width = chosen.shape[0], pair.shape[1]
    for e in range(ATT_EXPERTS):
        chosen[:, e * width : (e + 1) * width] = of_expert_rows(pair, routes, e, s)


def causal(i, shape):
    row = (iota(shape, 0) & (CHUNK - 1)) + i * CHUNK
    return iota(shape, 1) <= row


def attend(q, k, v, ga, o_out, og_out, lse_out):
    s, width = k.shape
    for i in range(s // CHUNK):
        end = (i + 1) * CHUNK
        first, second = slice(i * CHUNK, end), slice(s + i * CHUNK, s + end)
        gates = [ga[first, 0:1], ga[first, 1:2]]
        log_totals = jnp.zeros((2 * CHUNK, LOW), f32)
        for h in range(width // HD):
            hs = slice(h * HD, (h + 1) * HD)
            queries = jnp.concatenate([q[first, hs], q[second, hs]], axis=0)
            scores = nt(queries, k[0:end, hs]) * score_scale
            scores = jnp.where(causal(i, scores.shape), scores, -1e30)
            peak = jnp.max(scores, axis=1, keepdims=True)
            weights = jnp.exp(scores - peak)
            total = jnp.sum(weights, axis=1, keepdims=True)
            mixed = nn(weights.astype(bf16), v[0:end, hs]) / total
            o_out[first, hs] = mixed[:CHUNK].astype(bf16)
            o_out[second, hs] = mixed[CHUNK:].astype(bf16)
            og_out[first, hs] = (mixed[:CHUNK] * gates[0]).astype(bf16)
            og_out[second, hs] = (mixed[CHUNK:] * gates[1]).astype(bf16)
            log_totals = log_totals + in_lane(peak + jnp.log(total), h)
        lse_out[first, :] = log_totals[:CHUNK]
        lse_out[second, :] = log_totals[CHUNK:]


def of_expert_rows(rows, routes, expert, s):
    return rows[0:s, :] * ones_where(routes[:, 0:1] == expert) + rows[s : 2 * s, :] * ones_where(
        routes[:, 1:2] == expert
    )


def second_norm(attn, tokens, gain):
    hidden = tokens[...].astype(f32) + attn[...].astype(f32)
    inverse = inverse_rms(hidden)
    return hidden, inverse, gain[...].astype(f32)


def dispatch_kernel(cap, attn, tokens, gain, router, mrow, mcol, rows_out, gm_out, m_out):
    hidden, inverse, scale = second_norm(attn, tokens, gain)
    m = (hidden * inverse * scale).astype(bf16)
    m_out[...] = m
    logits = nt(m, router[...])
    gates = softmax_pair(
        *[
            jnp.sum(
                jnp.where(
                    expert_lanes(mcol[:, k : k + 1], cap, logits.shape, 1),
                    logits,
                    0.0,
                ),
                axis=1,
                keepdims=True,
            )
            for k in range(2)
        ]
    )
    gm_out[...] = in_lane(gates[0], 0) + in_lane(gates[1], 1)
    slot = iota((rows_out.shape[0], mrow.shape[1]), 0)
    picks = [ones_where(mrow[k : k + 1, :] == slot) for k in range(2)]
    rows_out[:, 0:D] = nn(picks[0] + picks[1], m).astype(bf16)
    total = jnp.zeros((rows_out.shape[0], LOW), f32)
    for k in range(2):
        high = gates[k].astype(bf16).astype(f32)
        middle = (gates[k] - high).astype(bf16).astype(f32)
        both = in_lane(high, 0) + in_lane(middle, 1)
        total = total + nn(picks[k], both.astype(bf16))
    rows_out[:, D : D + LOW] = total.astype(bf16)


def fold(first_lane):
    row, column = iota((LOW, LOW), 0), iota((LOW, LOW), 1)
    return ones_where(column == (row & (RANK - 1)) + first_lane)


def spread(first_lane):
    row, column = iota((LOW, LOW), 0), iota((LOW, LOW), 1)
    return ones_where(row == (column & (RANK - 1)) + first_lane)


def combine_kernel(cap, ze, attn, tokens, cot, gm, mcol, layer_out, dlm_out, low_out):
    hidden = tokens[...].astype(f32) + attn[...].astype(f32)
    grad = cot[...].astype(f32)
    lane = iota((mcol.shape[0], ze.shape[0]), 1)
    gates, slopes, lows = [], [], []
    for k in range(2):
        gates.append(gm[:, k : k + 1])
        pick = ones_where(mcol[:, k : k + 1] == lane)
        expert_out = nn(pick, ze[:, 0:D])
        lows.append(gates[k] * nn(pick, ze[:, D : D + LOW]))
        slopes.append(jnp.sum(grad * expert_out, axis=1, keepdims=True))
        hidden = hidden + gates[k] * expert_out
    layer_out[...] = hidden.astype(bf16)
    low_out[...] = lows[0] + pltpu.roll(lows[1], 3 * RANK, 1)
    mean = gates[0] * slopes[0] + gates[1] * slopes[1]
    total = jnp.zeros(dlm_out.shape, f32)
    for k in range(2):
        mine = expert_lanes(mcol[:, k : k + 1], cap, dlm_out.shape, 1)
        total = total + jnp.where(mine, gates[k] * (slopes[k] - mean), 0.0)
    dlm_out[...] = total.astype(bf16)


def hidden_grad_kernel(
    rows, dlm, low, attn, tokens, cot, gain, router, mcol, routes, dh1_out, da_left, da_right
):
    hidden, inverse, scale = second_norm(attn, tokens, gain)
    lane = iota((mcol.shape[0], rows.shape[0]), 1)
    picks = [ones_where(mcol[:, k : k + 1] == lane) for k in range(2)]
    grad_m = nn(picks[0] + picks[1], rows[:, 0:D]) + nn(dlm[:, 0 : router.shape[0]], router[...])
    lows = [nn(pick, rows[:, D : D + LOW]) for pick in picks]
    total = low[...] + lows[0] + pltpu.roll(lows[1], 3 * RANK, 1)
    for k in range(2):
        total = total + in_lane(routes[:, k : k + 1].astype(f32), ROUTE_LANE + k)
    grad = cot[...].astype(f32) + norm_backward(hidden, inverse, scale, grad_m)
    dh1_out[...] = grad
    split = da_left.shape[1]
    da_left[...] = grad[:, :split].astype(bf16)
    da_right[:, 0 : D - split] = grad[:, split:].astype(bf16)
    da_right[:, D - split :] = total.astype(bf16)


def select_columns(places, shards, select):
    row, column = iota(select.shape, 0), iota(select.shape, 1)
    size = places[shards]
    group = lax.div(column, size)
    source = group * (size * shards) + places[0] * size + (column - group * size)
    select[...] = ones_where(row == source)


def own_columns_kernel(shards, places, *refs):
    parts, (out, gathered, select) = refs[: shards + 1], refs[shards + 1 :]
    select_columns(places, shards, select)
    join_rows(places, parts[0], parts[1:], gathered)
    out[...] = nn(gathered[...], select[...]).astype(bf16)


def owner_kernel(shards, places, *refs):
    da_refs, refs = refs[: shards + 1], refs[shards + 1 :]
    out_lows, columns, factors, grad_ob, da_own, gathered, select = refs
    own = da_own.shape[1]
    select_columns(places, shards, select)
    join_rows(places, da_refs[0], da_refs[1:], gathered)
    da_own[...] = nn(gathered[...], select[...]).astype(bf16)
    grad_ob[...] = tn(out_lows[...], da_own[...]).astype(bf16)
    right = D - da_refs[0].shape[1]
    lows = jnp.concatenate([ref[:, right : right + LOW] for ref in da_refs[1:]], axis=0)
    lane = (iota(lows.shape, 1) // RANK).astype(f32)
    mine = [lane_of(lows.astype(f32), ROUTE_LANE + k) == lane for k in range(2)]
    for part in range(3):
        dense = jnp.zeros(lows.shape, f32)
        for k in range(2):
            wide = nn(lows, spread((3 * k + part) * RANK))
            dense = dense + jnp.where(mine[k], wide, 0.0)
        at = slice(own, 2 * own) if part == 2 else slice(0, own)
        factors[part * LOW : (part + 1) * LOW, :] = tn(dense.astype(bf16), columns[:, at]).astype(
            bf16
        )


def identity():
    return ones_where(iota((LOW, LOW), 0) == iota((LOW, LOW), 1))


def expert_up_kernel(
    x, mask, ga, ua, gate_far, up_far, gate_b, up_b, g_out, u_out, lg_out, lu_out,
    gate_w, up_w, sems,
):
    x = x.at[:, 0:D]
    f = pl.program_id(0)
    width = gate_w.shape[2]
    prime, advance = weight_stream(
        f,
        gate_far.shape[1] // width,
        lambda n, slot: [
            pltpu.make_async_copy(
                gate_far.at[:, block_at(n, width)], gate_w.at[slot], sems.at[0, slot]
            ),
            pltpu.make_async_copy(
                up_far.at[:, block_at(n, width)], up_w.at[slot], sems.at[1, slot]
            ),
        ],
    )

    @pl.when(f == 0)
    def _():
        prime()
        lg_out[...] = nt(x[...], ga[...]).astype(bf16) * mask[...]
        lu_out[...] = nt(x[...], ua[...]).astype(bf16) * mask[...]

    advance()
    slot = lax.rem(f, DEPTH)
    g_out[...] = (nn(x[...], gate_w[slot]) + nn(lg_out[...], gate_b[...])).astype(bf16)
    u_out[...] = (nn(x[...], up_w[slot]) + nn(lu_out[...], up_b[...])).astype(bf16)


def expert_down_kernel(
    grads, x, mask, db, lg, lu, g, u, down_far, gate_b, up_b, down_a,
    ze_out, dg_out, du_out, dlg_out, dlu_out, *rest,
):
    *tables_out, dy, total, pd, dlg, dlu, dpd, lg_t, lu_t, dpd_t, tables, down, sems = rest
    f = pl.program_id(0)
    width = down.shape[1]
    prime, advance = weight_stream(
        f,
        down_far.shape[0] // width,
        lambda n, slot: [
            pltpu.make_async_copy(
                down_far.at[block_at(n, width), :], down.at[slot], sems.at[slot]
            ),
        ],
    )

    @pl.when(f == 0)
    def _():
        prime()
        gate = x[:, D : D + LOW].astype(f32)
        gate = lane_of(gate, 0) + lane_of(gate, 1)
        dy[...] = (gate * grads[...].astype(f32)).astype(bf16)
        dpd[...] = nt(dy[...], db[...]).astype(bf16) * mask[...]
        lg_t[...] = nt(identity(), lg[...]).astype(bf16)
        lu_t[...] = nt(identity(), lu[...]).astype(bf16)
        dpd_t[...] = nt(identity(), dpd[...]).astype(bf16)
        for sums in (total, pd, dlg, dlu):
            sums[...] = jnp.zeros_like(sums)

    advance()
    down_w = down.at[lax.rem(f, DEPTH)]
    dh = nt(dy[...], down_w[...]) + nn(dpd[...], down_a[...])
    gate = g[...].astype(f32)
    up = u[...].astype(f32)
    sig = jax.nn.sigmoid(gate)
    act = gate * sig
    hidden = (act * up).astype(bf16)
    dgate = (dh * up * (sig + act * (1.0 - sig))).astype(bf16)
    dup = (dh * act).astype(bf16)
    dg_out[...] = dgate
    du_out[...] = dup
    total[...] += nn(hidden, down_w[...])
    pd[...] += nt(hidden, down_a[...])
    dlg[...] += nt(dgate, gate_b[...])
    dlu[...] += nt(dup, up_b[...])
    at = pl.ds(pl.multiple_of(f * width, LOW), width)
    tables[0:LOW, at] = nn(lg_t[...], dgate).astype(bf16)
    tables[LOW : 2 * LOW, at] = nn(lu_t[...], dup).astype(bf16)
    tables[2 * LOW : 3 * LOW, at] = nn(dpd_t[...], hidden).astype(bf16)

    @pl.when(f == pl.num_programs(0) - 1)
    def _():
        low = pd[...].astype(bf16) * mask[...]
        ze_out[:, 0:D] = (total[...] + nn(low, db[...])).astype(bf16)
        ze_out[:, D : D + LOW] = nn(low, fold(2 * RANK)).astype(bf16)
        dlg_out[...] = dlg[...].astype(bf16) * mask[...]
        dlu_out[...] = dlu[...].astype(bf16) * mask[...]
        first = 0
        for out in tables_out:
            parts, _, size = out.shape
            for z in range(parts):
                start = z * (tables.shape[1] // parts) + first
                out[z] = tables[:, start : start + size]
            first += size


def expert_rows_kernel(
    dg_far, du_far, dlg, dlu, gate_far, up_far, ga, ua, dm_out,
    dg, du, gate_w, up_w, load_sems, sems,
):
    n = pl.program_id(0)
    width, depth = gate_w.shape[1:]
    span = depth // load_sems.shape[1]
    prime, advance = weight_stream(
        n,
        D // width,
        lambda at, slot: [
            pltpu.make_async_copy(
                gate_far.at[block_at(at, width), :], gate_w.at[slot], sems.at[0, slot]
            ),
            pltpu.make_async_copy(
                up_far.at[block_at(at, width), :], up_w.at[slot], sems.at[1, slot]
            ),
        ],
    )
    parts = [slice(j * span, (j + 1) * span) for j in range(load_sems.shape[1])]
    loads = [
        (
            pltpu.make_async_copy(dg_far.at[:, at], dg.at[:, at], load_sems.at[0, j]),
            pltpu.make_async_copy(du_far.at[:, at], du.at[:, at], load_sems.at[1, j]),
        )
        for j, at in enumerate(parts)
    ]
    slot = lax.rem(n, DEPTH)

    def give(total):
        total = total + nn(dlg[...], ga[...]) + nn(dlu[...], ua[...])
        dm_out[:, block_at(n, width)] = total.astype(bf16)

    @pl.when(n == 0)
    def _():
        for pair in loads[:1]:
            for load in pair:
                load.start()
        prime()
        for pair in loads[1:]:
            for load in pair:
                load.start()
        low = nn(dlg[...], fold(0)) + nn(dlu[...], fold(RANK))
        dm_out[:, D : D + LOW] = low.astype(bf16)

    advance()

    @pl.when(n == 0)
    def _():
        total = None
        for at, pair in zip(parts, loads, strict=True):
            for load in pair:
                load.wait()
            new = nt(dg[:, at], gate_w[slot, :, at]) + nt(du[:, at], up_w[slot, :, at])
            total = new if total is None else total + new
        give(total)

    @pl.when(n > 0)
    def _():
        give(nt(dg[...], gate_w[slot]) + nt(du[...], up_w[slot]))


def attention_back_kernel(shards, places, left, *refs):
    parts, refs = refs[:shards], refs[shards:]
    *refs, da = refs

    @pl.when(pl.program_id(0) == 0)
    def _():
        join_rows(places, left, parts, da)

    attention_back_steps(da, *refs)


def attention_back_steps(
    da, wo_far, wq_far, wk, wv, aq, amisc, bcat, kb, vb, oa, ob, routes,
    ga_far, o_far, q_far, k_far, v_far, lse_far, low_far, misc_far, cosf_far, sinf_far,
    dx_out, lows_out, grad_oa_out, grad_qb_out, grad_kv_out,
    ga, o, q, k, v, lse, low, misc, cosf, sinf, sems,
    dzl, dosum, do, stats, dq, dk, dv, lows_dense, dk_sum, dv_sum, chosen, wo, wq, wo_sems, wq_sems,
):
    step = pl.program_id(0)
    s, width = k.shape
    width_d = wq.shape[2]
    prime_o, next_o = weight_stream(
        step,
        ATT_EXPERTS,
        lambda n, slot: [
            pltpu.make_async_copy(wo_far.at[n], wo.at[slot], wo_sems.at[slot]),
        ],
    )
    prime_q, next_q = weight_stream(
        step - ATT_EXPERTS,
        D // width_d,
        lambda n, slot: [
            pltpu.make_async_copy(
                wq_far.at[:, block_at(n, width_d), :], wq.at[slot], wq_sems.at[slot]
            ),
        ],
    )
    loads = copies(
        (ga_far, o_far, q_far, k_far, v_far, lse_far, low_far, misc_far, cosf_far, sinf_far),
        (ga, o, q, k, v, lse, low, misc, cosf, sinf),
        sems,
    )

    @pl.when(step == 0)
    def _():
        prime_o()
        for load in loads:
            load.start()
        dzl[...] = nt(da[...], ob[...])
        for j in range(2):
            mine = routed(routes[:, j : j + 1], (s, LOW))
            part = jnp.where(mine, dzl[...], 0.0).astype(bf16)
            dosum[j * s : (j + 1) * s, :] = nn(part, oa[...])

    @pl.when(step < ATT_EXPERTS)
    def _():
        next_o()
        select_add(dosum, nt(da[...], wo[lax.rem(step, DEPTH)]), routes, step)

    @pl.when(step == ATT_EXPERTS - 1)
    def _():
        prime_q()
        for load in loads:
            load.wait()
        out_back(routes, ga, o, dzl, dosum, do, stats, grad_oa_out)
        attend_back(
            q, k, v, do, lse, stats, cosf, sinf, bcat, kb, vb, low, misc, routes,
            dq, dk, dv, lows_out, lows_dense, grad_qb_out, grad_kv_out, dk_sum, dv_sum,
        )
        spread_rows(dq, routes, chosen)

    @pl.when(step >= ATT_EXPERTS)
    def _():
        next_q()
        slot = lax.rem(step - ATT_EXPERTS, DEPTH)
        total = (
            nn(lows_dense[:, 0:LOW], aq[...])
            + nn(lows_dense[:, LOW : 2 * LOW], amisc[...])
            + nt(dk[...], wk[...])
            + nt(dv[...], wv[...])
        )
        for e in range(ATT_EXPERTS):
            total = total + nt(chosen[:, e * width : (e + 1) * width], wq[slot, e])
        dx_out[...] = total.astype(bf16)


def out_back(routes, ga, o, dzl, dosum, do_out, stats_out, grad_oa_out):
    s, width = o.shape[0] // 2, o.shape[1]
    grad_oa = jnp.zeros((LOW, width), f32)
    for k in range(2):
        at = slice(k * s, (k + 1) * s)
        gate = ga[:, k : k + 1]
        mine = routed(routes[:, k : k + 1], (s, LOW))
        low = jnp.where(mine, gate * dzl[...], 0.0).astype(bf16)
        grad_oa = grad_oa + tn(low, o[at, :])
        stats = jnp.zeros((s, LOW), f32)
        slope = jnp.zeros((s, 1), f32)
        for h in range(width // HD):
            hs = slice(h * HD, (h + 1) * HD)
            before = dosum[at, hs]
            part = jnp.sum(o[at, hs].astype(f32) * before, axis=1, keepdims=True)
            slope = slope + part
            stats = stats + in_lane(gate * part, h)
            do_out[at, hs] = (gate * before).astype(bf16)
        stats_out[at, :] = stats + in_lane(slope, GATE_LANE)
    grad_oa_out[...] = grad_oa.astype(bf16)


def attend_back(
    q, k, v, do, lse, stats, cosf, sinf, bcat, kb, vb, low, misc, routes,
    dq_out, dk_out, dv_out, lows_out, misc_back_out, grad_qb_out, grad_kv_out, dk_sum, dv_sum,
):
    s, width = k.shape
    for h in range(width // HD):
        hs = slice(h * HD, (h + 1) * HD)
        dk_sum[...] = jnp.zeros_like(dk_sum)
        dv_sum[...] = jnp.zeros_like(dv_sum)
        for i in range(s // CHUNK):
            end = (i + 1) * CHUNK
            first, second = slice(i * CHUNK, end), slice(s + i * CHUNK, s + end)
            queries = jnp.concatenate([q[first, hs], q[second, hs]], axis=0)
            grads = jnp.concatenate([do[first, hs], do[second, hs]], axis=0)
            logs = jnp.concatenate([lse[first, h : h + 1], lse[second, h : h + 1]], axis=0)
            centre = jnp.concatenate([stats[first, h : h + 1], stats[second, h : h + 1]], axis=0)
            scores = nt(queries, k[0:end, hs]) * score_scale
            weights = jnp.where(causal(i, scores.shape), jnp.exp(scores - logs), 0.0)
            dscores = (weights * (nt(grads, v[0:end, hs]) - centre)).astype(bf16)
            dq = nn(dscores, k[0:end, hs]) * score_scale
            cosine, sine = cosf[first, :], sinf[first, :]
            dq_out[first, hs] = unrope(dq[:CHUNK], cosine, sine).astype(bf16)
            dq_out[second, hs] = unrope(dq[CHUNK:], cosine, sine).astype(bf16)
            dk_sum[0:end, :] += tn(dscores, queries)
            dv_sum[0:end, :] += tn(weights.astype(bf16), grads)
        dk_out[:, hs] = unrope(dk_sum[...] * score_scale, cosf[...], sinf[...]).astype(bf16)
        dv_out[:, hs] = dv_sum[...].astype(bf16)
    row, column = iota((LOW, LOW), 0), iota((LOW, LOW), 1)
    grad_qb = jnp.zeros((LOW, width), f32)
    chunks = s // CHUNK
    half = chunks // 2
    packed = [None] * half
    slopes = jnp.zeros((16, LOW), f32)
    line, at_lane = iota((16, LOW), 0), iota((16, LOW), 1) == GATE_LANE
    for i in range(chunks):
        rs = slice(i * CHUNK, (i + 1) * CHUNK)
        misc_back = (nt(dk_out[rs, :], kb[...]) + nt(dv_out[rs, :], vb[...])).astype(bf16)
        lows = nn(misc_back, ones_where((column == row + 2 * RANK) & (row < 2 * RANK)))
        dense = jnp.zeros((CHUNK, LOW), f32)
        for j in range(2):
            at = slice(j * s + i * CHUNK, j * s + (i + 1) * CHUNK)
            mine = routed(routes[rs, j : j + 1], (CHUNK, LOW))
            part = jnp.where(mine, nt(dq_out[at, :], bcat[...]), 0.0).astype(bf16)
            dense = dense + part.astype(f32)
            fold_pair = ones_where((column == (row & (RANK - 1)) + j * RANK) & (column < 2 * RANK))
            lows = lows + nn(part, fold_pair)
            mark = ones_where((line == j * chunks + i) & at_lane)
            slopes = slopes + nt(mark, stats[at, :].astype(bf16))
            grad_qb = grad_qb + tn(
                jnp.where(mine, low[rs, :], jnp.zeros((), bf16)), dq_out[at, :]
            )
        if i < half:
            packed[i] = lows
        else:
            together = packed[i - half] + pltpu.roll(lows, LOW // 2, 1)
            lows_out[(i - half) * CHUNK : (i - half + 1) * CHUNK, :] = together.astype(bf16)
        misc_back_out[rs, 0:LOW] = dense.astype(bf16)
        misc_back_out[rs, LOW : 2 * LOW] = misc_back
    lows_out[half * CHUNK : half * CHUNK + 16, :] = slopes.astype(bf16)
    grad_qb_out[...] = grad_qb.astype(bf16)
    grad_kv_out[0:LOW, :] = tn(misc[...], dk_out[...]).astype(bf16)
    grad_kv_out[LOW : 2 * LOW, :] = tn(misc[...], dv_out[...]).astype(bf16)


def input_grad_kernel(dx, slopes, ga, tokens, gain, router, dh1, routes, out):
    x = tokens[...].astype(f32)
    gates = [ga[:, k : k + 1] for k in range(2)]
    slope = [slopes[:, k : k + 1] for k in range(2)]
    mean = gates[0] * slope[0] + gates[1] * slope[1]
    total = jnp.zeros(ga.shape, f32)
    lane = iota(ga.shape, 1)
    for k in range(2):
        mine = lane == routes[:, k : k + 1]
        total = total + jnp.where(mine, gates[k] * (slope[k] - mean), 0.0)
    grad = dx[...].astype(f32) + nn(total[:, 0 : router.shape[0]].astype(bf16), router[...])
    out[...] = dh1[...] + norm_backward(x, inverse_rms(x), gain[...].astype(f32), grad)


def after(value, *earlier):
    return lax.optimization_barrier((value, *earlier))[0]


def slot_places(routes, expert_count, capacity):
    choose = (routes[:, :, None] == jnp.arange(expert_count, dtype=jnp.int32)).astype(bf16)
    member = choose[:, 0] + choose[:, 1]
    count = routes.shape[0]
    before = (iota((count, count), 1) < iota((count, count), 0)).astype(bf16)
    slots = nn(before, member)
    mine = jnp.sum(slots[:, None, :] * choose.astype(f32), axis=2)
    return routes * capacity + mine.astype(jnp.int32)


def rotary_tables(count):
    half = HD // 2
    freq = jnp.exp(jnp.arange(half, dtype=f32) * (-2.0 * math.log(10000.0) / HD))
    angles = jnp.arange(count, dtype=jnp.int32).astype(f32)[:, None] * freq
    cosine, sine = jnp.cos(angles), jnp.sin(angles)
    return (
        jnp.concatenate([cosine, cosine], axis=1),
        jnp.concatenate([-sine, sine], axis=1),
    )


def on_device(
    tokens, cotangent, gain_first, gain_second, router_attn, router_mlp, query_w, key_w, value_w,
    output_w, gate_w, up_w, down_w, query_a, query_b, key_a, key_b, value_a, value_b, output_a,
    output_b, gate_a, gate_b, up_a, up_b, down_a, down_b, adapter_ids, attn_routes, mlp_routes,
):
    shards = lax.axis_size("shard")
    groups = lax.axis_size("dp")
    shard_at = lax.axis_index("shard")
    group_at = lax.axis_index("dp")
    rows = tokens.shape[0]
    seq = rows * shards
    cap_mlp = rows // 4 + rows // 16
    slices = groups // EXPERTS
    ff = gate_w.shape[1]
    width = key_w.shape[1]
    block = D // (groups * shards)
    own = groups * block
    adapter = adapter_ids[group_at]
    expert = group_at // slices

    x = tokens.astype(f32)
    normed = (x * inverse_rms(x) * gain_first.astype(f32)).astype(bf16)
    split = (D // LOW * 9 // 16) * LOW
    places = lax.rem(shard_at + shards - jnp.arange(shards, dtype=jnp.int32), shards)

    def shifted(part, step):
        pairs = [(i, (i + step) % shards) for i in range(shards)]
        return lax.ppermute(part, "shard", pairs) if step else part

    def gathered(left, right):
        return [lax.all_gather(left, "shard", axis=0, tiled=True)] + [
            shifted(right, step) for step in range(shards)
        ]

    xn_parts = gathered(normed[:, :split], normed[:, split:])

    mcol = slot_places(mlp_routes, EXPERTS, cap_mlp)
    mrow = mcol.T
    cosf, sinf = rotary_tables(seq)

    def ranks_first(factor):
        return jnp.swapaxes(factor, -1, -2)

    def of_adapter(factor, axis):
        return lax.dynamic_index_in_dim(factor, adapter, axis, keepdims=False)

    def pad_rows(parts, count=LOW):
        have = sum(p.shape[0] for p in parts)
        fill = jnp.zeros((count - have, parts[0].shape[1]), bf16)
        return jnp.concatenate(list(parts) + [fill], axis=0)

    aq = of_adapter(ranks_first(query_a), 1).reshape(LOW, D)
    amisc = pad_rows(
        [of_adapter(ranks_first(key_a), 0), of_adapter(ranks_first(value_a), 0), router_attn.T]
    )
    bcat = of_adapter(query_b, 1).reshape(LOW, width)
    key_second, value_second = of_adapter(key_b, 0), of_adapter(value_b, 0)
    kb = pad_rows([key_second])
    vb = pad_rows([jnp.zeros_like(value_second), value_second])
    oa = of_adapter(ranks_first(output_a), 1).reshape(LOW, width)
    ob = of_adapter(output_b, 1).reshape(LOW, D)
    router = pad_rows([router_mlp.T], 2 * EXPERTS)
    router_first = pad_rows([router_attn.T], 2 * ATT_EXPERTS)
    gain1, gain2 = gain_first.reshape(1, D), gain_second.reshape(1, D)

    def of_expert(factor):
        return lax.dynamic_index_in_dim(factor, expert, 0, keepdims=False).reshape(LOW, D)

    gate_first = of_expert(ranks_first(gate_a))
    up_first = of_expert(ranks_first(up_a))
    down_second = of_expert(down_b)
    gate_table = gate_b.reshape(LOW, ff)
    up_table = up_b.reshape(LOW, ff)
    down_table = ranks_first(down_a).reshape(LOW, ff)
    expert_rows = groups * cap_mlp
    source_adapter = jnp.repeat(adapter_ids, cap_mlp)
    mask = (
        source_adapter[:, None] == (jnp.arange(LOW, dtype=jnp.int32) // RANK)[None, :]
    ).astype(bf16)

    experts = (ATT_EXPERTS,)
    batch = 2
    batches = (ATT_EXPERTS // batch,)
    def to_experts(sent):
        wide = sent.shape[1]
        sent = jnp.repeat(sent.reshape(EXPERTS, cap_mlp, wide), slices, axis=0)
        got = lax.all_to_all(sent, "dp", split_axis=0, concat_axis=0, tiled=True)
        return got.reshape(expert_rows, wide)

    sent_rows = EXPERTS * cap_mlp
    picked = (mrow[0][None, :] == iota((sent_rows, rows), 0)) | (
        mrow[1][None, :] == iota((sent_rows, rows), 0)
    )
    grads_in = to_experts(nn(picked.astype(bf16), cotangent).astype(bf16))
    own_rows = lambda array: lax.dynamic_slice_in_dim(array, shard_at * rows, rows, 0)
    routes_own = own_rows(attn_routes)
    early_made = (router, router_first, gain1, gain2, mask, mrow, mcol, routes_own)
    early_made += (gate_first, up_first, down_second)
    early_made, xn_parts, grads_in = lax.optimization_barrier((early_made, xn_parts, grads_in))
    router, router_first, gain1, gain2, mask, mrow, mcol, routes_own, *firsts = early_made
    gate_first, up_first, down_second = firsts

    column_parts = 8
    width_d = D // column_parts
    steps_attn = ATT_EXPERTS + column_parts
    late = lambda e: jnp.maximum(e - ATT_EXPERTS, 0)
    column_block = pl.BlockSpec((LOW, width_d), lambda e: (0, late(e)))
    out_block = pl.BlockSpec((seq, width_d), lambda e: (0, late(e)))
    key_block = pl.BlockSpec((width_d, width), lambda e: (late(e), 0))
    far = pl.BlockSpec(memory_space=pl.ANY)
    project_flops = 4 * ATT_EXPERTS * seq * D * width
    weight_bytes = 4 * ATT_EXPERTS * D * width
    pair, row = ((2 * seq, width), bf16), ((seq, width), bf16)
    narrow, stat = ((seq, LOW), bf16), ((2 * seq, LOW), f32)
    saved = [pair, row, row, ((seq, LOW), f32), narrow, narrow, pair, stat]

    attn_part, low_part, q, k, v, ga, low, misc, o, lse = call(
        lambda *refs: attention_kernel(shards, *refs),
        (steps_attn,),
        [pl.BlockSpec(memory_space=pltpu.SMEM)]
        + [whole()] * (1 + shards)
        + [
            far,
            far,
            column_block,
            far,
            far,
        ]
        + [whole()] * 9,
        [out_block, whole()] + [far] * 8,
        [sds((seq, D), bf16), sds(*narrow)] + [sds(*shape) for shape in saved],
        [pltpu.VMEM(*shape) for shape in saved]
        + [
            pltpu.VMEM((2 * seq, width), f32),
            pltpu.VMEM(*pair),
            pltpu.VMEM((seq, ATT_EXPERTS * width), bf16),
            pltpu.VMEM((D, width), bf16),
            pltpu.VMEM((D, width), bf16),
            pltpu.SemaphoreType.DMA((2,)),
            pltpu.SemaphoreType.DMA((8,)),
            pltpu.VMEM((DEPTH, D, width), bf16),
            pltpu.VMEM((DEPTH, ATT_EXPERTS, width, width_d), bf16),
            pltpu.SemaphoreType.DMA((DEPTH,)),
            pltpu.SemaphoreType.DMA((DEPTH,)),
            pltpu.VMEM((seq, D), bf16),
        ],
        project_flops,
        weight_bytes,
    )(places, *xn_parts, query_w, output_w, ob, key_w, value_w, aq, amisc, bcat, kb, vb, attn_routes, cosf, sinf, oa)

    attn = lax.psum_scatter(attn_part, "shard", scatter_dimension=0, tiled=True)

    rows_sent, gm, m = call(
        lambda *refs: dispatch_kernel(cap_mlp, *refs),
        (),
        [whole()] * 6,
        [whole()] * 3,
        [
            sds((sent_rows, D + LOW), bf16),
            sds((rows, LOW), f32),
            sds((rows, D), bf16),
        ],
        [],
        6 * sent_rows * rows * D,
        8 * sent_rows * D,
    )(attn, tokens, gain2, router, mrow, mcol)

    def from_experts(made):
        got = lax.all_to_all(
            made.reshape(groups, cap_mlp, D + LOW), "dp", split_axis=0, concat_axis=0, tiled=True
        )
        if slices > 1:
            parts = got.reshape(EXPERTS, slices, cap_mlp, D + LOW).astype(f32)
            got = jnp.sum(parts, axis=1).astype(bf16)
        return got.reshape(sent_rows, D + LOW)

    def by_column_owner(part):
        split = part.reshape(rows, groups, shards, block)
        return split.transpose(2, 0, 1, 3).reshape(shards, rows, own)

    columns_sent = jnp.concatenate([by_column_owner(m), by_column_owner(cotangent)], axis=2)
    low_lanes = low_part.reshape(shards, rows, LOW).transpose(1, 0, 2).reshape(rows, shards * LOW)
    arrived = []
    for step in range(shards):
        piece = lax.dynamic_index_in_dim(
            columns_sent, lax.rem(shard_at + step, shards), 0, keepdims=False
        )
        piece = jnp.concatenate([piece, low_lanes], axis=1)
        arrived.append(shifted(piece, step))

    rows_in = to_experts(rows_sent)

    steps = 11
    fb = ff // steps
    table = pl.BlockSpec((LOW, fb), lambda f: (0, f))
    kept = pl.BlockSpec((expert_rows, fb), lambda f: (0, f))
    weight_flops = 2 * expert_rows * D * ff
    weight_moved = 2 * D * ff
    low_shape = sds((expert_rows, LOW), bf16)
    wide_shape = sds((expert_rows, ff), bf16)
    out_shape = sds((expert_rows, D + LOW), bf16)

    g, u, lg, lu = call(
        expert_up_kernel,
        (steps,),
        [whole()] * 4 + [far, far, table, table],
        [kept, kept, whole(), whole()],
        [wide_shape, wide_shape, low_shape, low_shape],
        [
            pltpu.VMEM((DEPTH, D, fb), bf16),
            pltpu.VMEM((DEPTH, D, fb), bf16),
            pltpu.SemaphoreType.DMA((2, DEPTH)),
        ],
        2 * weight_flops,
        2 * weight_moved,
    )(rows_in, mask, gate_first, up_first, gate_w, up_w, gate_table, up_table)

    g, *arrived = lax.optimization_barrier((g, *arrived))
    arrived = jnp.concatenate(arrived, axis=0)
    mlp_columns = arrived[:, : 2 * own]
    out_lows = jnp.sum(
        arrived[:, 2 * own :].reshape(shards, rows, shards, LOW).astype(f32), axis=0
    )
    out_lows = out_lows.astype(bf16).transpose(1, 0, 2).reshape(seq, LOW)

    each = ff // shards
    head = (each // LOW * 2 // 3) * LOW
    spans = [head, each - head] if each % LOW == 0 else [each]
    low_sum = pltpu.VMEM((expert_rows, LOW), f32)
    low_turned = pltpu.VMEM((LOW, expert_rows), bf16)
    ze, dg, du, dlg, dlu, *tables = call(
        expert_down_kernel,
        (steps,),
        [whole()] * 6 + [kept, kept, far, table, table, table],
        [whole(), kept, kept, whole(), whole()] + [whole() for _ in spans],
        [out_shape, wide_shape, wide_shape, low_shape, low_shape]
        + [sds((shards, 3 * LOW, span), bf16) for span in spans],
        [pltpu.VMEM((expert_rows, D), bf16)]
        + [pltpu.VMEM((expert_rows, D), f32), low_sum, low_sum, low_sum]
        + [pltpu.VMEM((expert_rows, LOW), bf16)]
        + [low_turned] * 3
        + [
            pltpu.VMEM((3 * LOW, ff), bf16),
            pltpu.VMEM((DEPTH, fb, D), bf16),
            pltpu.SemaphoreType.DMA((DEPTH,)),
        ],
        2 * weight_flops,
        weight_moved,
    )(grads_in, rows_in, mask, down_second, lg, lu, g, u, down_w, gate_table, up_table, down_table)

    ze_back = from_experts(ze)

    def table_sum(part):
        part = part.reshape(-1, part.shape[-1])
        return lax.psum_scatter(part, "shard", scatter_dimension=0, tiled=True)

    head_tables = table_sum(tables[0])

    parts = 4
    db = D // parts
    loads = ff // (11 * LOW) if ff % (11 * LOW) == 0 else 1
    low_block = pl.BlockSpec((LOW, db), lambda n: (0, n))
    dm = call(
        expert_rows_kernel,
        (parts,),
        [far, far, whole(), whole(), far, far, low_block, low_block],
        whole(),
        out_shape,
        [
            pltpu.VMEM((expert_rows, ff), bf16),
            pltpu.VMEM((expert_rows, ff), bf16),
            pltpu.VMEM((DEPTH, db, ff), bf16),
            pltpu.VMEM((DEPTH, db, ff), bf16),
            pltpu.SemaphoreType.DMA((2, loads)),
            pltpu.SemaphoreType.DMA((2, DEPTH)),
        ],
        2 * weight_flops,
        2 * weight_moved,
    )(dg, du, dlg, dlu, gate_w, up_w, gate_first, up_first)

    dm_back = from_experts(dm)

    layer_out, dlm, low_down = call(
        lambda *refs: combine_kernel(cap_mlp, *refs),
        (),
        [whole()] * 6,
        [whole()] * 3,
        [sds((rows, D), bf16), sds((rows, LOW), bf16), sds((rows, LOW), f32)],
        [],
        4 * sent_rows * rows * D,
        4 * sent_rows * D,
    )(ze_back, attn, tokens, cotangent, gm, mcol)

    dm_back = after(dm_back, head_tables)
    dh1, da_left, da_right = call(
        hidden_grad_kernel,
        (),
        [whole()] * 10,
        [whole()] * 3,
        [
            sds((rows, D), f32),
            sds((rows, split), bf16),
            sds((rows, D - split + LOW), bf16),
        ],
        [],
        2 * sent_rows * rows * D,
        4 * sent_rows * D,
    )(dm_back, dlm, low_down, attn, tokens, cotangent, gain2, router, mcol, mlp_routes)

    da_parts = gathered(da_left, da_right)
    owner_places = jnp.concatenate([places, jnp.full((1,), block, jnp.int32)])
    xn_own = call(
        lambda *refs: own_columns_kernel(shards, *refs),
        (),
        [pl.BlockSpec(memory_space=pltpu.SMEM)] + [whole()] * (shards + 1),
        whole(),
        sds((seq, own), bf16),
        [pltpu.VMEM((seq, D), bf16), pltpu.VMEM((D, own), bf16)],
        0,
        0,
    )(owner_places, *after(xn_parts, da_left))
    *da_parts, xn_own = lax.optimization_barrier((*da_parts, xn_own))
    tables_sum = [head_tables] + [table_sum(after(part, *da_parts)) for part in tables[1:]]

    loaded = [((seq, LOW), f32), pair, pair, row, row, stat, narrow, narrow]
    loaded += [((seq, HD), f32), ((seq, HD), f32)]
    dx_part, lows, grad_oa, grad_qb, grad_kv = call(
        lambda *refs: attention_back_kernel(shards, *refs),
        (steps_attn,),
        [pl.BlockSpec(memory_space=pltpu.SMEM)]
        + [whole()] * (1 + shards)
        + [
            far,
            far,
            key_block,
            key_block,
            column_block,
            column_block,
        ]
        + [whole()] * 6
        + [far] * 10,
        [out_block] + [whole()] * 4,
        [
            sds((seq, D), bf16),
            sds((seq // 2 + 16, LOW), bf16),
            sds((LOW, width), bf16),
            sds((LOW, width), bf16),
            sds((2 * LOW, width), bf16),
        ],
        [pltpu.VMEM(*shape) for shape in loaded]
        + [
            pltpu.SemaphoreType.DMA((10,)),
            pltpu.VMEM((seq, LOW), f32),
            pltpu.VMEM((2 * seq, width), f32),
            pltpu.VMEM(*pair),
            pltpu.VMEM(*stat),
            pltpu.VMEM(*pair),
            pltpu.VMEM(*row),
            pltpu.VMEM(*row),
            pltpu.VMEM((seq, 2 * LOW), bf16),
            pltpu.VMEM((seq, HD), f32),
            pltpu.VMEM((seq, HD), f32),
            pltpu.VMEM((seq, ATT_EXPERTS * width), bf16),
            pltpu.VMEM((DEPTH, width, D), bf16),
            pltpu.VMEM((DEPTH, ATT_EXPERTS, width_d, width), bf16),
            pltpu.SemaphoreType.DMA((DEPTH,)),
            pltpu.SemaphoreType.DMA((DEPTH,)),
            pltpu.VMEM((seq, D), bf16),
        ],
        project_flops,
        weight_bytes,
    )(places, *da_parts, output_w, query_w, key_w, value_w, aq, amisc, bcat, kb, vb, oa, ob, attn_routes, ga, o, q, k, v, lse, low, misc, cosf, sinf)

    held = (dx_part, lows, grad_oa, grad_qb, grad_kv, *da_parts, *tables_sum)
    dx_part, lows, grad_oa, grad_qb, grad_kv, *held = lax.optimization_barrier(held)
    da_parts, tables_sum = held[: shards + 1], held[shards + 1 :]
    lows_parts = [lows] + [shifted(lows, step) for step in range(1, shards)]
    chain = (*lows_parts, *da_parts)
    chain = lax.optimization_barrier(chain)
    lows_parts, da_parts = chain[:shards], chain[shards:]
    factors, grad_ob_own = call(
        lambda *refs: owner_kernel(shards, *refs),
        (),
        [pl.BlockSpec(memory_space=pltpu.SMEM)] + [whole()] * (shards + 3),
        [whole()] * 2,
        [sds((3 * LOW, own), bf16), sds((LOW, own), bf16)],
        [
            pltpu.VMEM((seq, own), bf16),
            pltpu.VMEM((seq, D), bf16),
            pltpu.VMEM((D, own), bf16),
        ],
        0,
        0,
    )(owner_places, *da_parts, out_lows, mlp_columns)
    lows_sum = sum(part.astype(f32) for part in lows_parts)
    half = LOW // 2
    lows_all = jnp.concatenate([lows_sum[: seq // 2, :half], lows_sum[: seq // 2, half:]], axis=0)
    lows_all = lows_all.astype(bf16)
    slopes = lows_sum[seq // 2 : seq // 2 + 2 * (seq // CHUNK)].reshape(2, seq).T
    dx = lax.psum_scatter(dx_part, "shard", scatter_dimension=0, tiled=True)

    input_grad = call(
        input_grad_kernel,
        (),
        [whole()] * 8,
        whole(),
        sds((rows, D), f32),
        [],
        2 * rows * LOW * D,
        24 * rows * D,
    )(dx, own_rows(slopes), own_rows(ga), tokens, gain1, router_first, dh1, routes_own)

    lane = jnp.arange(LOW, dtype=jnp.int32)
    dense = jnp.zeros((seq, LOW), f32)
    for j in range(2):
        spread = (iota((half, LOW), 0) == (lane % RANK + j * RANK)[None, :]).astype(bf16)
        chosen = attn_routes[:, j : j + 1] == (lane // RANK)[None, :]
        dense = dense + jnp.where(chosen, nn(lows_all, spread), 0.0)
    grad_qa_own = tn(dense.astype(bf16), xn_own)
    grad_kva_own = tn(lows_all[:, 2 * RANK : 4 * RANK], xn_own)

    def to_owner_columns(part):
        return part.reshape(-1, groups, block).transpose(1, 0, 2).reshape(groups, -1)

    def to_owner_ranks(part):
        parts = part.reshape(-1, groups, RANK // groups, width)
        return parts.transpose(1, 0, 2, 3).reshape(groups, -1)

    sending = [
        to_owner_columns(grad_qa_own.astype(bf16)),
        to_owner_columns(grad_ob_own),
        to_owner_columns(grad_kva_own.astype(bf16)),
        to_owner_ranks(grad_qb),
        to_owner_ranks(grad_oa),
        to_owner_ranks(jnp.concatenate([grad_kv[:RANK], grad_kv[LOW + RANK : LOW + 2 * RANK]])),
        to_owner_columns(factors),
    ]
    sizes = [piece.shape[1] for piece in sending]
    sent = jnp.concatenate(sending, axis=1).reshape(groups, -1, LOW)
    got = lax.all_to_all(sent, "dp", split_axis=0, concat_axis=0, tiled=True)
    got = got.reshape(groups, -1).astype(f32)
    pick_source = (adapter_ids[:, None] == jnp.arange(ADAPTERS, dtype=jnp.int32)[None, :]).astype(
        f32
    )
    placed_sums = jnp.einsum("sa,sn->an", pick_source, got, precision=precise)
    parts = []
    start = 0
    for size in sizes:
        parts.append(placed_sums[:, start : start + size])
        start += size
    ranks_own = RANK // groups

    def columns_out(part, count):
        return part.reshape(ADAPTERS, count, RANK, block)

    def ranks_out(part, count):
        return part.reshape(ADAPTERS, count, ranks_own, width)

    query_a_sum = columns_out(parts[0], ATT_EXPERTS).transpose(1, 0, 3, 2)
    output_b_sum = columns_out(parts[1], ATT_EXPERTS).transpose(1, 0, 2, 3)
    kv_a_sum = columns_out(parts[2], 2).transpose(1, 0, 3, 2)
    query_b_sum = ranks_out(parts[3], ATT_EXPERTS).transpose(1, 0, 2, 3)
    output_a_sum = ranks_out(parts[4], ATT_EXPERTS).transpose(1, 0, 3, 2)
    kv_b_sum = ranks_out(parts[5], 2).transpose(1, 0, 2, 3)
    factor_sum = columns_out(parts[6], 3 * EXPERTS).transpose(1, 0, 2, 3)
    gate_a_sum = factor_sum[:EXPERTS].transpose(0, 1, 3, 2)
    up_a_sum = factor_sum[EXPERTS : 2 * EXPERTS].transpose(0, 1, 3, 2)
    down_b_sum = factor_sum[2 * EXPERTS :]

    joined = jnp.concatenate(tables_sum, axis=1) if len(tables_sum) > 1 else tables_sum[0]
    joined = joined.astype(f32).reshape(3, ADAPTERS, RANK, each)

    return (
        layer_out,
        input_grad,
        query_a_sum,
        query_b_sum,
        kv_a_sum[0],
        kv_b_sum[0],
        kv_a_sum[1],
        kv_b_sum[1],
        output_a_sum,
        output_b_sum,
        gate_a_sum,
        joined[0],
        up_a_sum,
        joined[1],
        ranks_first(joined[2]),
        down_b_sum,
    )


def solution(mesh):
    placed = (
        P(("dp", "shard"), None),
        P(("dp", "shard"), None),
        P(),
        P(),
        P(),
        P(),
        P(None, None, "shard"),
        P(None, "shard"),
        P(None, "shard"),
        P(None, "shard", None),
        P(None, "dp"),
        P(None, "dp"),
        P("dp", None),
        P(),
        P(None, None, None, "shard"),
        P(),
        P(None, None, "shard"),
        P(),
        P(None, None, "shard"),
        P(None, None, "shard", None),
        P(),
        P(),
        P(None, None, "dp"),
        P(),
        P(None, None, "dp"),
        P(None, "dp", None),
        P(),
        P(),
        P("dp", None),
        P(("dp", "shard"), None),
    )
    return jax.shard_map(
        on_device,
        mesh=mesh,
        in_specs=placed,
        out_specs=(
            P(("dp", "shard"), None),
            P(("dp", "shard"), None),
            P(None, None, ("dp", "shard"), None),
            P(None, None, "dp", "shard"),
            P(None, ("dp", "shard"), None),
            P(None, "dp", "shard"),
            P(None, ("dp", "shard"), None),
            P(None, "dp", "shard"),
            P(None, None, "shard", "dp"),
            P(None, None, None, ("dp", "shard")),
            P(None, None, ("dp", "shard"), None),
            P(None, None, ("dp", "shard")),
            P(None, None, ("dp", "shard"), None),
            P(None, None, ("dp", "shard")),
            P(None, ("dp", "shard"), None),
            P(None, None, None, ("dp", "shard")),
        ),
        check_vma=False,
    )
```

```python
import math

import jax
import jax.numpy as jnp
from jax import lax
from jax.experimental import pallas as pl
from jax.experimental.pallas import tpu as pltpu
from jax.sharding import PartitionSpec as P

D = 2048
HD = 128
EXPERTS = 8
ATT_EXPERTS = 8
ADAPTERS = 8
RANK = 16
LOW = 128
CHUNK = 128
GATE_LANE = 64
ROUTE_LANE = 96
ROUTER_ROW = 32
DEPTH = 3


f32 = jnp.float32
bf16 = jnp.bfloat16
precise = lax.Precision.HIGHEST
eps = 1e-05
score_scale = HD ** (-0.5)


def nn(a, b):
    return lax.dot_general(a, b, (((1,), (0,)), ((), ())), preferred_element_type=f32)


def nt(a, b):
    return lax.dot_general(a, b, (((1,), (1,)), ((), ())), preferred_element_type=f32)


def tn(a, b):
    return lax.dot_general(a, b, (((0,), (0,)), ((), ())), preferred_element_type=f32)


def iota(shape, axis):
    return lax.broadcasted_iota(jnp.int32, shape, axis)


def ones_where(condition):
    return jnp.where(condition, 1.0, 0.0).astype(bf16)


def inverse_rms(values):
    return lax.rsqrt(jnp.mean(values * values, axis=-1, keepdims=True) + eps)


def norm_backward(values, inverse, gain_vector, grad_normed):
    weighted = gain_vector * grad_normed
    return inverse * weighted - values * (inverse * inverse * inverse) * jnp.mean(
        values * weighted, axis=-1, keepdims=True
    )


def softmax_pair(first, second):
    peak = jnp.maximum(first, second)
    one, two = jnp.exp(first - peak), jnp.exp(second - peak)
    total = one + two
    return one / total, two / total


def in_lane(column, lane, width=LOW):
    shape = (column.shape[0], width)
    return jnp.where(iota(shape, 1) == lane, column, 0.0)


def lane_of(values, lane):
    return jnp.sum(jnp.where(iota(values.shape, 1) == lane, values, 0.0), axis=1, keepdims=True)


def expert_lanes(dest, capacity, shape, group):
    lane = iota(shape, 1)
    low = (lane // group) * capacity
    return (dest >= low) & (dest < low + capacity)


def whole():
    return pl.BlockSpec(memory_space=pltpu.VMEM)


def sds(shape, dtype):
    return jax.ShapeDtypeStruct(shape, dtype)


def call(kernel, grid, in_specs, out_specs, out_shape, scratch, flops, moved):
    return pl.pallas_call(
        kernel,
        grid=grid,
        in_specs=in_specs,
        out_specs=out_specs,
        out_shape=out_shape,
        scratch_shapes=scratch,
        compiler_params=pltpu.CompilerParams(
            vmem_limit_bytes=60 * 1024 * 1024,
            dimension_semantics=("arbitrary",) * len(grid) if grid else None,
        ),
        cost_estimate=pl.CostEstimate(
            flops=4 * flops, bytes_accessed=4 * moved, transcendentals=0
        ),
    )


def rope(values, cosine, sine):
    return values * cosine + pltpu.roll(values, HD // 2, 1) * sine


def unrope(values, cosine, sine):
    return values * cosine - pltpu.roll(values, HD // 2, 1) * sine


def routed(route, shape):
    return (iota(shape, 1) // RANK) == route


def select_add(total, parts, routes, expert):
    s = parts[0].shape[0]
    for k in range(2):
        route = routes[:, k : k + 1]
        chosen = jnp.where(route == expert + 1, parts[1], 0.0)
        total[k * s : (k + 1) * s, :] += jnp.where(route == expert, parts[0], chosen)


def weight_stream(n, count, fetch):
    def prime():
        for j in range(min(DEPTH - 1, count)):
            for copy in fetch(j, j):
                copy.start()

    def advance():
        later = n + DEPTH - 1

        @pl.when(later < count)
        def _():
            for copy in fetch(later, lax.rem(later, DEPTH)):
                copy.start()

        for copy in fetch(n, lax.rem(n, DEPTH)):
            copy.wait()

    return prime, advance


def block_at(n, width):
    return pl.ds(pl.multiple_of(n * width, LOW), width)


def copies(sources, targets, sems):
    return [
        pltpu.make_async_copy(source, target, sems.at[j])
        for j, (source, target) in enumerate(zip(sources, targets, strict=True))
    ]


def join_rows(places, left, parts, out):
    split, rows = left.shape[1], parts[0].shape[0]
    out[:, 0:split] = left[...]
    for j, part in enumerate(parts):
        at = pl.ds(pl.multiple_of(places[j] * rows, 16), rows)
        out[at, split:] = part[:, 0 : out.shape[1] - split]


def attention_kernel(shards, places, left, *refs):
    parts, refs = refs[:shards], refs[shards:]
    *refs, xn = refs

    @pl.when(pl.program_id(0) == 0)
    def _():
        join_rows(places, left, parts, xn)

    attention_steps(xn, *refs)


def attention_steps(
    xn, wq_far, wo_far, ob, wk_far, wv_far, aq, amisc, bcat, kb, vb, routes, cosf, sinf, oa,
    attn_out, out_low, q_far, k_far, v_far, ga_far, low_far, misc_far, o_far, lse_far,
    q, k, v, ga, low, misc, o, lse, qsum, og, chosen, wk, wv, load_sems, save_sems, wq, wo, wq_sems, wo_sems,
):
    step = pl.program_id(0)
    phase = ATT_EXPERTS // 2
    s, width = k.shape
    loads = copies((wk_far, wv_far), (wk, wv), load_sems)
    width_d = wo.shape[3]
    prime_q, next_q = weight_stream(
        step,
        phase,
        lambda n, slot: [
            pltpu.make_async_copy(
                wq_far.at[pl.ds(2 * n, 2)], wq.at[slot], wq_sems.at[slot]
            ),
        ],
    )
    prime_o, next_o = weight_stream(
        step - phase,
        D // width_d,
        lambda n, slot: [
            pltpu.make_async_copy(
                wo_far.at[:, :, block_at(n, width_d)], wo.at[slot], wo_sems.at[slot]
            ),
        ],
    )
    saves = copies(
        (q, k, v, ga, low, misc, o, lse),
        (q_far, k_far, v_far, ga_far, low_far, misc_far, o_far, lse_far),
        save_sems,
    )

    @pl.when(step == 0)
    def _():
        prime_q()
        for load in loads:
            load.start()
        x = xn[...]
        low[...] = nt(x, aq[...]).astype(bf16)
        scores = nt(x, amisc[...])
        misc[...] = scores.astype(bf16)
        lane = iota((s, LOW), 1) - ROUTER_ROW
        gates = [
            jnp.sum(jnp.where(lane == routes[:, j : j + 1], scores, 0.0), axis=1, keepdims=True)
            for j in range(2)
        ]
        one, two = softmax_pair(*gates)
        ga[...] = in_lane(one, 0) + in_lane(two, 1)
        for j in range(2):
            mine = routed(routes[:, j : j + 1], (s, LOW))
            part = jnp.where(mine, low[...], jnp.zeros((), bf16))
            qsum[j * s : (j + 1) * s, :] = nn(part, bcat[...])

    @pl.when(step < phase)
    def _():
        next_q()
        slot = lax.rem(step, DEPTH)
        parts = [nn(xn[...], wq[slot, j]) for j in range(2)]
        select_add(qsum, parts, routes, 2 * step)

    @pl.when(step == phase - 1)
    def _():
        prime_o()
        for load in loads:
            load.wait()
        x = xn[...]
        keys = nn(x, wk[...]) + nn(misc[...], kb[...])
        for h in range(width // HD):
            hs = slice(h * HD, (h + 1) * HD)
            k[:, hs] = rope(keys[:, hs], cosf[...], sinf[...]).astype(bf16)
            for j in range(2):
                at = slice(j * s, (j + 1) * s)
                q[at, hs] = rope(qsum[at, hs], cosf[...], sinf[...]).astype(bf16)
        v[...] = (nn(x, wv[...]) + nn(misc[...], vb[...])).astype(bf16)
        attend(q, k, v, ga, o, og, lse)
        for save in saves:
            save.start()
        total = jnp.zeros((s, LOW), f32)
        for j in range(2):
            part = nt(og[j * s : (j + 1) * s, :], oa[...])
            total = total + jnp.where(routed(routes[:, j : j + 1], (s, LOW)), part, 0.0)
        out_low[...] = total.astype(bf16)
        spread_rows(og, routes, chosen)

    @pl.when(step >= phase)
    def _():
        next_o()
        weights = wo[lax.rem(step - phase, DEPTH)].reshape(chosen.shape[1], width_d)
        attn_out[...] = (nn(chosen[...], weights) + nn(out_low[...], ob[...])).astype(bf16)

    @pl.when(step == pl.num_programs(0) - 1)
    def _():
        for save in saves:
            save.wait()


def spread_rows(pair, routes, chosen):
    s, width = chosen.shape[0], pair.shape[1]
    for e in range(ATT_EXPERTS):
        chosen[:, e * width : (e + 1) * width] = of_expert_rows(pair, routes, e, s)


def causal(i, shape):
    row = (iota(shape, 0) & (CHUNK - 1)) + i * CHUNK
    return iota(shape, 1) <= row


def attend(q, k, v, ga, o_out, og_out, lse_out):
    s, width = k.shape
    for i in range(s // CHUNK):
        end = (i + 1) * CHUNK
        first, second = slice(i * CHUNK, end), slice(s + i * CHUNK, s + end)
        gates = [ga[first, 0:1], ga[first, 1:2]]
        log_totals = jnp.zeros((2 * CHUNK, LOW), f32)
        for h in range(width // HD):
            hs = slice(h * HD, (h + 1) * HD)
            queries = jnp.concatenate([q[first, hs], q[second, hs]], axis=0)
            scores = nt(queries, k[0:end, hs]) * score_scale
            scores = jnp.where(causal(i, scores.shape), scores, -1e30)
            peak = jnp.max(scores, axis=1, keepdims=True)
            weights = jnp.exp(scores - peak)
            total = jnp.sum(weights, axis=1, keepdims=True)
            mixed = nn(weights.astype(bf16), v[0:end, hs]) / total
            o_out[first, hs] = mixed[:CHUNK].astype(bf16)
            o_out[second, hs] = mixed[CHUNK:].astype(bf16)
            og_out[first, hs] = (mixed[:CHUNK] * gates[0]).astype(bf16)
            og_out[second, hs] = (mixed[CHUNK:] * gates[1]).astype(bf16)
            log_totals = log_totals + in_lane(peak + jnp.log(total), h)
        lse_out[first, :] = log_totals[:CHUNK]
        lse_out[second, :] = log_totals[CHUNK:]


def of_expert_rows(rows, routes, expert, s):
    return rows[0:s, :] * ones_where(routes[:, 0:1] == expert) + rows[s : 2 * s, :] * ones_where(
        routes[:, 1:2] == expert
    )


def second_norm(attn, tokens, gain):
    hidden = tokens[...].astype(f32) + attn[...].astype(f32)
    inverse = inverse_rms(hidden)
    return hidden, inverse, gain[...].astype(f32)


def dispatch_kernel(cap, attn, tokens, gain, router, mrow, mcol, rows_out, gm_out, m_out):
    hidden, inverse, scale = second_norm(attn, tokens, gain)
    m = (hidden * inverse * scale).astype(bf16)
    m_out[...] = m
    logits = nt(m, router[...])
    gates = softmax_pair(
        *[
            jnp.sum(
                jnp.where(
                    expert_lanes(mcol[:, k : k + 1], cap, logits.shape, 1),
                    logits,
                    0.0,
                ),
                axis=1,
                keepdims=True,
            )
            for k in range(2)
        ]
    )
    gm_out[...] = in_lane(gates[0], 0) + in_lane(gates[1], 1)
    slot = iota((rows_out.shape[0], mrow.shape[1]), 0)
    picks = [ones_where(mrow[k : k + 1, :] == slot) for k in range(2)]
    rows_out[:, 0:D] = nn(picks[0] + picks[1], m).astype(bf16)
    total = jnp.zeros((rows_out.shape[0], LOW), f32)
    for k in range(2):
        high = gates[k].astype(bf16).astype(f32)
        middle = (gates[k] - high).astype(bf16).astype(f32)
        both = in_lane(high, 0) + in_lane(middle, 1)
        total = total + nn(picks[k], both.astype(bf16))
    rows_out[:, D : D + LOW] = total.astype(bf16)


def fold(first_lane):
    row, column = iota((LOW, LOW), 0), iota((LOW, LOW), 1)
    return ones_where(column == (row & (RANK - 1)) + first_lane)


def spread(first_lane):
    row, column = iota((LOW, LOW), 0), iota((LOW, LOW), 1)
    return ones_where(row == (column & (RANK - 1)) + first_lane)


def combine_kernel(cap, ze, attn, tokens, cot, gm, mcol, layer_out, dlm_out, low_out):
    hidden = tokens[...].astype(f32) + attn[...].astype(f32)
    grad = cot[...].astype(f32)
    lane = iota((mcol.shape[0], ze.shape[0]), 1)
    gates, slopes, lows = [], [], []
    for k in range(2):
        gates.append(gm[:, k : k + 1])
        pick = ones_where(mcol[:, k : k + 1] == lane)
        expert_out = nn(pick, ze[:, 0:D])
        lows.append(gates[k] * nn(pick, ze[:, D : D + LOW]))
        slopes.append(jnp.sum(grad * expert_out, axis=1, keepdims=True))
        hidden = hidden + gates[k] * expert_out
    layer_out[...] = hidden.astype(bf16)
    low_out[...] = lows[0] + pltpu.roll(lows[1], 3 * RANK, 1)
    mean = gates[0] * slopes[0] + gates[1] * slopes[1]
    total = jnp.zeros(dlm_out.shape, f32)
    for k in range(2):
        mine = expert_lanes(mcol[:, k : k + 1], cap, dlm_out.shape, 1)
        total = total + jnp.where(mine, gates[k] * (slopes[k] - mean), 0.0)
    dlm_out[...] = total.astype(bf16)


def hidden_grad_kernel(
    rows, dlm, low, attn, tokens, cot, gain, router, mcol, routes, dh1_out, da_left, da_right
):
    hidden, inverse, scale = second_norm(attn, tokens, gain)
    lane = iota((mcol.shape[0], rows.shape[0]), 1)
    picks = [ones_where(mcol[:, k : k + 1] == lane) for k in range(2)]
    grad_m = nn(picks[0] + picks[1], rows[:, 0:D]) + nn(dlm[:, 0 : router.shape[0]], router[...])
    lows = [nn(pick, rows[:, D : D + LOW]) for pick in picks]
    total = low[...] + lows[0] + pltpu.roll(lows[1], 3 * RANK, 1)
    for k in range(2):
        total = total + in_lane(routes[:, k : k + 1].astype(f32), ROUTE_LANE + k)
    grad = cot[...].astype(f32) + norm_backward(hidden, inverse, scale, grad_m)
    dh1_out[...] = grad
    split = da_left.shape[1]
    da_left[...] = grad[:, :split].astype(bf16)
    da_right[:, 0 : D - split] = grad[:, split:].astype(bf16)
    da_right[:, D - split :] = total.astype(bf16)


def select_columns(places, shards, select):
    row, column = iota(select.shape, 0), iota(select.shape, 1)
    size = places[shards]
    group = lax.div(column, size)
    source = group * (size * shards) + places[0] * size + (column - group * size)
    select[...] = ones_where(row == source)


def own_columns_kernel(shards, places, *refs):
    parts, (out, gathered, select) = refs[: shards + 1], refs[shards + 1 :]
    select_columns(places, shards, select)
    join_rows(places, parts[0], parts[1:], gathered)
    out[...] = nn(gathered[...], select[...]).astype(bf16)


def owner_kernel(shards, places, *refs):
    da_refs, refs = refs[: shards + 1], refs[shards + 1 :]
    out_lows, columns, factors, grad_ob, da_own, gathered, select = refs
    own = da_own.shape[1]
    select_columns(places, shards, select)
    join_rows(places, da_refs[0], da_refs[1:], gathered)
    da_own[...] = nn(gathered[...], select[...]).astype(bf16)
    grad_ob[...] = tn(out_lows[...], da_own[...]).astype(bf16)
    right = D - da_refs[0].shape[1]
    lows = jnp.concatenate([ref[:, right : right + LOW] for ref in da_refs[1:]], axis=0)
    lane = (iota(lows.shape, 1) // RANK).astype(f32)
    mine = [lane_of(lows.astype(f32), ROUTE_LANE + k) == lane for k in range(2)]
    for part in range(3):
        dense = jnp.zeros(lows.shape, f32)
        for k in range(2):
            wide = nn(lows, spread((3 * k + part) * RANK))
            dense = dense + jnp.where(mine[k], wide, 0.0)
        at = slice(own, 2 * own) if part == 2 else slice(0, own)
        factors[part * LOW : (part + 1) * LOW, :] = tn(dense.astype(bf16), columns[:, at]).astype(
            bf16
        )


def identity():
    return ones_where(iota((LOW, LOW), 0) == iota((LOW, LOW), 1))


def expert_up_kernel(
    x, mask, ga, ua, gate_far, up_far, gate_b, up_b, g_out, u_out, lg_out, lu_out,
    gate_w, up_w, sems,
):
    x = x.at[:, 0:D]
    f = pl.program_id(0)
    width = gate_w.shape[2]
    prime, advance = weight_stream(
        f,
        gate_far.shape[1] // width,
        lambda n, slot: [
            pltpu.make_async_copy(
                gate_far.at[:, block_at(n, width)], gate_w.at[slot], sems.at[0, slot]
            ),
            pltpu.make_async_copy(
                up_far.at[:, block_at(n, width)], up_w.at[slot], sems.at[1, slot]
            ),
        ],
    )

    @pl.when(f == 0)
    def _():
        prime()
        lg_out[...] = nt(x[...], ga[...]).astype(bf16) * mask[...]
        lu_out[...] = nt(x[...], ua[...]).astype(bf16) * mask[...]

    advance()
    slot = lax.rem(f, DEPTH)
    g_out[...] = (nn(x[...], gate_w[slot]) + nn(lg_out[...], gate_b[...])).astype(bf16)
    u_out[...] = (nn(x[...], up_w[slot]) + nn(lu_out[...], up_b[...])).astype(bf16)


def expert_down_kernel(
    grads, x, mask, db, lg, lu, g, u, down_far, gate_b, up_b, down_a,
    ze_out, dg_out, du_out, dlg_out, dlu_out, *rest,
):
    *tables_out, dy, total, pd, dlg, dlu, dpd, lg_t, lu_t, dpd_t, tables, down, sems = rest
    f = pl.program_id(0)
    width = down.shape[1]
    prime, advance = weight_stream(
        f,
        down_far.shape[0] // width,
        lambda n, slot: [
            pltpu.make_async_copy(
                down_far.at[block_at(n, width), :], down.at[slot], sems.at[slot]
            ),
        ],
    )

    @pl.when(f == 0)
    def _():
        prime()
        gate = x[:, D : D + LOW].astype(f32)
        gate = lane_of(gate, 0) + lane_of(gate, 1)
        dy[...] = (gate * grads[...].astype(f32)).astype(bf16)
        dpd[...] = nt(dy[...], db[...]).astype(bf16) * mask[...]
        lg_t[...] = nt(identity(), lg[...]).astype(bf16)
        lu_t[...] = nt(identity(), lu[...]).astype(bf16)
        dpd_t[...] = nt(identity(), dpd[...]).astype(bf16)
        for sums in (total, pd, dlg, dlu):
            sums[...] = jnp.zeros_like(sums)

    advance()
    down_w = down.at[lax.rem(f, DEPTH)]
    dh = nt(dy[...], down_w[...]) + nn(dpd[...], down_a[...])
    gate = g[...].astype(f32)
    up = u[...].astype(f32)
    sig = jax.nn.sigmoid(gate)
    act = gate * sig
    hidden = (act * up).astype(bf16)
    dgate = (dh * up * (sig + act * (1.0 - sig))).astype(bf16)
    dup = (dh * act).astype(bf16)
    dg_out[...] = dgate
    du_out[...] = dup
    total[...] += nn(hidden, down_w[...])
    pd[...] += nt(hidden, down_a[...])
    dlg[...] += nt(dgate, gate_b[...])
    dlu[...] += nt(dup, up_b[...])
    at = pl.ds(pl.multiple_of(f * width, LOW), width)
    tables[0:LOW, at] = nn(lg_t[...], dgate).astype(bf16)
    tables[LOW : 2 * LOW, at] = nn(lu_t[...], dup).astype(bf16)
    tables[2 * LOW : 3 * LOW, at] = nn(dpd_t[...], hidden).astype(bf16)

    @pl.when(f == pl.num_programs(0) - 1)
    def _():
        low = pd[...].astype(bf16) * mask[...]
        ze_out[:, 0:D] = (total[...] + nn(low, db[...])).astype(bf16)
        ze_out[:, D : D + LOW] = nn(low, fold(2 * RANK)).astype(bf16)
        dlg_out[...] = dlg[...].astype(bf16) * mask[...]
        dlu_out[...] = dlu[...].astype(bf16) * mask[...]
        first = 0
        for out in tables_out:
            parts, _, size = out.shape
            for z in range(parts):
                start = z * (tables.shape[1] // parts) + first
                out[z] = tables[:, start : start + size]
            first += size


def expert_rows_kernel(
    dg_far, du_far, dlg, dlu, gate_far, up_far, ga, ua, dm_out,
    dg, du, gate_w, up_w, load_sems, sems,
):
    n = pl.program_id(0)
    width, depth = gate_w.shape[1:]
    span = depth // load_sems.shape[1]
    prime, advance = weight_stream(
        n,
        D // width,
        lambda at, slot: [
            pltpu.make_async_copy(
                gate_far.at[block_at(at, width), :], gate_w.at[slot], sems.at[0, slot]
            ),
            pltpu.make_async_copy(
                up_far.at[block_at(at, width), :], up_w.at[slot], sems.at[1, slot]
            ),
        ],
    )
    parts = [slice(j * span, (j + 1) * span) for j in range(load_sems.shape[1])]
    loads = [
        (
            pltpu.make_async_copy(dg_far.at[:, at], dg.at[:, at], load_sems.at[0, j]),
            pltpu.make_async_copy(du_far.at[:, at], du.at[:, at], load_sems.at[1, j]),
        )
        for j, at in enumerate(parts)
    ]
    slot = lax.rem(n, DEPTH)

    def give(total):
        total = total + nn(dlg[...], ga[...]) + nn(dlu[...], ua[...])
        dm_out[:, block_at(n, width)] = total.astype(bf16)

    @pl.when(n == 0)
    def _():
        for pair in loads[:1]:
            for load in pair:
                load.start()
        prime()
        for pair in loads[1:]:
            for load in pair:
                load.start()
        low = nn(dlg[...], fold(0)) + nn(dlu[...], fold(RANK))
        dm_out[:, D : D + LOW] = low.astype(bf16)

    advance()

    @pl.when(n == 0)
    def _():
        total = None
        for at, pair in zip(parts, loads, strict=True):
            for load in pair:
                load.wait()
            new = nt(dg[:, at], gate_w[slot, :, at]) + nt(du[:, at], up_w[slot, :, at])
            total = new if total is None else total + new
        give(total)

    @pl.when(n > 0)
    def _():
        give(nt(dg[...], gate_w[slot]) + nt(du[...], up_w[slot]))


def attention_back_kernel(shards, places, left, *refs):
    parts, refs = refs[:shards], refs[shards:]
    *refs, da = refs

    @pl.when(pl.program_id(0) == 0)
    def _():
        join_rows(places, left, parts, da)

    attention_back_steps(da, *refs)


def attention_back_steps(
    da, wo_far, wq_far, wk, wv, aq, amisc, bcat, kb, vb, oa, ob, routes,
    ga_far, o_far, q_far, k_far, v_far, lse_far, low_far, misc_far, cosf_far, sinf_far,
    dx_out, lows_out, grad_oa_out, grad_qb_out, grad_kv_out,
    ga, o, q, k, v, lse, low, misc, cosf, sinf, sems,
    dzl, dosum, do, stats, dq, dk, dv, lows_dense, dk_sum, dv_sum, chosen, wo, wq, wo_sems, wq_sems,
):
    step = pl.program_id(0)
    phase = ATT_EXPERTS // 2
    s, width = k.shape
    width_d = wq.shape[2]
    prime_o, next_o = weight_stream(
        step,
        phase,
        lambda n, slot: [
            pltpu.make_async_copy(
                wo_far.at[pl.ds(2 * n, 2)], wo.at[slot], wo_sems.at[slot]
            ),
        ],
    )
    prime_q, next_q = weight_stream(
        step - phase,
        D // width_d,
        lambda n, slot: [
            pltpu.make_async_copy(
                wq_far.at[:, block_at(n, width_d), :], wq.at[slot], wq_sems.at[slot]
            ),
        ],
    )
    loads = copies(
        (ga_far, o_far, q_far, k_far, v_far, lse_far, low_far, misc_far, cosf_far, sinf_far),
        (ga, o, q, k, v, lse, low, misc, cosf, sinf),
        sems,
    )

    @pl.when(step == 0)
    def _():
        prime_o()
        for load in loads:
            load.start()
        dzl[...] = nt(da[...], ob[...])
        for j in range(2):
            mine = routed(routes[:, j : j + 1], (s, LOW))
            part = jnp.where(mine, dzl[...], 0.0).astype(bf16)
            dosum[j * s : (j + 1) * s, :] = nn(part, oa[...])

    @pl.when(step < phase)
    def _():
        next_o()
        slot = lax.rem(step, DEPTH)
        parts = [nt(da[...], wo[slot, j]) for j in range(2)]
        select_add(dosum, parts, routes, 2 * step)

    @pl.when(step == phase - 1)
    def _():
        prime_q()
        for load in loads:
            load.wait()
        out_back(routes, ga, o, dzl, dosum, do, stats, grad_oa_out)
        attend_back(
            q, k, v, do, lse, stats, cosf, sinf, bcat, kb, vb, low, misc, routes,
            dq, dk, dv, lows_out, lows_dense, grad_qb_out, grad_kv_out, dk_sum, dv_sum,
        )
        spread_rows(dq, routes, chosen)

    @pl.when(step >= phase)
    def _():
        next_q()
        slot = lax.rem(step - phase, DEPTH)
        total = (
            nn(lows_dense[:, 0:LOW], aq[...])
            + nn(lows_dense[:, LOW : 2 * LOW], amisc[...])
            + nt(dk[...], wk[...])
            + nt(dv[...], wv[...])
        )
        for e in range(ATT_EXPERTS):
            total = total + nt(chosen[:, e * width : (e + 1) * width], wq[slot, e])
        dx_out[...] = total.astype(bf16)


def out_back(routes, ga, o, dzl, dosum, do_out, stats_out, grad_oa_out):
    s, width = o.shape[0] // 2, o.shape[1]
    grad_oa = jnp.zeros((LOW, width), f32)
    for k in range(2):
        at = slice(k * s, (k + 1) * s)
        gate = ga[:, k : k + 1]
        mine = routed(routes[:, k : k + 1], (s, LOW))
        low = jnp.where(mine, gate * dzl[...], 0.0).astype(bf16)
        grad_oa = grad_oa + tn(low, o[at, :])
        stats = jnp.zeros((s, LOW), f32)
        slope = jnp.zeros((s, 1), f32)
        for h in range(width // HD):
            hs = slice(h * HD, (h + 1) * HD)
            before = dosum[at, hs]
            part = jnp.sum(o[at, hs].astype(f32) * before, axis=1, keepdims=True)
            slope = slope + part
            stats = stats + in_lane(gate * part, h)
            do_out[at, hs] = (gate * before).astype(bf16)
        stats_out[at, :] = stats + in_lane(slope, GATE_LANE)
    grad_oa_out[...] = grad_oa.astype(bf16)


def attend_back(
    q, k, v, do, lse, stats, cosf, sinf, bcat, kb, vb, low, misc, routes,
    dq_out, dk_out, dv_out, lows_out, misc_back_out, grad_qb_out, grad_kv_out, dk_sum, dv_sum,
):
    s, width = k.shape
    for h in range(width // HD):
        hs = slice(h * HD, (h + 1) * HD)
        dk_sum[...] = jnp.zeros_like(dk_sum)
        dv_sum[...] = jnp.zeros_like(dv_sum)
        for i in range(s // CHUNK):
            end = (i + 1) * CHUNK
            first, second = slice(i * CHUNK, end), slice(s + i * CHUNK, s + end)
            queries = jnp.concatenate([q[first, hs], q[second, hs]], axis=0)
            grads = jnp.concatenate([do[first, hs], do[second, hs]], axis=0)
            logs = jnp.concatenate([lse[first, h : h + 1], lse[second, h : h + 1]], axis=0)
            centre = jnp.concatenate([stats[first, h : h + 1], stats[second, h : h + 1]], axis=0)
            scores = nt(queries, k[0:end, hs]) * score_scale
            weights = jnp.where(causal(i, scores.shape), jnp.exp(scores - logs), 0.0)
            dscores = (weights * (nt(grads, v[0:end, hs]) - centre)).astype(bf16)
            dq = nn(dscores, k[0:end, hs]) * score_scale
            cosine, sine = cosf[first, :], sinf[first, :]
            dq_out[first, hs] = unrope(dq[:CHUNK], cosine, sine).astype(bf16)
            dq_out[second, hs] = unrope(dq[CHUNK:], cosine, sine).astype(bf16)
            dk_sum[0:end, :] += tn(dscores, queries)
            dv_sum[0:end, :] += tn(weights.astype(bf16), grads)
        dk_out[:, hs] = unrope(dk_sum[...] * score_scale, cosf[...], sinf[...]).astype(bf16)
        dv_out[:, hs] = dv_sum[...].astype(bf16)
    row, column = iota((LOW, LOW), 0), iota((LOW, LOW), 1)
    grad_qb = jnp.zeros((LOW, width), f32)
    chunks = s // CHUNK
    half = chunks // 2
    packed = [None] * half
    slopes = jnp.zeros((16, LOW), f32)
    line, at_lane = iota((16, LOW), 0), iota((16, LOW), 1) == GATE_LANE
    for i in range(chunks):
        rs = slice(i * CHUNK, (i + 1) * CHUNK)
        misc_back = (nt(dk_out[rs, :], kb[...]) + nt(dv_out[rs, :], vb[...])).astype(bf16)
        lows = nn(misc_back, ones_where((column == row + 2 * RANK) & (row < 2 * RANK)))
        dense = jnp.zeros((CHUNK, LOW), f32)
        for j in range(2):
            at = slice(j * s + i * CHUNK, j * s + (i + 1) * CHUNK)
            mine = routed(routes[rs, j : j + 1], (CHUNK, LOW))
            part = jnp.where(mine, nt(dq_out[at, :], bcat[...]), 0.0).astype(bf16)
            dense = dense + part.astype(f32)
            fold_pair = ones_where((column == (row & (RANK - 1)) + j * RANK) & (column < 2 * RANK))
            lows = lows + nn(part, fold_pair)
            mark = ones_where((line == j * chunks + i) & at_lane)
            slopes = slopes + nt(mark, stats[at, :].astype(bf16))
            grad_qb = grad_qb + tn(
                jnp.where(mine, low[rs, :], jnp.zeros((), bf16)), dq_out[at, :]
            )
        if i < half:
            packed[i] = lows
        else:
            together = packed[i - half] + pltpu.roll(lows, LOW // 2, 1)
            lows_out[(i - half) * CHUNK : (i - half + 1) * CHUNK, :] = together.astype(bf16)
        misc_back_out[rs, 0:LOW] = dense.astype(bf16)
        misc_back_out[rs, LOW : 2 * LOW] = misc_back
    lows_out[half * CHUNK : half * CHUNK + 16, :] = slopes.astype(bf16)
    grad_qb_out[...] = grad_qb.astype(bf16)
    grad_kv_out[0:LOW, :] = tn(misc[...], dk_out[...]).astype(bf16)
    grad_kv_out[LOW : 2 * LOW, :] = tn(misc[...], dv_out[...]).astype(bf16)


def input_grad_kernel(dx, slopes, ga, tokens, gain, router, dh1, routes, out):
    x = tokens[...].astype(f32)
    gates = [ga[:, k : k + 1] for k in range(2)]
    slope = [slopes[:, k : k + 1] for k in range(2)]
    mean = gates[0] * slope[0] + gates[1] * slope[1]
    total = jnp.zeros(ga.shape, f32)
    lane = iota(ga.shape, 1)
    for k in range(2):
        mine = lane == routes[:, k : k + 1]
        total = total + jnp.where(mine, gates[k] * (slope[k] - mean), 0.0)
    grad = dx[...].astype(f32) + nn(total[:, 0 : router.shape[0]].astype(bf16), router[...])
    out[...] = dh1[...] + norm_backward(x, inverse_rms(x), gain[...].astype(f32), grad)


def after(value, *earlier):
    return lax.optimization_barrier((value, *earlier))[0]


def slot_places(routes, expert_count, capacity):
    choose = (routes[:, :, None] == jnp.arange(expert_count, dtype=jnp.int32)).astype(bf16)
    member = choose[:, 0] + choose[:, 1]
    count = routes.shape[0]
    before = (iota((count, count), 1) < iota((count, count), 0)).astype(bf16)
    slots = nn(before, member)
    mine = jnp.sum(slots[:, None, :] * choose.astype(f32), axis=2)
    return routes * capacity + mine.astype(jnp.int32)


def rotary_tables(count):
    half = HD // 2
    freq = jnp.exp(jnp.arange(half, dtype=f32) * (-2.0 * math.log(10000.0) / HD))
    angles = jnp.arange(count, dtype=jnp.int32).astype(f32)[:, None] * freq
    cosine, sine = jnp.cos(angles), jnp.sin(angles)
    return (
        jnp.concatenate([cosine, cosine], axis=1),
        jnp.concatenate([-sine, sine], axis=1),
    )


def on_device(
    tokens, cotangent, gain_first, gain_second, router_attn, router_mlp, query_w, key_w, value_w,
    output_w, gate_w, up_w, down_w, query_a, query_b, key_a, key_b, value_a, value_b, output_a,
    output_b, gate_a, gate_b, up_a, up_b, down_a, down_b, adapter_ids, attn_routes, mlp_routes,
):
    shards = lax.axis_size("shard")
    groups = lax.axis_size("dp")
    shard_at = lax.axis_index("shard")
    group_at = lax.axis_index("dp")
    rows = tokens.shape[0]
    seq = rows * shards
    cap_mlp = rows // 4 + rows // 16
    slices = groups // EXPERTS
    ff = gate_w.shape[1]
    width = key_w.shape[1]
    block = D // (groups * shards)
    own = groups * block
    adapter = adapter_ids[group_at]
    expert = group_at // slices

    x = tokens.astype(f32)
    normed = (x * inverse_rms(x) * gain_first.astype(f32)).astype(bf16)
    split = (D // LOW * 9 // 16) * LOW
    places = lax.rem(shard_at + shards - jnp.arange(shards, dtype=jnp.int32), shards)

    def shifted(part, step):
        pairs = [(i, (i + step) % shards) for i in range(shards)]
        return lax.ppermute(part, "shard", pairs) if step else part

    def gathered(left, right):
        return [lax.all_gather(left, "shard", axis=0, tiled=True)] + [
            shifted(right, step) for step in range(shards)
        ]

    xn_parts = gathered(normed[:, :split], normed[:, split:])

    mcol = slot_places(mlp_routes, EXPERTS, cap_mlp)
    mrow = mcol.T
    cosf, sinf = rotary_tables(seq)

    def ranks_first(factor):
        return jnp.swapaxes(factor, -1, -2)

    def of_adapter(factor, axis):
        return lax.dynamic_index_in_dim(factor, adapter, axis, keepdims=False)

    def pad_rows(parts, count=LOW):
        have = sum(p.shape[0] for p in parts)
        fill = jnp.zeros((count - have, parts[0].shape[1]), bf16)
        return jnp.concatenate(list(parts) + [fill], axis=0)

    aq = of_adapter(ranks_first(query_a), 1).reshape(LOW, D)
    amisc = pad_rows(
        [of_adapter(ranks_first(key_a), 0), of_adapter(ranks_first(value_a), 0), router_attn.T]
    )
    bcat = of_adapter(query_b, 1).reshape(LOW, width)
    key_second, value_second = of_adapter(key_b, 0), of_adapter(value_b, 0)
    kb = pad_rows([key_second])
    vb = pad_rows([jnp.zeros_like(value_second), value_second])
    oa = of_adapter(ranks_first(output_a), 1).reshape(LOW, width)
    ob = of_adapter(output_b, 1).reshape(LOW, D)
    router = pad_rows([router_mlp.T], 2 * EXPERTS)
    router_first = pad_rows([router_attn.T], 2 * ATT_EXPERTS)
    gain1, gain2 = gain_first.reshape(1, D), gain_second.reshape(1, D)

    def of_expert(factor):
        return lax.dynamic_index_in_dim(factor, expert, 0, keepdims=False).reshape(LOW, D)

    gate_first = of_expert(ranks_first(gate_a))
    up_first = of_expert(ranks_first(up_a))
    down_second = of_expert(down_b)
    gate_table = gate_b.reshape(LOW, ff)
    up_table = up_b.reshape(LOW, ff)
    down_table = ranks_first(down_a).reshape(LOW, ff)
    expert_rows = groups * cap_mlp
    source_adapter = jnp.repeat(adapter_ids, cap_mlp)
    mask = (
        source_adapter[:, None] == (jnp.arange(LOW, dtype=jnp.int32) // RANK)[None, :]
    ).astype(bf16)

    experts = (ATT_EXPERTS,)
    batch = 2
    batches = (ATT_EXPERTS // batch,)
    def to_experts(sent):
        wide = sent.shape[1]
        sent = jnp.repeat(sent.reshape(EXPERTS, cap_mlp, wide), slices, axis=0)
        got = lax.all_to_all(sent, "dp", split_axis=0, concat_axis=0, tiled=True)
        return got.reshape(expert_rows, wide)

    sent_rows = EXPERTS * cap_mlp
    picked = (mrow[0][None, :] == iota((sent_rows, rows), 0)) | (
        mrow[1][None, :] == iota((sent_rows, rows), 0)
    )
    grads_in = to_experts(nn(picked.astype(bf16), cotangent).astype(bf16))
    own_rows = lambda array: lax.dynamic_slice_in_dim(array, shard_at * rows, rows, 0)
    routes_own = own_rows(attn_routes)
    owner_places = jnp.concatenate([places, jnp.full((1,), block, jnp.int32)])
    early_made = (router, router_first, gain1, gain2, mask, mrow, mcol, routes_own)
    early_made += (gate_first, up_first, down_second, owner_places)
    early_made, xn_parts, grads_in = lax.optimization_barrier((early_made, xn_parts, grads_in))
    router, router_first, gain1, gain2, mask, mrow, mcol, routes_own, *firsts = early_made
    gate_first, up_first, down_second, owner_places = firsts

    column_parts = 4
    width_d = D // column_parts
    steps_attn = ATT_EXPERTS // 2 + column_parts
    late = lambda e: jnp.maximum(e - ATT_EXPERTS // 2, 0)
    column_block = pl.BlockSpec((LOW, width_d), lambda e: (0, late(e)))
    out_block = pl.BlockSpec((seq, width_d), lambda e: (0, late(e)))
    key_block = pl.BlockSpec((width_d, width), lambda e: (late(e), 0))
    far = pl.BlockSpec(memory_space=pl.ANY)
    project_flops = 4 * ATT_EXPERTS * seq * D * width
    weight_bytes = 4 * ATT_EXPERTS * D * width
    pair, row = ((2 * seq, width), bf16), ((seq, width), bf16)
    narrow, stat = ((seq, LOW), bf16), ((2 * seq, LOW), f32)
    saved = [pair, row, row, ((seq, LOW), f32), narrow, narrow, pair, stat]

    attn_part, low_part, q, k, v, ga, low, misc, o, lse = call(
        lambda *refs: attention_kernel(shards, *refs),
        (steps_attn,),
        [pl.BlockSpec(memory_space=pltpu.SMEM)]
        + [whole()] * (1 + shards)
        + [
            far,
            far,
            column_block,
            far,
            far,
        ]
        + [whole()] * 9,
        [out_block, whole()] + [far] * 8,
        [sds((seq, D), bf16), sds(*narrow)] + [sds(*shape) for shape in saved],
        [pltpu.VMEM(*shape) for shape in saved]
        + [
            pltpu.VMEM((2 * seq, width), f32),
            pltpu.VMEM(*pair),
            pltpu.VMEM((seq, ATT_EXPERTS * width), bf16),
            pltpu.VMEM((D, width), bf16),
            pltpu.VMEM((D, width), bf16),
            pltpu.SemaphoreType.DMA((2,)),
            pltpu.SemaphoreType.DMA((8,)),
            pltpu.VMEM((DEPTH, 2, D, width), bf16),
            pltpu.VMEM((DEPTH, ATT_EXPERTS, width, width_d), bf16),
            pltpu.SemaphoreType.DMA((DEPTH,)),
            pltpu.SemaphoreType.DMA((DEPTH,)),
            pltpu.VMEM((seq, D), bf16),
        ],
        project_flops,
        weight_bytes,
    )(places, *xn_parts, query_w, output_w, ob, key_w, value_w, aq, amisc, bcat, kb, vb, attn_routes, cosf, sinf, oa)

    attn = lax.psum_scatter(attn_part, "shard", scatter_dimension=0, tiled=True)

    rows_sent, gm, m = call(
        lambda *refs: dispatch_kernel(cap_mlp, *refs),
        (),
        [whole()] * 6,
        [whole()] * 3,
        [
            sds((sent_rows, D + LOW), bf16),
            sds((rows, LOW), f32),
            sds((rows, D), bf16),
        ],
        [],
        6 * sent_rows * rows * D,
        8 * sent_rows * D,
    )(attn, tokens, gain2, router, mrow, mcol)

    def from_experts(made):
        got = lax.all_to_all(
            made.reshape(groups, cap_mlp, D + LOW), "dp", split_axis=0, concat_axis=0, tiled=True
        )
        if slices > 1:
            parts = got.reshape(EXPERTS, slices, cap_mlp, D + LOW).astype(f32)
            got = jnp.sum(parts, axis=1).astype(bf16)
        return got.reshape(sent_rows, D + LOW)

    def by_column_owner(part):
        split = part.reshape(rows, groups, shards, block)
        return split.transpose(2, 0, 1, 3).reshape(shards, rows, own)

    columns_sent = jnp.concatenate([by_column_owner(m), by_column_owner(cotangent)], axis=2)
    low_lanes = low_part.reshape(shards, rows, LOW).transpose(1, 0, 2).reshape(rows, shards * LOW)
    arrived = []
    for step in range(shards):
        piece = lax.dynamic_index_in_dim(
            columns_sent, lax.rem(shard_at + step, shards), 0, keepdims=False
        )
        piece = jnp.concatenate([piece, low_lanes], axis=1)
        arrived.append(shifted(piece, step))

    rows_in = to_experts(rows_sent)

    steps = 11
    fb = ff // steps
    table = pl.BlockSpec((LOW, fb), lambda f: (0, f))
    kept = pl.BlockSpec((expert_rows, fb), lambda f: (0, f))
    weight_flops = 2 * expert_rows * D * ff
    weight_moved = 2 * D * ff
    low_shape = sds((expert_rows, LOW), bf16)
    wide_shape = sds((expert_rows, ff), bf16)
    out_shape = sds((expert_rows, D + LOW), bf16)

    g, u, lg, lu = call(
        expert_up_kernel,
        (steps,),
        [whole()] * 4 + [far, far, table, table],
        [kept, kept, whole(), whole()],
        [wide_shape, wide_shape, low_shape, low_shape],
        [
            pltpu.VMEM((DEPTH, D, fb), bf16),
            pltpu.VMEM((DEPTH, D, fb), bf16),
            pltpu.SemaphoreType.DMA((2, DEPTH)),
        ],
        2 * weight_flops,
        2 * weight_moved,
    )(rows_in, mask, gate_first, up_first, gate_w, up_w, gate_table, up_table)

    g, ga_own, *arrived = lax.optimization_barrier((g, own_rows(ga), *arrived))
    arrived = jnp.concatenate(arrived, axis=0)
    mlp_columns = arrived[:, : 2 * own]
    out_lows = jnp.sum(
        arrived[:, 2 * own :].reshape(shards, rows, shards, LOW).astype(f32), axis=0
    )
    out_lows = out_lows.astype(bf16).transpose(1, 0, 2).reshape(seq, LOW)

    each = ff // shards
    head = (each // LOW * 2 // 3) * LOW
    spans = [head, each - head] if each % LOW == 0 else [each]
    low_sum = pltpu.VMEM((expert_rows, LOW), f32)
    low_turned = pltpu.VMEM((LOW, expert_rows), bf16)
    ze, dg, du, dlg, dlu, *tables = call(
        expert_down_kernel,
        (steps,),
        [whole()] * 6 + [kept, kept, far, table, table, table],
        [whole(), kept, kept, whole(), whole()] + [whole() for _ in spans],
        [out_shape, wide_shape, wide_shape, low_shape, low_shape]
        + [sds((shards, 3 * LOW, span), bf16) for span in spans],
        [pltpu.VMEM((expert_rows, D), bf16)]
        + [pltpu.VMEM((expert_rows, D), f32), low_sum, low_sum, low_sum]
        + [pltpu.VMEM((expert_rows, LOW), bf16)]
        + [low_turned] * 3
        + [
            pltpu.VMEM((3 * LOW, ff), bf16),
            pltpu.VMEM((DEPTH, fb, D), bf16),
            pltpu.SemaphoreType.DMA((DEPTH,)),
        ],
        2 * weight_flops,
        weight_moved,
    )(grads_in, rows_in, mask, down_second, lg, lu, g, u, down_w, gate_table, up_table, down_table)

    ze_back = from_experts(ze)

    def table_sum(part):
        part = part.reshape(-1, part.shape[-1])
        return lax.psum_scatter(part, "shard", scatter_dimension=0, tiled=True)

    head_tables = table_sum(tables[0])

    parts = 4
    db = D // parts
    loads = ff // (11 * LOW) if ff % (11 * LOW) == 0 else 1
    low_block = pl.BlockSpec((LOW, db), lambda n: (0, n))
    dm = call(
        expert_rows_kernel,
        (parts,),
        [far, far, whole(), whole(), far, far, low_block, low_block],
        whole(),
        out_shape,
        [
            pltpu.VMEM((expert_rows, ff), bf16),
            pltpu.VMEM((expert_rows, ff), bf16),
            pltpu.VMEM((DEPTH, db, ff), bf16),
            pltpu.VMEM((DEPTH, db, ff), bf16),
            pltpu.SemaphoreType.DMA((2, loads)),
            pltpu.SemaphoreType.DMA((2, DEPTH)),
        ],
        2 * weight_flops,
        2 * weight_moved,
    )(dg, du, dlg, dlu, gate_w, up_w, gate_first, up_first)

    dm_back = from_experts(dm)

    layer_out, dlm, low_down = call(
        lambda *refs: combine_kernel(cap_mlp, *refs),
        (),
        [whole()] * 6,
        [whole()] * 3,
        [sds((rows, D), bf16), sds((rows, LOW), bf16), sds((rows, LOW), f32)],
        [],
        4 * sent_rows * rows * D,
        4 * sent_rows * D,
    )(ze_back, attn, tokens, cotangent, gm, mcol)

    dm_back = after(dm_back, head_tables)
    dh1, da_left, da_right = call(
        hidden_grad_kernel,
        (),
        [whole()] * 10,
        [whole()] * 3,
        [
            sds((rows, D), f32),
            sds((rows, split), bf16),
            sds((rows, D - split + LOW), bf16),
        ],
        [],
        2 * sent_rows * rows * D,
        4 * sent_rows * D,
    )(dm_back, dlm, low_down, attn, tokens, cotangent, gain2, router, mcol, mlp_routes)

    da_parts = gathered(da_left, da_right)
    xn_own = call(
        lambda *refs: own_columns_kernel(shards, *refs),
        (),
        [pl.BlockSpec(memory_space=pltpu.SMEM)] + [whole()] * (shards + 1),
        whole(),
        sds((seq, own), bf16),
        [pltpu.VMEM((seq, D), bf16), pltpu.VMEM((D, own), bf16)],
        0,
        0,
    )(owner_places, *after(xn_parts, da_left))
    *da_parts, xn_own = lax.optimization_barrier((*da_parts, xn_own))
    tables_sum = [head_tables] + [table_sum(after(part, *da_parts)) for part in tables[1:]]

    loaded = [((seq, LOW), f32), pair, pair, row, row, stat, narrow, narrow]
    loaded += [((seq, HD), f32), ((seq, HD), f32)]
    dx_part, lows, grad_oa, grad_qb, grad_kv = call(
        lambda *refs: attention_back_kernel(shards, *refs),
        (steps_attn,),
        [pl.BlockSpec(memory_space=pltpu.SMEM)]
        + [whole()] * (1 + shards)
        + [
            far,
            far,
            key_block,
            key_block,
            column_block,
            column_block,
        ]
        + [whole()] * 6
        + [far] * 10,
        [out_block] + [whole()] * 4,
        [
            sds((seq, D), bf16),
            sds((seq // 2 + 16, LOW), bf16),
            sds((LOW, width), bf16),
            sds((LOW, width), bf16),
            sds((2 * LOW, width), bf16),
        ],
        [pltpu.VMEM(*shape) for shape in loaded]
        + [
            pltpu.SemaphoreType.DMA((10,)),
            pltpu.VMEM((seq, LOW), f32),
            pltpu.VMEM((2 * seq, width), f32),
            pltpu.VMEM(*pair),
            pltpu.VMEM(*stat),
            pltpu.VMEM(*pair),
            pltpu.VMEM(*row),
            pltpu.VMEM(*row),
            pltpu.VMEM((seq, 2 * LOW), bf16),
            pltpu.VMEM((seq, HD), f32),
            pltpu.VMEM((seq, HD), f32),
            pltpu.VMEM((seq, ATT_EXPERTS * width), bf16),
            pltpu.VMEM((DEPTH, 2, width, D), bf16),
            pltpu.VMEM((DEPTH, ATT_EXPERTS, width_d, width), bf16),
            pltpu.SemaphoreType.DMA((DEPTH,)),
            pltpu.SemaphoreType.DMA((DEPTH,)),
            pltpu.VMEM((seq, D), bf16),
        ],
        project_flops,
        weight_bytes,
    )(places, *da_parts, output_w, query_w, key_w, value_w, aq, amisc, bcat, kb, vb, oa, ob, attn_routes, ga, o, q, k, v, lse, low, misc, cosf, sinf)

    held = (dx_part, lows, grad_oa, grad_qb, grad_kv, *da_parts, *tables_sum)
    dx_part, lows, grad_oa, grad_qb, grad_kv, *held = lax.optimization_barrier(held)
    da_parts, tables_sum = held[: shards + 1], held[shards + 1 :]
    lows_parts = [lows] + [shifted(lows, step) for step in range(1, shards)]
    lows_parts[1], *da_parts = lax.optimization_barrier((lows_parts[1], *da_parts))
    factors, grad_ob_own = call(
        lambda *refs: owner_kernel(shards, *refs),
        (),
        [pl.BlockSpec(memory_space=pltpu.SMEM)] + [whole()] * (shards + 3),
        [whole()] * 2,
        [sds((3 * LOW, own), bf16), sds((LOW, own), bf16)],
        [
            pltpu.VMEM((seq, own), bf16),
            pltpu.VMEM((seq, D), bf16),
            pltpu.VMEM((D, own), bf16),
        ],
        0,
        0,
    )(owner_places, *da_parts, out_lows, mlp_columns)
    lows_sum = sum(part.astype(f32) for part in lows_parts)
    half = LOW // 2
    lows_all = jnp.concatenate([lows_sum[: seq // 2, :half], lows_sum[: seq // 2, half:]], axis=0)
    lows_all = lows_all.astype(bf16)
    slopes = lows_sum[seq // 2 : seq // 2 + 2 * (seq // CHUNK)].reshape(2, seq).T
    dx = lax.psum_scatter(dx_part, "shard", scatter_dimension=0, tiled=True)

    input_grad = call(
        input_grad_kernel,
        (),
        [whole()] * 8,
        whole(),
        sds((rows, D), f32),
        [],
        2 * rows * LOW * D,
        24 * rows * D,
    )(dx, own_rows(slopes), ga_own, tokens, gain1, router_first, dh1, routes_own)

    lane = jnp.arange(LOW, dtype=jnp.int32)
    dense = jnp.zeros((seq, LOW), f32)
    for j in range(2):
        spread = (iota((half, LOW), 0) == (lane % RANK + j * RANK)[None, :]).astype(bf16)
        chosen = attn_routes[:, j : j + 1] == (lane // RANK)[None, :]
        dense = dense + jnp.where(chosen, nn(lows_all, spread), 0.0)
    grad_qa_own = tn(dense.astype(bf16), xn_own)
    grad_kva_own = tn(lows_all[:, 2 * RANK : 4 * RANK], xn_own)

    def to_owner_columns(part):
        return part.reshape(-1, groups, block).transpose(1, 0, 2).reshape(groups, -1)

    def to_owner_ranks(part):
        parts = part.reshape(-1, groups, RANK // groups, width)
        return parts.transpose(1, 0, 2, 3).reshape(groups, -1)

    sending = [
        to_owner_columns(grad_qa_own.astype(bf16)),
        to_owner_columns(grad_ob_own),
        to_owner_columns(grad_kva_own.astype(bf16)),
        to_owner_ranks(grad_qb),
        to_owner_ranks(grad_oa),
        to_owner_ranks(jnp.concatenate([grad_kv[:RANK], grad_kv[LOW + RANK : LOW + 2 * RANK]])),
        to_owner_columns(factors),
    ]
    sizes = [piece.shape[1] for piece in sending]
    sent = jnp.concatenate(sending, axis=1).reshape(groups, -1, LOW)
    got = lax.all_to_all(sent, "dp", split_axis=0, concat_axis=0, tiled=True)
    got = got.reshape(groups, -1).astype(f32)
    pick_source = (adapter_ids[:, None] == jnp.arange(ADAPTERS, dtype=jnp.int32)[None, :]).astype(
        f32
    )
    placed_sums = jnp.einsum("sa,sn->an", pick_source, got, precision=precise)
    parts = []
    start = 0
    for size in sizes:
        parts.append(placed_sums[:, start : start + size])
        start += size
    ranks_own = RANK // groups

    def columns_out(part, count):
        return part.reshape(ADAPTERS, count, RANK, block)

    def ranks_out(part, count):
        return part.reshape(ADAPTERS, count, ranks_own, width)

    query_a_sum = columns_out(parts[0], ATT_EXPERTS).transpose(1, 0, 3, 2)
    output_b_sum = columns_out(parts[1], ATT_EXPERTS).transpose(1, 0, 2, 3)
    kv_a_sum = columns_out(parts[2], 2).transpose(1, 0, 3, 2)
    query_b_sum = ranks_out(parts[3], ATT_EXPERTS).transpose(1, 0, 2, 3)
    output_a_sum = ranks_out(parts[4], ATT_EXPERTS).transpose(1, 0, 3, 2)
    kv_b_sum = ranks_out(parts[5], 2).transpose(1, 0, 2, 3)
    factor_sum = columns_out(parts[6], 3 * EXPERTS).transpose(1, 0, 2, 3)
    gate_a_sum = factor_sum[:EXPERTS].transpose(0, 1, 3, 2)
    up_a_sum = factor_sum[EXPERTS : 2 * EXPERTS].transpose(0, 1, 3, 2)
    down_b_sum = factor_sum[2 * EXPERTS :]

    joined = jnp.concatenate(tables_sum, axis=1) if len(tables_sum) > 1 else tables_sum[0]
    joined = joined.astype(f32).reshape(3, ADAPTERS, RANK, each)

    return (
        layer_out,
        input_grad,
        query_a_sum,
        query_b_sum,
        kv_a_sum[0],
        kv_b_sum[0],
        kv_a_sum[1],
        kv_b_sum[1],
        output_a_sum,
        output_b_sum,
        gate_a_sum,
        joined[0],
        up_a_sum,
        joined[1],
        ranks_first(joined[2]),
        down_b_sum,
    )


def solution(mesh):
    placed = (
        P(("dp", "shard"), None),
        P(("dp", "shard"), None),
        P(),
        P(),
        P(),
        P(),
        P(None, None, "shard"),
        P(None, "shard"),
        P(None, "shard"),
        P(None, "shard", None),
        P(None, "dp"),
        P(None, "dp"),
        P("dp", None),
        P(),
        P(None, None, None, "shard"),
        P(),
        P(None, None, "shard"),
        P(),
        P(None, None, "shard"),
        P(None, None, "shard", None),
        P(),
        P(),
        P(None, None, "dp"),
        P(),
        P(None, None, "dp"),
        P(None, "dp", None),
        P(),
        P(),
        P("dp", None),
        P(("dp", "shard"), None),
    )
    return jax.shard_map(
        on_device,
        mesh=mesh,
        in_specs=placed,
        out_specs=(
            P(("dp", "shard"), None),
            P(("dp", "shard"), None),
            P(None, None, ("dp", "shard"), None),
            P(None, None, "dp", "shard"),
            P(None, ("dp", "shard"), None),
            P(None, "dp", "shard"),
            P(None, ("dp", "shard"), None),
            P(None, "dp", "shard"),
            P(None, None, "shard", "dp"),
            P(None, None, None, ("dp", "shard")),
            P(None, None, ("dp", "shard"), None),
            P(None, None, ("dp", "shard")),
            P(None, None, ("dp", "shard"), None),
            P(None, None, ("dp", "shard")),
            P(None, ("dp", "shard"), None),
            P(None, None, None, ("dp", "shard")),
        ),
        check_vma=False,
    )
```

```python
import math

import jax
import jax.numpy as jnp
from jax import lax
from jax.experimental import pallas as pl
from jax.experimental.pallas import tpu as pltpu
from jax.sharding import PartitionSpec as P

D = 2048
HD = 128
EXPERTS = 8
ATT_EXPERTS = 8
ADAPTERS = 8
RANK = 16
LOW = 128
CHUNK = 128
GATE_LANE = 64
ROUTE_LANE = 96
ROUTER_ROW = 32
DEPTH = 3


f32 = jnp.float32
bf16 = jnp.bfloat16
precise = lax.Precision.HIGHEST
eps = 1e-05
score_scale = HD ** (-0.5)


def nn(a, b):
    return lax.dot_general(a, b, (((1,), (0,)), ((), ())), preferred_element_type=f32)


def nt(a, b):
    return lax.dot_general(a, b, (((1,), (1,)), ((), ())), preferred_element_type=f32)


def tn(a, b):
    return lax.dot_general(a, b, (((0,), (0,)), ((), ())), preferred_element_type=f32)


def iota(shape, axis):
    return lax.broadcasted_iota(jnp.int32, shape, axis)


def ones_where(condition):
    return jnp.where(condition, 1.0, 0.0).astype(bf16)


def inverse_rms(values):
    return lax.rsqrt(jnp.mean(values * values, axis=-1, keepdims=True) + eps)


def norm_backward(values, inverse, gain_vector, grad_normed):
    weighted = gain_vector * grad_normed
    return inverse * weighted - values * (inverse * inverse * inverse) * jnp.mean(
        values * weighted, axis=-1, keepdims=True
    )


def softmax_pair(first, second):
    peak = jnp.maximum(first, second)
    one, two = jnp.exp(first - peak), jnp.exp(second - peak)
    total = one + two
    return one / total, two / total


def in_lane(column, lane, width=LOW):
    shape = (column.shape[0], width)
    return jnp.where(iota(shape, 1) == lane, column, 0.0)


def lane_of(values, lane):
    return jnp.sum(jnp.where(iota(values.shape, 1) == lane, values, 0.0), axis=1, keepdims=True)


def expert_lanes(dest, capacity, shape, group):
    lane = iota(shape, 1)
    low = (lane // group) * capacity
    return (dest >= low) & (dest < low + capacity)


def whole():
    return pl.BlockSpec(memory_space=pltpu.VMEM)


def sds(shape, dtype):
    return jax.ShapeDtypeStruct(shape, dtype)


def call(kernel, grid, in_specs, out_specs, out_shape, scratch, flops, moved, grant=60):
    return pl.pallas_call(
        kernel,
        grid=grid,
        in_specs=in_specs,
        out_specs=out_specs,
        out_shape=out_shape,
        scratch_shapes=scratch,
        compiler_params=pltpu.CompilerParams(
            vmem_limit_bytes=grant * 1024 * 1024,
            dimension_semantics=("arbitrary",) * len(grid) if grid else None,
        ),
        cost_estimate=pl.CostEstimate(
            flops=4 * flops, bytes_accessed=4 * moved, transcendentals=0
        ),
    )


def rope(values, cosine, sine):
    return values * cosine + pltpu.roll(values, HD // 2, 1) * sine


def unrope(values, cosine, sine):
    return values * cosine - pltpu.roll(values, HD // 2, 1) * sine


def routed(route, shape):
    return (iota(shape, 1) // RANK) == route


def select_add(total, parts, routes, expert):
    s = parts[0].shape[0]
    for k in range(2):
        route = routes[:, k : k + 1]
        chosen = jnp.where(route == expert + 1, parts[1], 0.0)
        total[k * s : (k + 1) * s, :] += jnp.where(route == expert, parts[0], chosen)


def weight_stream(n, count, fetch):
    def prime():
        for j in range(min(DEPTH - 1, count)):
            for copy in fetch(j, j):
                copy.start()

    def advance():
        later = n + DEPTH - 1

        @pl.when(later < count)
        def _():
            for copy in fetch(later, lax.rem(later, DEPTH)):
                copy.start()

        for copy in fetch(n, lax.rem(n, DEPTH)):
            copy.wait()

    return prime, advance


def block_at(n, width):
    return pl.ds(pl.multiple_of(n * width, LOW), width)


def copies(sources, targets, sems):
    return [
        pltpu.make_async_copy(source, target, sems.at[j])
        for j, (source, target) in enumerate(zip(sources, targets, strict=True))
    ]


def join_rows(places, left, parts, out):
    split, rows = left.shape[1], parts[0].shape[0]
    out[:, 0:split] = left[...]
    for j, part in enumerate(parts):
        at = pl.ds(pl.multiple_of(places[j] * rows, 16), rows)
        out[at, split:] = part[:, 0 : out.shape[1] - split]


def attention_kernel(shards, places, left, *refs):
    parts, refs = refs[:shards], refs[shards:]
    *refs, xn = refs

    @pl.when(pl.program_id(0) == 0)
    def _():
        join_rows(places, left, parts, xn)

    attention_steps(xn, *refs)


def attention_steps(
    xn, wq_far, wo_far, ob, wk_far, wv_far, aq, amisc, bcat, kb, vb, routes, cosf, sinf, oa,
    attn_out, out_low, q_far, k_far, v_far, ga_far, low_far, misc_far, o_far, lse_far,
    q, k, v, ga, low, misc, o, lse, qsum, og, chosen, wk, wv, load_sems, save_sems, wq, wo, wq_sems, wo_sems,
):
    step = pl.program_id(0)
    phase = ATT_EXPERTS // 2
    s, width = k.shape
    loads = copies((wk_far, wv_far), (wk, wv), load_sems)
    width_d = wo.shape[3]
    prime_q, next_q = weight_stream(
        step,
        phase,
        lambda n, slot: [
            pltpu.make_async_copy(
                wq_far.at[pl.ds(2 * n, 2)], wq.at[slot], wq_sems.at[slot]
            ),
        ],
    )
    prime_o, next_o = weight_stream(
        step - phase,
        D // width_d,
        lambda n, slot: [
            pltpu.make_async_copy(
                wo_far.at[:, :, block_at(n, width_d)], wo.at[slot], wo_sems.at[slot]
            ),
        ],
    )
    saves = copies(
        (q, k, v, ga, low, misc, o, lse),
        (q_far, k_far, v_far, ga_far, low_far, misc_far, o_far, lse_far),
        save_sems,
    )

    @pl.when(step == 0)
    def _():
        prime_q()
        for load in loads:
            load.start()
        x = xn[...]
        low[...] = nt(x, aq[...]).astype(bf16)
        scores = nt(x, amisc[...])
        misc[...] = scores.astype(bf16)
        lane = iota((s, LOW), 1) - ROUTER_ROW
        gates = [
            jnp.sum(jnp.where(lane == routes[:, j : j + 1], scores, 0.0), axis=1, keepdims=True)
            for j in range(2)
        ]
        one, two = softmax_pair(*gates)
        ga[...] = in_lane(one, 0) + in_lane(two, 1)
        for j in range(2):
            mine = routed(routes[:, j : j + 1], (s, LOW))
            part = jnp.where(mine, low[...], jnp.zeros((), bf16))
            qsum[j * s : (j + 1) * s, :] = nn(part, bcat[...])

    @pl.when(step < phase)
    def _():
        next_q()
        slot = lax.rem(step, DEPTH)
        parts = [nn(xn[...], wq[slot, j]) for j in range(2)]
        select_add(qsum, parts, routes, 2 * step)

    @pl.when(step == phase - 1)
    def _():
        prime_o()
        for load in loads:
            load.wait()
        x = xn[...]
        keys = nn(x, wk[...]) + nn(misc[...], kb[...])
        for h in range(width // HD):
            hs = slice(h * HD, (h + 1) * HD)
            k[:, hs] = rope(keys[:, hs], cosf[...], sinf[...]).astype(bf16)
            for j in range(2):
                at = slice(j * s, (j + 1) * s)
                q[at, hs] = rope(qsum[at, hs], cosf[...], sinf[...]).astype(bf16)
        v[...] = (nn(x, wv[...]) + nn(misc[...], vb[...])).astype(bf16)
        attend(q, k, v, ga, o, og, lse)
        for save in saves:
            save.start()
        total = jnp.zeros((s, LOW), f32)
        for j in range(2):
            part = nt(og[j * s : (j + 1) * s, :], oa[...])
            total = total + jnp.where(routed(routes[:, j : j + 1], (s, LOW)), part, 0.0)
        out_low[...] = total.astype(bf16)
        spread_rows(og, routes, chosen)

    @pl.when(step >= phase)
    def _():
        next_o()
        weights = wo[lax.rem(step - phase, DEPTH)].reshape(chosen.shape[1], width_d)
        attn_out[...] = (nn(chosen[...], weights) + nn(out_low[...], ob[...])).astype(bf16)

    @pl.when(step == pl.num_programs(0) - 1)
    def _():
        for save in saves:
            save.wait()


def spread_rows(pair, routes, chosen):
    s, width = chosen.shape[0], pair.shape[1]
    for e in range(ATT_EXPERTS):
        chosen[:, e * width : (e + 1) * width] = of_expert_rows(pair, routes, e, s)


def causal(i, shape):
    row = (iota(shape, 0) & (CHUNK - 1)) + i * CHUNK
    return iota(shape, 1) <= row


def attend(q, k, v, ga, o_out, og_out, lse_out):
    s, width = k.shape
    for i in range(s // CHUNK):
        end = (i + 1) * CHUNK
        first, second = slice(i * CHUNK, end), slice(s + i * CHUNK, s + end)
        gates = [ga[first, 0:1], ga[first, 1:2]]
        log_totals = jnp.zeros((2 * CHUNK, LOW), f32)
        for h in range(width // HD):
            hs = slice(h * HD, (h + 1) * HD)
            queries = jnp.concatenate([q[first, hs], q[second, hs]], axis=0)
            scores = nt(queries, k[0:end, hs]) * score_scale
            scores = jnp.where(causal(i, scores.shape), scores, -1e30)
            peak = jnp.max(scores, axis=1, keepdims=True)
            weights = jnp.exp(scores - peak)
            total = jnp.sum(weights, axis=1, keepdims=True)
            mixed = nn(weights.astype(bf16), v[0:end, hs]) / total
            o_out[first, hs] = mixed[:CHUNK].astype(bf16)
            o_out[second, hs] = mixed[CHUNK:].astype(bf16)
            og_out[first, hs] = (mixed[:CHUNK] * gates[0]).astype(bf16)
            og_out[second, hs] = (mixed[CHUNK:] * gates[1]).astype(bf16)
            log_totals = log_totals + in_lane(peak + jnp.log(total), h)
        lse_out[first, :] = log_totals[:CHUNK]
        lse_out[second, :] = log_totals[CHUNK:]


def of_expert_rows(rows, routes, expert, s):
    return rows[0:s, :] * ones_where(routes[:, 0:1] == expert) + rows[s : 2 * s, :] * ones_where(
        routes[:, 1:2] == expert
    )


def second_norm(attn, tokens, gain):
    hidden = tokens[...].astype(f32) + attn[...].astype(f32)
    inverse = inverse_rms(hidden)
    return hidden, inverse, gain[...].astype(f32)


def dispatch_kernel(cap, attn, tokens, gain, router, mrow, mcol, rows_out, gm_out, m_out):
    hidden, inverse, scale = second_norm(attn, tokens, gain)
    m = (hidden * inverse * scale).astype(bf16)
    m_out[...] = m
    logits = nt(m, router[...])
    gates = softmax_pair(
        *[
            jnp.sum(
                jnp.where(
                    expert_lanes(mcol[:, k : k + 1], cap, logits.shape, 1),
                    logits,
                    0.0,
                ),
                axis=1,
                keepdims=True,
            )
            for k in range(2)
        ]
    )
    gm_out[...] = in_lane(gates[0], 0) + in_lane(gates[1], 1)
    slot = iota((rows_out.shape[0], mrow.shape[1]), 0)
    picks = [ones_where(mrow[k : k + 1, :] == slot) for k in range(2)]
    rows_out[:, 0:D] = nn(picks[0] + picks[1], m).astype(bf16)
    total = jnp.zeros((rows_out.shape[0], LOW), f32)
    for k in range(2):
        high = gates[k].astype(bf16).astype(f32)
        middle = (gates[k] - high).astype(bf16).astype(f32)
        both = in_lane(high, 0) + in_lane(middle, 1)
        total = total + nn(picks[k], both.astype(bf16))
    rows_out[:, D : D + LOW] = total.astype(bf16)


def fold(first_lane):
    row, column = iota((LOW, LOW), 0), iota((LOW, LOW), 1)
    return ones_where(column == (row & (RANK - 1)) + first_lane)


def spread(first_lane):
    row, column = iota((LOW, LOW), 0), iota((LOW, LOW), 1)
    return ones_where(row == (column & (RANK - 1)) + first_lane)


def combine_kernel(cap, ze, attn, tokens, cot, gm, mcol, layer_out, dlm_out, low_out):
    hidden = tokens[...].astype(f32) + attn[...].astype(f32)
    grad = cot[...].astype(f32)
    lane = iota((mcol.shape[0], ze.shape[0]), 1)
    gates, slopes, lows = [], [], []
    for k in range(2):
        gates.append(gm[:, k : k + 1])
        pick = ones_where(mcol[:, k : k + 1] == lane)
        expert_out = nn(pick, ze[:, 0:D])
        lows.append(gates[k] * nn(pick, ze[:, D : D + LOW]))
        slopes.append(jnp.sum(grad * expert_out, axis=1, keepdims=True))
        hidden = hidden + gates[k] * expert_out
    layer_out[...] = hidden.astype(bf16)
    low_out[...] = lows[0] + pltpu.roll(lows[1], 3 * RANK, 1)
    mean = gates[0] * slopes[0] + gates[1] * slopes[1]
    total = jnp.zeros(dlm_out.shape, f32)
    for k in range(2):
        mine = expert_lanes(mcol[:, k : k + 1], cap, dlm_out.shape, 1)
        total = total + jnp.where(mine, gates[k] * (slopes[k] - mean), 0.0)
    dlm_out[...] = total.astype(bf16)


def hidden_grad_kernel(
    rows, dlm, low, attn, tokens, cot, gain, router, mcol, routes, dh1_out, da_left, da_right
):
    hidden, inverse, scale = second_norm(attn, tokens, gain)
    lane = iota((mcol.shape[0], rows.shape[0]), 1)
    picks = [ones_where(mcol[:, k : k + 1] == lane) for k in range(2)]
    grad_m = nn(picks[0] + picks[1], rows[:, 0:D]) + nn(dlm[:, 0 : router.shape[0]], router[...])
    lows = [nn(pick, rows[:, D : D + LOW]) for pick in picks]
    total = low[...] + lows[0] + pltpu.roll(lows[1], 3 * RANK, 1)
    for k in range(2):
        total = total + in_lane(routes[:, k : k + 1].astype(f32), ROUTE_LANE + k)
    grad = cot[...].astype(f32) + norm_backward(hidden, inverse, scale, grad_m)
    dh1_out[...] = grad
    split = da_left.shape[1]
    da_left[...] = grad[:, :split].astype(bf16)
    da_right[:, 0 : D - split] = grad[:, split:].astype(bf16)
    da_right[:, D - split :] = total.astype(bf16)


def select_columns(places, shards, select):
    row, column = iota(select.shape, 0), iota(select.shape, 1)
    size = places[shards]
    group = lax.div(column, size)
    source = group * (size * shards) + places[0] * size + (column - group * size)
    select[...] = ones_where(row == source)


def own_columns_kernel(shards, places, *refs):
    parts, (out, gathered, select) = refs[: shards + 1], refs[shards + 1 :]
    select_columns(places, shards, select)
    join_rows(places, parts[0], parts[1:], gathered)
    out[...] = nn(gathered[...], select[...]).astype(bf16)


def owner_kernel(shards, places, *refs):
    da_refs, refs = refs[: shards + 1], refs[shards + 1 :]
    out_lows, columns, factors, grad_ob, da_own, gathered, select = refs
    own = da_own.shape[1]
    select_columns(places, shards, select)
    join_rows(places, da_refs[0], da_refs[1:], gathered)
    da_own[...] = nn(gathered[...], select[...]).astype(bf16)
    grad_ob[...] = tn(out_lows[...], da_own[...]).astype(bf16)
    right = D - da_refs[0].shape[1]
    lows = jnp.concatenate([ref[:, right : right + LOW] for ref in da_refs[1:]], axis=0)
    lane = (iota(lows.shape, 1) // RANK).astype(f32)
    mine = [lane_of(lows.astype(f32), ROUTE_LANE + k) == lane for k in range(2)]
    for part in range(3):
        dense = jnp.zeros(lows.shape, f32)
        for k in range(2):
            wide = nn(lows, spread((3 * k + part) * RANK))
            dense = dense + jnp.where(mine[k], wide, 0.0)
        at = slice(own, 2 * own) if part == 2 else slice(0, own)
        factors[part * LOW : (part + 1) * LOW, :] = tn(dense.astype(bf16), columns[:, at]).astype(
            bf16
        )


def identity():
    return ones_where(iota((LOW, LOW), 0) == iota((LOW, LOW), 1))


def expert_up_kernel(
    x, mask, ga, ua, gate_far, up_far, gate_b, up_b, g_out, u_out, lg_out, lu_out,
    gate_w, up_w, sems,
):
    x = x.at[:, 0:D]
    f = pl.program_id(0)
    width = gate_w.shape[2]
    prime, advance = weight_stream(
        f,
        gate_far.shape[1] // width,
        lambda n, slot: [
            pltpu.make_async_copy(
                gate_far.at[:, block_at(n, width)], gate_w.at[slot], sems.at[0, slot]
            ),
            pltpu.make_async_copy(
                up_far.at[:, block_at(n, width)], up_w.at[slot], sems.at[1, slot]
            ),
        ],
    )

    @pl.when(f == 0)
    def _():
        prime()
        lg_out[...] = nt(x[...], ga[...]).astype(bf16) * mask[...]
        lu_out[...] = nt(x[...], ua[...]).astype(bf16) * mask[...]

    advance()
    slot = lax.rem(f, DEPTH)
    g_out[...] = (nn(x[...], gate_w[slot]) + nn(lg_out[...], gate_b[...])).astype(bf16)
    u_out[...] = (nn(x[...], up_w[slot]) + nn(lu_out[...], up_b[...])).astype(bf16)


def expert_down_kernel(
    grads, x, mask, db, lg, lu, g, u, down_far, gate_b, up_b, down_a,
    ze_out, dg_out, du_out, dlg_out, dlu_out, *rest,
):
    *tables_out, dy, total, pd, dlg, dlu, dpd, lg_t, lu_t, dpd_t, tables, down, sems = rest
    f = pl.program_id(0)
    width = down.shape[1]
    prime, advance = weight_stream(
        f,
        down_far.shape[0] // width,
        lambda n, slot: [
            pltpu.make_async_copy(
                down_far.at[block_at(n, width), :], down.at[slot], sems.at[slot]
            ),
        ],
    )

    @pl.when(f == 0)
    def _():
        prime()
        gate = x[:, D : D + LOW].astype(f32)
        gate = lane_of(gate, 0) + lane_of(gate, 1)
        dy[...] = (gate * grads[...].astype(f32)).astype(bf16)
        dpd[...] = nt(dy[...], db[...]).astype(bf16) * mask[...]
        lg_t[...] = nt(identity(), lg[...]).astype(bf16)
        lu_t[...] = nt(identity(), lu[...]).astype(bf16)
        dpd_t[...] = nt(identity(), dpd[...]).astype(bf16)
        for sums in (total, pd, dlg, dlu):
            sums[...] = jnp.zeros_like(sums)

    advance()
    down_w = down.at[lax.rem(f, DEPTH)]
    dh = nt(dy[...], down_w[...]) + nn(dpd[...], down_a[...])
    gate = g[...].astype(f32)
    up = u[...].astype(f32)
    sig = jax.nn.sigmoid(gate)
    act = gate * sig
    hidden = (act * up).astype(bf16)
    dgate = (dh * up * (sig + act * (1.0 - sig))).astype(bf16)
    dup = (dh * act).astype(bf16)
    dg_out[...] = dgate
    du_out[...] = dup
    total[...] += nn(hidden, down_w[...])
    pd[...] += nt(hidden, down_a[...])
    dlg[...] += nt(dgate, gate_b[...])
    dlu[...] += nt(dup, up_b[...])
    at = pl.ds(pl.multiple_of(f * width, LOW), width)
    tables[0:LOW, at] = nn(lg_t[...], dgate).astype(bf16)
    tables[LOW : 2 * LOW, at] = nn(lu_t[...], dup).astype(bf16)
    tables[2 * LOW : 3 * LOW, at] = nn(dpd_t[...], hidden).astype(bf16)

    @pl.when(f == pl.num_programs(0) - 1)
    def _():
        low = pd[...].astype(bf16) * mask[...]
        ze_out[:, 0:D] = (total[...] + nn(low, db[...])).astype(bf16)
        ze_out[:, D : D + LOW] = nn(low, fold(2 * RANK)).astype(bf16)
        dlg_out[...] = dlg[...].astype(bf16) * mask[...]
        dlu_out[...] = dlu[...].astype(bf16) * mask[...]
        first = 0
        for out in tables_out:
            parts, _, size = out.shape
            for z in range(parts):
                start = z * (tables.shape[1] // parts) + first
                out[z] = tables[:, start : start + size]
            first += size


def expert_rows_kernel(
    dg_far, du_far, dlg, dlu, gate_far, up_far, ga, ua, dm_out,
    dg, du, gate_w, up_w, load_sems, sems,
):
    n = pl.program_id(0)
    width, depth = gate_w.shape[1:]
    span = depth // load_sems.shape[1]
    prime, advance = weight_stream(
        n,
        D // width,
        lambda at, slot: [
            pltpu.make_async_copy(
                gate_far.at[block_at(at, width), :], gate_w.at[slot], sems.at[0, slot]
            ),
            pltpu.make_async_copy(
                up_far.at[block_at(at, width), :], up_w.at[slot], sems.at[1, slot]
            ),
        ],
    )
    parts = [slice(j * span, (j + 1) * span) for j in range(load_sems.shape[1])]
    loads = [
        (
            pltpu.make_async_copy(dg_far.at[:, at], dg.at[:, at], load_sems.at[0, j]),
            pltpu.make_async_copy(du_far.at[:, at], du.at[:, at], load_sems.at[1, j]),
        )
        for j, at in enumerate(parts)
    ]
    slot = lax.rem(n, DEPTH)

    def give(total):
        total = total + nn(dlg[...], ga[...]) + nn(dlu[...], ua[...])
        dm_out[:, block_at(n, width)] = total.astype(bf16)

    @pl.when(n == 0)
    def _():
        for pair in loads[:1]:
            for load in pair:
                load.start()
        prime()
        for pair in loads[1:]:
            for load in pair:
                load.start()
        low = nn(dlg[...], fold(0)) + nn(dlu[...], fold(RANK))
        dm_out[:, D : D + LOW] = low.astype(bf16)

    advance()

    @pl.when(n == 0)
    def _():
        total = None
        for at, pair in zip(parts, loads, strict=True):
            for load in pair:
                load.wait()
            new = nt(dg[:, at], gate_w[slot, :, at]) + nt(du[:, at], up_w[slot, :, at])
            total = new if total is None else total + new
        give(total)

    @pl.when(n > 0)
    def _():
        give(nt(dg[...], gate_w[slot]) + nt(du[...], up_w[slot]))


def attention_back_kernel(shards, places, left, *refs):
    parts, refs = refs[:shards], refs[shards:]
    *refs, da = refs

    @pl.when(pl.program_id(0) == 0)
    def _():
        join_rows(places, left, parts, da)

    attention_back_steps(da, *refs)


def attention_back_steps(
    da, wo_far, wq_far, wk, wv, aq, amisc, bcat, kb, vb, oa, ob, routes,
    ga_far, o_far, q_far, k_far, v_far, lse_far, low_far, misc_far, cosf_far, sinf_far,
    dx_out, lows_out, grad_oa_out, grad_qb_out, grad_kv_out,
    ga, o, q, k, v, lse, low, misc, cosf, sinf, sems,
    dzl, dosum, do, stats, dq, dk, dv, lows_dense, dk_sum, dv_sum, chosen, wo, wq, wo_sems, wq_sems,
):
    step = pl.program_id(0)
    phase = ATT_EXPERTS // 2
    s, width = k.shape
    width_d = wq.shape[2]
    prime_o, next_o = weight_stream(
        step,
        phase,
        lambda n, slot: [
            pltpu.make_async_copy(
                wo_far.at[pl.ds(2 * n, 2)], wo.at[slot], wo_sems.at[slot]
            ),
        ],
    )
    prime_q, next_q = weight_stream(
        step - phase,
        D // width_d,
        lambda n, slot: [
            pltpu.make_async_copy(
                wq_far.at[:, block_at(n, width_d), :], wq.at[slot], wq_sems.at[slot]
            ),
        ],
    )
    loads = copies(
        (ga_far, o_far, q_far, k_far, v_far, lse_far, low_far, misc_far, cosf_far, sinf_far),
        (ga, o, q, k, v, lse, low, misc, cosf, sinf),
        sems,
    )

    @pl.when(step == 0)
    def _():
        prime_o()
        for load in loads:
            load.start()
        dzl[...] = nt(da[...], ob[...])
        for j in range(2):
            mine = routed(routes[:, j : j + 1], (s, LOW))
            part = jnp.where(mine, dzl[...], 0.0).astype(bf16)
            dosum[j * s : (j + 1) * s, :] = nn(part, oa[...])

    @pl.when(step < phase)
    def _():
        next_o()
        slot = lax.rem(step, DEPTH)
        parts = [nt(da[...], wo[slot, j]) for j in range(2)]
        select_add(dosum, parts, routes, 2 * step)

    @pl.when(step == phase - 1)
    def _():
        prime_q()
        for load in loads:
            load.wait()
        out_back(routes, ga, o, dzl, dosum, do, stats, grad_oa_out)
        attend_back(
            q, k, v, do, lse, stats, cosf, sinf, bcat, kb, vb, low, misc, routes,
            dq, dk, dv, lows_out, lows_dense, grad_qb_out, grad_kv_out, dk_sum, dv_sum,
        )
        spread_rows(dq, routes, chosen)

    @pl.when(step >= phase)
    def _():
        next_q()
        slot = lax.rem(step - phase, DEPTH)
        total = (
            nn(lows_dense[:, 0:LOW], aq[...])
            + nn(lows_dense[:, LOW : 2 * LOW], amisc[...])
            + nt(dk[...], wk[...])
            + nt(dv[...], wv[...])
        )
        for e in range(ATT_EXPERTS):
            total = total + nt(chosen[:, e * width : (e + 1) * width], wq[slot, e])
        dx_out[...] = total.astype(bf16)


def out_back(routes, ga, o, dzl, dosum, do_out, stats_out, grad_oa_out):
    s, width = o.shape[0] // 2, o.shape[1]
    grad_oa = jnp.zeros((LOW, width), f32)
    for k in range(2):
        at = slice(k * s, (k + 1) * s)
        gate = ga[:, k : k + 1]
        mine = routed(routes[:, k : k + 1], (s, LOW))
        low = jnp.where(mine, gate * dzl[...], 0.0).astype(bf16)
        grad_oa = grad_oa + tn(low, o[at, :])
        stats = jnp.zeros((s, LOW), f32)
        slope = jnp.zeros((s, 1), f32)
        for h in range(width // HD):
            hs = slice(h * HD, (h + 1) * HD)
            before = dosum[at, hs]
            part = jnp.sum(o[at, hs].astype(f32) * before, axis=1, keepdims=True)
            slope = slope + part
            stats = stats + in_lane(gate * part, h)
            do_out[at, hs] = (gate * before).astype(bf16)
        stats_out[at, :] = stats + in_lane(slope, GATE_LANE)
    grad_oa_out[...] = grad_oa.astype(bf16)


def attend_back(
    q, k, v, do, lse, stats, cosf, sinf, bcat, kb, vb, low, misc, routes,
    dq_out, dk_out, dv_out, lows_out, misc_back_out, grad_qb_out, grad_kv_out, dk_sum, dv_sum,
):
    s, width = k.shape
    for h in range(width // HD):
        hs = slice(h * HD, (h + 1) * HD)
        dk_sum[...] = jnp.zeros_like(dk_sum)
        dv_sum[...] = jnp.zeros_like(dv_sum)
        for i in range(s // CHUNK):
            end = (i + 1) * CHUNK
            first, second = slice(i * CHUNK, end), slice(s + i * CHUNK, s + end)
            queries = jnp.concatenate([q[first, hs], q[second, hs]], axis=0)
            grads = jnp.concatenate([do[first, hs], do[second, hs]], axis=0)
            logs = jnp.concatenate([lse[first, h : h + 1], lse[second, h : h + 1]], axis=0)
            centre = jnp.concatenate([stats[first, h : h + 1], stats[second, h : h + 1]], axis=0)
            scores = nt(queries, k[0:end, hs]) * score_scale
            weights = jnp.where(causal(i, scores.shape), jnp.exp(scores - logs), 0.0)
            dscores = (weights * (nt(grads, v[0:end, hs]) - centre)).astype(bf16)
            dq = nn(dscores, k[0:end, hs]) * score_scale
            cosine, sine = cosf[first, :], sinf[first, :]
            dq_out[first, hs] = unrope(dq[:CHUNK], cosine, sine).astype(bf16)
            dq_out[second, hs] = unrope(dq[CHUNK:], cosine, sine).astype(bf16)
            dk_sum[0:end, :] += tn(dscores, queries)
            dv_sum[0:end, :] += tn(weights.astype(bf16), grads)
        dk_out[:, hs] = unrope(dk_sum[...] * score_scale, cosf[...], sinf[...]).astype(bf16)
        dv_out[:, hs] = dv_sum[...].astype(bf16)
    row, column = iota((LOW, LOW), 0), iota((LOW, LOW), 1)
    grad_qb = jnp.zeros((LOW, width), f32)
    chunks = s // CHUNK
    half = chunks // 2
    packed = [None] * half
    slopes = jnp.zeros((16, LOW), f32)
    line, at_lane = iota((16, LOW), 0), iota((16, LOW), 1) == GATE_LANE
    for i in range(chunks):
        rs = slice(i * CHUNK, (i + 1) * CHUNK)
        misc_back = (nt(dk_out[rs, :], kb[...]) + nt(dv_out[rs, :], vb[...])).astype(bf16)
        lows = nn(misc_back, ones_where((column == row + 2 * RANK) & (row < 2 * RANK)))
        dense = jnp.zeros((CHUNK, LOW), f32)
        for j in range(2):
            at = slice(j * s + i * CHUNK, j * s + (i + 1) * CHUNK)
            mine = routed(routes[rs, j : j + 1], (CHUNK, LOW))
            part = jnp.where(mine, nt(dq_out[at, :], bcat[...]), 0.0).astype(bf16)
            dense = dense + part.astype(f32)
            fold_pair = ones_where((column == (row & (RANK - 1)) + j * RANK) & (column < 2 * RANK))
            lows = lows + nn(part, fold_pair)
            mark = ones_where((line == j * chunks + i) & at_lane)
            slopes = slopes + nt(mark, stats[at, :].astype(bf16))
            grad_qb = grad_qb + tn(
                jnp.where(mine, low[rs, :], jnp.zeros((), bf16)), dq_out[at, :]
            )
        if i < half:
            packed[i] = lows
        else:
            together = packed[i - half] + pltpu.roll(lows, LOW // 2, 1)
            lows_out[(i - half) * CHUNK : (i - half + 1) * CHUNK, :] = together.astype(bf16)
        misc_back_out[rs, 0:LOW] = dense.astype(bf16)
        misc_back_out[rs, LOW : 2 * LOW] = misc_back
    lows_out[half * CHUNK : half * CHUNK + 16, :] = slopes.astype(bf16)
    grad_qb_out[...] = grad_qb.astype(bf16)
    grad_kv_out[0:LOW, :] = tn(misc[...], dk_out[...]).astype(bf16)
    grad_kv_out[LOW : 2 * LOW, :] = tn(misc[...], dv_out[...]).astype(bf16)


def input_grad_kernel(dx, slopes, ga, tokens, gain, router, dh1, routes, out):
    x = tokens[...].astype(f32)
    gates = [ga[:, k : k + 1] for k in range(2)]
    slope = [slopes[:, k : k + 1] for k in range(2)]
    mean = gates[0] * slope[0] + gates[1] * slope[1]
    total = jnp.zeros(ga.shape, f32)
    lane = iota(ga.shape, 1)
    for k in range(2):
        mine = lane == routes[:, k : k + 1]
        total = total + jnp.where(mine, gates[k] * (slope[k] - mean), 0.0)
    grad = dx[...].astype(f32) + nn(total[:, 0 : router.shape[0]].astype(bf16), router[...])
    out[...] = dh1[...] + norm_backward(x, inverse_rms(x), gain[...].astype(f32), grad)


def after(value, *earlier):
    return lax.optimization_barrier((value, *earlier))[0]


def slot_places(routes, expert_count, capacity):
    choose = (routes[:, :, None] == jnp.arange(expert_count, dtype=jnp.int32)).astype(bf16)
    member = choose[:, 0] + choose[:, 1]
    count = routes.shape[0]
    before = (iota((count, count), 1) < iota((count, count), 0)).astype(bf16)
    slots = nn(before, member)
    mine = jnp.sum(slots[:, None, :] * choose.astype(f32), axis=2)
    return routes * capacity + mine.astype(jnp.int32)


def rotary_tables(count):
    half = HD // 2
    freq = jnp.exp(jnp.arange(half, dtype=f32) * (-2.0 * math.log(10000.0) / HD))
    angles = jnp.arange(count, dtype=jnp.int32).astype(f32)[:, None] * freq
    cosine, sine = jnp.cos(angles), jnp.sin(angles)
    return (
        jnp.concatenate([cosine, cosine], axis=1),
        jnp.concatenate([-sine, sine], axis=1),
    )


def on_device(
    tokens, cotangent, gain_first, gain_second, router_attn, router_mlp, query_w, key_w, value_w,
    output_w, gate_w, up_w, down_w, query_a, query_b, key_a, key_b, value_a, value_b, output_a,
    output_b, gate_a, gate_b, up_a, up_b, down_a, down_b, adapter_ids, attn_routes, mlp_routes,
):
    shards = lax.axis_size("shard")
    groups = lax.axis_size("dp")
    shard_at = lax.axis_index("shard")
    group_at = lax.axis_index("dp")
    rows = tokens.shape[0]
    seq = rows * shards
    cap_mlp = rows // 4 + rows // 16
    slices = groups // EXPERTS
    ff = gate_w.shape[1]
    width = key_w.shape[1]
    block = D // (groups * shards)
    own = groups * block
    adapter = adapter_ids[group_at]
    expert = group_at // slices

    x = tokens.astype(f32)
    normed = (x * inverse_rms(x) * gain_first.astype(f32)).astype(bf16)
    split = (D // LOW * 9 // 16) * LOW
    places = lax.rem(shard_at + shards - jnp.arange(shards, dtype=jnp.int32), shards)

    def shifted(part, step):
        pairs = [(i, (i + step) % shards) for i in range(shards)]
        return lax.ppermute(part, "shard", pairs) if step else part

    def gathered(left, right):
        return [lax.all_gather(left, "shard", axis=0, tiled=True)] + [
            shifted(right, step) for step in range(shards)
        ]

    xn_parts = gathered(normed[:, :split], normed[:, split:])

    mcol = slot_places(mlp_routes, EXPERTS, cap_mlp)
    mrow = mcol.T
    cosf, sinf = rotary_tables(seq)

    def ranks_first(factor):
        return jnp.swapaxes(factor, -1, -2)

    def of_adapter(factor, axis):
        return lax.dynamic_index_in_dim(factor, adapter, axis, keepdims=False)

    def pad_rows(parts, count=LOW):
        have = sum(p.shape[0] for p in parts)
        fill = jnp.zeros((count - have, parts[0].shape[1]), bf16)
        return jnp.concatenate(list(parts) + [fill], axis=0)

    aq = of_adapter(ranks_first(query_a), 1).reshape(LOW, D)
    amisc = pad_rows(
        [of_adapter(ranks_first(key_a), 0), of_adapter(ranks_first(value_a), 0), router_attn.T]
    )
    bcat = of_adapter(query_b, 1).reshape(LOW, width)
    key_second, value_second = of_adapter(key_b, 0), of_adapter(value_b, 0)
    kb = pad_rows([key_second])
    vb = pad_rows([jnp.zeros_like(value_second), value_second])
    oa = of_adapter(ranks_first(output_a), 1).reshape(LOW, width)
    ob = of_adapter(output_b, 1).reshape(LOW, D)
    router = pad_rows([router_mlp.T], 2 * EXPERTS)
    router_first = pad_rows([router_attn.T], 2 * ATT_EXPERTS)
    gain1, gain2 = gain_first.reshape(1, D), gain_second.reshape(1, D)

    def of_expert(factor):
        return lax.dynamic_index_in_dim(factor, expert, 0, keepdims=False).reshape(LOW, D)

    gate_first = of_expert(ranks_first(gate_a))
    up_first = of_expert(ranks_first(up_a))
    down_second = of_expert(down_b)
    gate_table = gate_b.reshape(LOW, ff)
    up_table = up_b.reshape(LOW, ff)
    down_table = ranks_first(down_a).reshape(LOW, ff)
    expert_rows = groups * cap_mlp
    source_adapter = jnp.repeat(adapter_ids, cap_mlp)
    mask = (
        source_adapter[:, None] == (jnp.arange(LOW, dtype=jnp.int32) // RANK)[None, :]
    ).astype(bf16)

    experts = (ATT_EXPERTS,)
    batch = 2
    batches = (ATT_EXPERTS // batch,)
    def to_experts(sent):
        wide = sent.shape[1]
        sent = jnp.repeat(sent.reshape(EXPERTS, cap_mlp, wide), slices, axis=0)
        got = lax.all_to_all(sent, "dp", split_axis=0, concat_axis=0, tiled=True)
        return got.reshape(expert_rows, wide)

    sent_rows = EXPERTS * cap_mlp
    picked = (mrow[0][None, :] == iota((sent_rows, rows), 0)) | (
        mrow[1][None, :] == iota((sent_rows, rows), 0)
    )
    grads_in = to_experts(nn(picked.astype(bf16), cotangent).astype(bf16))
    own_rows = lambda array: lax.dynamic_slice_in_dim(array, shard_at * rows, rows, 0)
    routes_own = own_rows(attn_routes)
    owner_places = jnp.concatenate([places, jnp.full((1,), block, jnp.int32)])
    early_made = (router, router_first, gain1, gain2, mask, mrow, mcol, routes_own)
    early_made += (gate_first, up_first, down_second, owner_places)
    early_made, xn_parts, grads_in = lax.optimization_barrier((early_made, xn_parts, grads_in))
    router, router_first, gain1, gain2, mask, mrow, mcol, routes_own, *firsts = early_made
    gate_first, up_first, down_second, owner_places = firsts

    column_parts = 4
    width_d = D // column_parts
    steps_attn = ATT_EXPERTS // 2 + column_parts
    late = lambda e: jnp.maximum(e - ATT_EXPERTS // 2, 0)
    column_block = pl.BlockSpec((LOW, width_d), lambda e: (0, late(e)))
    out_block = pl.BlockSpec((seq, width_d), lambda e: (0, late(e)))
    key_block = pl.BlockSpec((width_d, width), lambda e: (late(e), 0))
    far = pl.BlockSpec(memory_space=pl.ANY)
    project_flops = 4 * ATT_EXPERTS * seq * D * width
    weight_bytes = 4 * ATT_EXPERTS * D * width
    pair, row = ((2 * seq, width), bf16), ((seq, width), bf16)
    narrow, stat = ((seq, LOW), bf16), ((2 * seq, LOW), f32)
    saved = [pair, row, row, ((seq, LOW), f32), narrow, narrow, pair, stat]

    attn_part, low_part, q, k, v, ga, low, misc, o, lse = call(
        lambda *refs: attention_kernel(shards, *refs),
        (steps_attn,),
        [pl.BlockSpec(memory_space=pltpu.SMEM)]
        + [whole()] * (1 + shards)
        + [
            far,
            far,
            column_block,
            far,
            far,
        ]
        + [whole()] * 9,
        [out_block, whole()] + [far] * 8,
        [sds((seq, D), bf16), sds(*narrow)] + [sds(*shape) for shape in saved],
        [pltpu.VMEM(*shape) for shape in saved]
        + [
            pltpu.VMEM((2 * seq, width), f32),
            pltpu.VMEM(*pair),
            pltpu.VMEM((seq, ATT_EXPERTS * width), bf16),
            pltpu.VMEM((D, width), bf16),
            pltpu.VMEM((D, width), bf16),
            pltpu.SemaphoreType.DMA((2,)),
            pltpu.SemaphoreType.DMA((8,)),
            pltpu.VMEM((DEPTH, 2, D, width), bf16),
            pltpu.VMEM((DEPTH, ATT_EXPERTS, width, width_d), bf16),
            pltpu.SemaphoreType.DMA((DEPTH,)),
            pltpu.SemaphoreType.DMA((DEPTH,)),
            pltpu.VMEM((seq, D), bf16),
        ],
        project_flops,
        weight_bytes,
    )(places, *xn_parts, query_w, output_w, ob, key_w, value_w, aq, amisc, bcat, kb, vb, attn_routes, cosf, sinf, oa)

    attn = lax.psum_scatter(attn_part, "shard", scatter_dimension=0, tiled=True)

    rows_sent, gm, m = call(
        lambda *refs: dispatch_kernel(cap_mlp, *refs),
        (),
        [whole()] * 6,
        [whole()] * 3,
        [
            sds((sent_rows, D + LOW), bf16),
            sds((rows, LOW), f32),
            sds((rows, D), bf16),
        ],
        [],
        6 * sent_rows * rows * D,
        8 * sent_rows * D,
    )(attn, tokens, gain2, router, mrow, mcol)

    def from_experts(made):
        got = lax.all_to_all(
            made.reshape(groups, cap_mlp, D + LOW), "dp", split_axis=0, concat_axis=0, tiled=True
        )
        if slices > 1:
            parts = got.reshape(EXPERTS, slices, cap_mlp, D + LOW).astype(f32)
            got = jnp.sum(parts, axis=1).astype(bf16)
        return got.reshape(sent_rows, D + LOW)

    def by_column_owner(part):
        split = part.reshape(rows, groups, shards, block)
        return split.transpose(2, 0, 1, 3).reshape(shards, rows, own)

    columns_sent = jnp.concatenate([by_column_owner(m), by_column_owner(cotangent)], axis=2)
    low_lanes = low_part.reshape(shards, rows, LOW).transpose(1, 0, 2).reshape(rows, shards * LOW)
    arrived = []
    for step in range(shards):
        piece = lax.dynamic_index_in_dim(
            columns_sent, lax.rem(shard_at + step, shards), 0, keepdims=False
        )
        piece = jnp.concatenate([piece, low_lanes], axis=1)
        arrived.append(shifted(piece, step))

    rows_in = to_experts(rows_sent)

    steps = 11
    fb = ff // steps
    table = pl.BlockSpec((LOW, fb), lambda f: (0, f))
    kept = pl.BlockSpec((expert_rows, fb), lambda f: (0, f))
    weight_flops = 2 * expert_rows * D * ff
    weight_moved = 2 * D * ff
    low_shape = sds((expert_rows, LOW), bf16)
    wide_shape = sds((expert_rows, ff), bf16)
    out_shape = sds((expert_rows, D + LOW), bf16)

    g, u, lg, lu = call(
        expert_up_kernel,
        (steps,),
        [whole()] * 4 + [far, far, table, table],
        [kept, kept, whole(), whole()],
        [wide_shape, wide_shape, low_shape, low_shape],
        [
            pltpu.VMEM((DEPTH, D, fb), bf16),
            pltpu.VMEM((DEPTH, D, fb), bf16),
            pltpu.SemaphoreType.DMA((2, DEPTH)),
        ],
        2 * weight_flops,
        2 * weight_moved,
    )(rows_in, mask, gate_first, up_first, gate_w, up_w, gate_table, up_table)

    g, ga_own, *arrived = lax.optimization_barrier((g, own_rows(ga), *arrived))
    arrived = jnp.concatenate(arrived, axis=0)
    mlp_columns = arrived[:, : 2 * own]
    out_lows = jnp.sum(
        arrived[:, 2 * own :].reshape(shards, rows, shards, LOW).astype(f32), axis=0
    )
    out_lows = out_lows.astype(bf16).transpose(1, 0, 2).reshape(seq, LOW)

    each = ff // shards
    head = (each // LOW * 2 // 3) * LOW
    spans = [head, each - head] if each % LOW == 0 else [each]
    low_sum = pltpu.VMEM((expert_rows, LOW), f32)
    low_turned = pltpu.VMEM((LOW, expert_rows), bf16)
    ze, dg, du, dlg, dlu, *tables = call(
        expert_down_kernel,
        (steps,),
        [whole()] * 6 + [kept, kept, far, table, table, table],
        [whole(), kept, kept, whole(), whole()] + [whole() for _ in spans],
        [out_shape, wide_shape, wide_shape, low_shape, low_shape]
        + [sds((shards, 3 * LOW, span), bf16) for span in spans],
        [pltpu.VMEM((expert_rows, D), bf16)]
        + [pltpu.VMEM((expert_rows, D), f32), low_sum, low_sum, low_sum]
        + [pltpu.VMEM((expert_rows, LOW), bf16)]
        + [low_turned] * 3
        + [
            pltpu.VMEM((3 * LOW, ff), bf16),
            pltpu.VMEM((DEPTH, fb, D), bf16),
            pltpu.SemaphoreType.DMA((DEPTH,)),
        ],
        2 * weight_flops,
        weight_moved,
    )(grads_in, rows_in, mask, down_second, lg, lu, g, u, down_w, gate_table, up_table, down_table)

    ze_back = from_experts(ze)

    def table_sum(part):
        part = part.reshape(-1, part.shape[-1])
        return lax.psum_scatter(part, "shard", scatter_dimension=0, tiled=True)

    head_tables = table_sum(tables[0])

    parts = 4
    db = D // parts
    loads = ff // (11 * LOW) if ff % (11 * LOW) == 0 else 1
    low_block = pl.BlockSpec((LOW, db), lambda n: (0, n))
    dm = call(
        expert_rows_kernel,
        (parts,),
        [far, far, whole(), whole(), far, far, low_block, low_block],
        whole(),
        out_shape,
        [
            pltpu.VMEM((expert_rows, ff), bf16),
            pltpu.VMEM((expert_rows, ff), bf16),
            pltpu.VMEM((DEPTH, db, ff), bf16),
            pltpu.VMEM((DEPTH, db, ff), bf16),
            pltpu.SemaphoreType.DMA((2, loads)),
            pltpu.SemaphoreType.DMA((2, DEPTH)),
        ],
        2 * weight_flops,
        2 * weight_moved,
    )(dg, du, dlg, dlu, gate_w, up_w, gate_first, up_first)

    dm_back = from_experts(dm)

    layer_out, dlm, low_down = call(
        lambda *refs: combine_kernel(cap_mlp, *refs),
        (),
        [whole()] * 6,
        [whole()] * 3,
        [sds((rows, D), bf16), sds((rows, LOW), bf16), sds((rows, LOW), f32)],
        [],
        4 * sent_rows * rows * D,
        4 * sent_rows * D,
    )(ze_back, attn, tokens, cotangent, gm, mcol)

    dm_back = after(dm_back, head_tables)
    dh1, da_left, da_right = call(
        hidden_grad_kernel,
        (),
        [whole()] * 10,
        [whole()] * 3,
        [
            sds((rows, D), f32),
            sds((rows, split), bf16),
            sds((rows, D - split + LOW), bf16),
        ],
        [],
        2 * sent_rows * rows * D,
        4 * sent_rows * D,
    )(dm_back, dlm, low_down, attn, tokens, cotangent, gain2, router, mcol, mlp_routes)

    da_parts = gathered(da_left, da_right)
    xn_own = call(
        lambda *refs: own_columns_kernel(shards, *refs),
        (),
        [pl.BlockSpec(memory_space=pltpu.SMEM)] + [whole()] * (shards + 1),
        whole(),
        sds((seq, own), bf16),
        [pltpu.VMEM((seq, D), bf16), pltpu.VMEM((D, own), bf16)],
        0,
        0,
    )(owner_places, *after(xn_parts, da_left))
    *da_parts, xn_own = lax.optimization_barrier((*da_parts, xn_own))
    tables_sum = [head_tables] + [table_sum(after(part, *da_parts)) for part in tables[1:]]

    loaded = [((seq, LOW), f32), pair, pair, row, row, stat, narrow, narrow]
    loaded += [((seq, HD), f32), ((seq, HD), f32)]
    dx_part, lows, grad_oa, grad_qb, grad_kv = call(
        lambda *refs: attention_back_kernel(shards, *refs),
        (steps_attn,),
        [pl.BlockSpec(memory_space=pltpu.SMEM)]
        + [whole()] * (1 + shards)
        + [
            far,
            far,
            key_block,
            key_block,
            column_block,
            column_block,
        ]
        + [whole()] * 6
        + [far] * 10,
        [out_block] + [whole()] * 4,
        [
            sds((seq, D), bf16),
            sds((seq // 2 + 16, LOW), bf16),
            sds((LOW, width), bf16),
            sds((LOW, width), bf16),
            sds((2 * LOW, width), bf16),
        ],
        [pltpu.VMEM(*shape) for shape in loaded]
        + [
            pltpu.SemaphoreType.DMA((10,)),
            pltpu.VMEM((seq, LOW), f32),
            pltpu.VMEM((2 * seq, width), f32),
            pltpu.VMEM(*pair),
            pltpu.VMEM(*stat),
            pltpu.VMEM(*pair),
            pltpu.VMEM(*row),
            pltpu.VMEM(*row),
            pltpu.VMEM((seq, 2 * LOW), bf16),
            pltpu.VMEM((seq, HD), f32),
            pltpu.VMEM((seq, HD), f32),
            pltpu.VMEM((seq, ATT_EXPERTS * width), bf16),
            pltpu.VMEM((DEPTH, 2, width, D), bf16),
            pltpu.VMEM((DEPTH, ATT_EXPERTS, width_d, width), bf16),
            pltpu.SemaphoreType.DMA((DEPTH,)),
            pltpu.SemaphoreType.DMA((DEPTH,)),
            pltpu.VMEM((seq, D), bf16),
        ],
        project_flops,
        weight_bytes,
    )(places, *da_parts, output_w, query_w, key_w, value_w, aq, amisc, bcat, kb, vb, oa, ob, attn_routes, ga, o, q, k, v, lse, low, misc, cosf, sinf)

    held = (dx_part, lows, grad_oa, grad_qb, grad_kv, *da_parts, *tables_sum)
    dx_part, lows, grad_oa, grad_qb, grad_kv, *held = lax.optimization_barrier(held)
    da_parts, tables_sum = held[: shards + 1], held[shards + 1 :]
    lows_parts = [lows] + [shifted(lows, step) for step in range(1, shards)]
    lows_parts[1], *da_parts = lax.optimization_barrier((lows_parts[1], *da_parts))
    factors, grad_ob_own = call(
        lambda *refs: owner_kernel(shards, *refs),
        (),
        [pl.BlockSpec(memory_space=pltpu.SMEM)] + [whole()] * (shards + 3),
        [whole()] * 2,
        [sds((3 * LOW, own), bf16), sds((LOW, own), bf16)],
        [
            pltpu.VMEM((seq, own), bf16),
            pltpu.VMEM((seq, D), bf16),
            pltpu.VMEM((D, own), bf16),
        ],
        0,
        0,
    )(owner_places, *da_parts, out_lows, mlp_columns)
    lows_sum = sum(part.astype(f32) for part in lows_parts)
    half = LOW // 2
    lows_all = jnp.concatenate([lows_sum[: seq // 2, :half], lows_sum[: seq // 2, half:]], axis=0)
    lows_all = lows_all.astype(bf16)
    slopes = lows_sum[seq // 2 : seq // 2 + 2 * (seq // CHUNK)].reshape(2, seq).T
    dx = lax.psum_scatter(dx_part, "shard", scatter_dimension=0, tiled=True)

    input_grad = call(
        input_grad_kernel,
        (),
        [whole()] * 8,
        whole(),
        sds((rows, D), f32),
        [],
        2 * rows * LOW * D,
        24 * rows * D,
        20,
    )(dx, own_rows(slopes), ga_own, tokens, gain1, router_first, dh1, routes_own)

    lane = jnp.arange(LOW, dtype=jnp.int32)
    dense = jnp.zeros((seq, LOW), f32)
    for j in range(2):
        spread = (iota((half, LOW), 0) == (lane % RANK + j * RANK)[None, :]).astype(bf16)
        chosen = attn_routes[:, j : j + 1] == (lane // RANK)[None, :]
        dense = dense + jnp.where(chosen, nn(lows_all, spread), 0.0)
    grad_qa_own = tn(dense.astype(bf16), xn_own)
    grad_kva_own = tn(lows_all[:, 2 * RANK : 4 * RANK], xn_own)

    def to_owner_columns(part):
        return part.reshape(-1, groups, block).transpose(1, 0, 2).reshape(groups, -1)

    def to_owner_ranks(part):
        parts = part.reshape(-1, groups, RANK // groups, width)
        return parts.transpose(1, 0, 2, 3).reshape(groups, -1)

    sending = [
        to_owner_columns(grad_qa_own.astype(bf16)),
        to_owner_columns(grad_ob_own),
        to_owner_columns(grad_kva_own.astype(bf16)),
        to_owner_ranks(grad_qb),
        to_owner_ranks(grad_oa),
        to_owner_ranks(jnp.concatenate([grad_kv[:RANK], grad_kv[LOW + RANK : LOW + 2 * RANK]])),
        to_owner_columns(factors),
    ]
    sizes = [piece.shape[1] for piece in sending]
    sent = jnp.concatenate(sending, axis=1).reshape(groups, -1, LOW)
    got = lax.all_to_all(sent, "dp", split_axis=0, concat_axis=0, tiled=True)
    got = got.reshape(groups, -1).astype(f32)
    pick_source = (adapter_ids[:, None] == jnp.arange(ADAPTERS, dtype=jnp.int32)[None, :]).astype(
        f32
    )
    placed_sums = jnp.einsum("sa,sn->an", pick_source, got, precision=precise)
    parts = []
    start = 0
    for size in sizes:
        parts.append(placed_sums[:, start : start + size])
        start += size
    ranks_own = RANK // groups

    def columns_out(part, count):
        return part.reshape(ADAPTERS, count, RANK, block)

    def ranks_out(part, count):
        return part.reshape(ADAPTERS, count, ranks_own, width)

    query_a_sum = columns_out(parts[0], ATT_EXPERTS).transpose(1, 0, 3, 2)
    output_b_sum = columns_out(parts[1], ATT_EXPERTS).transpose(1, 0, 2, 3)
    kv_a_sum = columns_out(parts[2], 2).transpose(1, 0, 3, 2)
    query_b_sum = ranks_out(parts[3], ATT_EXPERTS).transpose(1, 0, 2, 3)
    output_a_sum = ranks_out(parts[4], ATT_EXPERTS).transpose(1, 0, 3, 2)
    kv_b_sum = ranks_out(parts[5], 2).transpose(1, 0, 2, 3)
    factor_sum = columns_out(parts[6], 3 * EXPERTS).transpose(1, 0, 2, 3)
    gate_a_sum = factor_sum[:EXPERTS].transpose(0, 1, 3, 2)
    up_a_sum = factor_sum[EXPERTS : 2 * EXPERTS].transpose(0, 1, 3, 2)
    down_b_sum = factor_sum[2 * EXPERTS :]

    joined = jnp.concatenate(tables_sum, axis=1) if len(tables_sum) > 1 else tables_sum[0]
    joined = joined.astype(f32).reshape(3, ADAPTERS, RANK, each)

    return (
        layer_out,
        input_grad,
        query_a_sum,
        query_b_sum,
        kv_a_sum[0],
        kv_b_sum[0],
        kv_a_sum[1],
        kv_b_sum[1],
        output_a_sum,
        output_b_sum,
        gate_a_sum,
        joined[0],
        up_a_sum,
        joined[1],
        ranks_first(joined[2]),
        down_b_sum,
    )


def solution(mesh):
    placed = (
        P(("dp", "shard"), None),
        P(("dp", "shard"), None),
        P(),
        P(),
        P(),
        P(),
        P(None, None, "shard"),
        P(None, "shard"),
        P(None, "shard"),
        P(None, "shard", None),
        P(None, "dp"),
        P(None, "dp"),
        P("dp", None),
        P(),
        P(None, None, None, "shard"),
        P(),
        P(None, None, "shard"),
        P(),
        P(None, None, "shard"),
        P(None, None, "shard", None),
        P(),
        P(),
        P(None, None, "dp"),
        P(),
        P(None, None, "dp"),
        P(None, "dp", None),
        P(),
        P(),
        P("dp", None),
        P(("dp", "shard"), None),
    )
    return jax.shard_map(
        on_device,
        mesh=mesh,
        in_specs=placed,
        out_specs=(
            P(("dp", "shard"), None),
            P(("dp", "shard"), None),
            P(None, None, ("dp", "shard"), None),
            P(None, None, "dp", "shard"),
            P(None, ("dp", "shard"), None),
            P(None, "dp", "shard"),
            P(None, ("dp", "shard"), None),
            P(None, "dp", "shard"),
            P(None, None, "shard", "dp"),
            P(None, None, None, ("dp", "shard")),
            P(None, None, ("dp", "shard"), None),
            P(None, None, ("dp", "shard")),
            P(None, None, ("dp", "shard"), None),
            P(None, None, ("dp", "shard")),
            P(None, ("dp", "shard"), None),
            P(None, None, None, ("dp", "shard")),
        ),
        check_vma=False,
    )
```
